32 devices in a mesh: rows: 8 (over z, x), heads: 4 (over y, core).
Axes of the slice: x: 2, y: 2, z: 4, core: 2. Of those that a mesh axis runs over, the one named last changes fastest.
Arguments:
- tokens: bfloat16 [16384, 768], P(('rows', 'heads')), may hold values from -6 to 6
- segment: int32 [16384], P(('rows', 'heads')), may hold values from 0 to 63, as said below
- live_token: int32 [16384], P(('rows', 'heads')), may hold values from 0 to 1, as said below
- prompt_slot: int32 [16384], P(('rows', 'heads')), may hold values from 0 to 50, as said below
- prompts: bfloat16 [50, 768], replicated, may hold values from -6 to 6
- attn_gain: bfloat16 [768], replicated, may hold values from 0.5 to 1.5
- attn_shift: bfloat16 [768], replicated, may hold values from -2.5 to 2.5
- qkv_weight: bfloat16 [768, 3, 768], P('rows', None, 'heads'), may hold values from -0.21875 to 0.21875
- out_weight: bfloat16 [768, 768], P('heads', 'rows'), may hold values from -0.75 to 0.75
- mlp_gain: bfloat16 [768], replicated, may hold values from 0.5 to 1.5
- mlp_shift: bfloat16 [768], replicated, may hold values from -2.5 to 2.5
- up_weight: bfloat16 [768, 3072], P(None, ('rows', 'heads')), may hold values from -0.21875 to 0.21875
- up_bias: bfloat16 [3072], P(('rows', 'heads')), may hold values from -3 to 3
- down_weight: bfloat16 [3072, 768], P(('rows', 'heads')), may hold values from -0.109375 to 0.109375
- cotangent: bfloat16 [16384, 768], P(('rows', 'heads')), may hold values from -6 to 6
Outputs:
- output: bfloat16 [16384, 768], P(('rows', 'heads'))
- grad_tokens: float32 [16384, 768], P(('rows', 'heads'))
- grad_prompts: float32 [50, 768], replicated
- grad_attn_gain: float32 [768], replicated
- grad_attn_shift: float32 [768], replicated
- grad_qkv: float32 [768, 3, 768], P('rows', None, 'heads')
- grad_out: float32 [768, 768], P('heads', 'rows')
- grad_mlp_gain: float32 [768], replicated
- grad_mlp_shift: float32 [768], replicated
- grad_up: float32 [768, 3072], P(None, ('rows', 'heads'))
- grad_up_bias: float32 [3072], P(('rows', 'heads'))
- grad_down: float32 [3072, 768], P(('rows', 'heads'))
The draws below stay inside these ranges and needn't reach their ends.
Inputs may be any that keep to these rules, and one draw needn't show every extreme that they name: `segment`: numbers images over all packed rows in order: packed row r holds images r * 8 to r * 8 + 7 of 247 consecutive tokens each, in that order, with padding before, between or after them; a padding token carries the number of the image before it in its row (or the row's first image). `live_token`: 1 on the tokens of images, 0 on padding; every packed row has 72 padding tokens. Within an image, token 0 is the class token, tokens 1 to 50 are prompts 0 to 49 in order, the rest are patches; prompt_slot is the prompt's number on prompt tokens and 50 on all others, padding included.
All inputs are finite; a program needn't handle non-finite values.
Results may differ from the reference program's by a relative error of at most 0.017.
Values may be sent and summed in bfloat16 or wider, within the bound.
No kernel may reach another device: no remote copies, remote signals or barrier semaphores. Data moves between devices by JAX's collectives and lax.ppermute only.
A program may use at most 128 MiB of HBM per device.

```python
import jax
import jax.numpy as jnp
from jax import lax

D = 768
HEADS = 12
HEAD = 64
FF = 3072
PROMPTS = 50
IMGS_ROW = 8
ROW = 2048
IMG = 247
TOKENS = 16384


def layout(key):
    rows_all = TOKENS // ROW
    spare_pads = ROW - IMGS_ROW * IMG
    gap_cuts = jnp.sort(jax.random.randint(key, (rows_all, IMGS_ROW), 0, spare_pads + 1), axis=1)
    starts = gap_cuts + jnp.arange(IMGS_ROW, dtype=jnp.int32)[None, :] * IMG
    places = jnp.arange(ROW, dtype=jnp.int32)
    begun = (places[None, :, None] >= starts[:, None, :]).astype(jnp.int32)
    started = jnp.sum(begun, axis=-1)
    image_index = jnp.maximum(started - 1, 0)
    chosen = (jnp.arange(IMGS_ROW, dtype=jnp.int32)[None, None, :] == image_index[:, :, None]).astype(jnp.int32)
    start_of = jnp.sum(chosen * starts[:, None, :], axis=-1)
    offset = places[None, :] - start_of
    is_live = ((started > 0) & (offset < IMG)).astype(jnp.int32)
    numbers = image_index + jnp.arange(rows_all, dtype=jnp.int32)[:, None] * IMGS_ROW
    is_prompt = (is_live > 0) & (offset >= 1) & (offset <= PROMPTS)
    slots = jnp.where(is_prompt, offset - 1, PROMPTS).astype(jnp.int32)
    return (numbers.reshape(-1).astype(jnp.int32), is_live.reshape(-1), slots.reshape(-1))


def draw_segment(key, part):
    return layout(key)[0]


def draw_live_token(key, part):
    return layout(key)[1]


def draw_prompt_slot(key, part):
    return layout(key)[2]


def levels(stream_key, shape, shards, least, top_value):
    def one(axis_at, shards_of):
        steps = jax.random.uniform(jax.random.fold_in(jax.random.fold_in(stream_key, 6), axis_at), (shards_of,), jnp.float32, least / len(shards), top_value / len(shards))
        return jnp.repeat(jnp.exp(steps), shape[axis_at] // shards_of).reshape((-1,) + (1,) * (len(shape) - axis_at - 1))

    level = one(*shards[0])
    for cut in shards[1:]:
        level = level * one(*cut)
    return level


def gaussian(own_key, shape, scale, limit, pieces=(), kind=jnp.bfloat16):
    factor_of = levels(own_key, shape, pieces, -0.22, 0.18) if pieces else 1.0
    drawn = jax.random.normal(own_key, shape, jnp.float32) * scale * factor_of
    return jnp.minimum(jnp.maximum(drawn, -limit), limit).astype(kind)


def setup_inputs(seed: int = 0) -> dict:
    key_of = jax.random.split(jax.random.key(seed), 16)
    return {
        "tokens": gaussian(key_of[0], (TOKENS, D), 1.0, 6.0, ((0, 32),)),
        "segment": draw_segment(jax.random.fold_in(key_of[15], 71), 0),
        "live_token": draw_live_token(jax.random.fold_in(key_of[15], 71), 0),
        "prompt_slot": draw_prompt_slot(jax.random.fold_in(key_of[15], 71), 0),
        "prompts": gaussian(key_of[4], (PROMPTS, D), 1.0, 6.0),
        "attn_gain": jnp.clip(1.0 + 0.1 * jax.random.normal(key_of[5], (D,), jnp.float32), 0.5, 1.5).astype(jnp.bfloat16),
        "attn_shift": gaussian(key_of[6], (D,), 0.3, 2.5),
        "qkv_weight": gaussian(key_of[7], (D, 3, D), D ** -0.5, 0.21875, ((0, 8), (2, 4))),
        "out_weight": gaussian(key_of[8], (D, D), HEAD ** -0.5, 0.75, ((0, 4), (1, 8))),
        "mlp_gain": jnp.clip(1.0 + 0.1 * jax.random.normal(key_of[9], (D,), jnp.float32), 0.5, 1.5).astype(jnp.bfloat16),
        "mlp_shift": gaussian(key_of[10], (D,), 0.3, 2.5),
        "up_weight": gaussian(key_of[11], (D, FF), D ** -0.5, 0.21875, ((1, 32),)),
        "up_bias": gaussian(key_of[12], (FF,), 0.5, 3.0, ((0, 32),)),
        "down_weight": gaussian(key_of[13], (FF, D), FF ** -0.5, 0.109375, ((0, 32),)),
        "cotangent": gaussian(key_of[14], (TOKENS, D), 1.0, 6.0, ((0, 32),)),
    }


@jax.custom_vjp
def low(v):
    return lax.optimization_barrier(v.astype(jnp.bfloat16)).astype(jnp.float32)

@jax.custom_vjp
def low_back(v):
    return v

def low_keep(v):
    return (low(v), None)

def low_pass(kept, grad):
    return (grad,)

def back_keep(v):
    return (v, None)

def back_low(kept, grad):
    return (low(grad),)
low.defvjp(low_keep, low_pass)
low_back.defvjp(back_keep, back_low)
EPSILON = 1e-06

def layer_norm(values, scale_gain, shift_vec):
    center = values - lax.optimization_barrier(jnp.mean(values, axis=-1, keepdims=True))
    spread = lax.optimization_barrier(jnp.mean(center * center, axis=-1, keepdims=True))
    return center * lax.rsqrt(spread + EPSILON) * scale_gain + shift_vec

def forward_row(segment, live_token, prompt_slot, tokens, prompts, attn_gain, attn_shift, qkv_weight, out_weight, mlp_gain, mlp_shift, up_weight, up_bias, down_weight):
    highest = lax.Precision.HIGHEST
    picked = prompts[jnp.minimum(prompt_slot, PROMPTS - 1)]
    inputs = jnp.where((prompt_slot < PROMPTS)[:, None], picked, tokens)
    normed = low(layer_norm(inputs, attn_gain, attn_shift))
    qkv_all = low(low_back(jnp.einsum('td,dcj->tcj', normed, qkv_weight, precision=highest)))
    split_heads = qkv_all.reshape(ROW, 3, HEADS, HEAD)
    queries = split_heads[:, 0]
    keys_all = split_heads[:, 1]
    values_all = split_heads[:, 2]
    scores = low_back(jnp.einsum('qhe,khe->hqk', queries, keys_all, precision=highest) * 0.125)
    places = jnp.arange(ROW, dtype=jnp.int32)
    same_image = (segment[:, None] == segment[None, :]) & (live_token[:, None] > 0) & (live_token[None, :] > 0)
    allowed = same_image | (places[:, None] == places[None, :])
    masked = jnp.where(allowed[None], scores, -jnp.inf)
    row_top = lax.optimization_barrier(jnp.max(masked, axis=-1, keepdims=True))
    exp_scores = jnp.exp(masked - row_top)
    soft_probs = low(exp_scores / lax.optimization_barrier(jnp.sum(exp_scores, axis=-1, keepdims=True)))
    attended = jnp.einsum('hqk,khe->qhe', soft_probs, values_all, precision=highest).reshape(ROW, D)
    attended = low(low_back(attended))
    projected = low_back(jnp.dot(attended, out_weight, precision=highest))
    middle = inputs + projected
    normed_two = low(layer_norm(middle, mlp_gain, mlp_shift))
    pre_act = low_back(jnp.dot(normed_two, up_weight, precision=highest) + up_bias)
    activated = low(jax.nn.gelu(pre_act, approximate=False))
    return middle + jnp.dot(activated, down_weight, precision=highest)

def reference(tokens, segment, live_token, prompt_slot, prompts, attn_gain, attn_shift, qkv_weight, out_weight, mlp_gain, mlp_shift, up_weight, up_bias, down_weight, cotangent):
    rows_all = tokens.shape[0] // ROW
    params = tuple((item.astype(jnp.float32) for item in (prompts, attn_gain, attn_shift, qkv_weight, out_weight, mlp_gain, mlp_shift, up_weight, up_bias, down_weight)))

    def one_row(totals, row_items):
        row_tokens, row_segment, row_live, row_slot, row_cot = row_items

        def wrapped(row_input, *weights):
            return forward_row(row_segment, row_live, row_slot, row_input, *weights)
        result, pullback = jax.vjp(wrapped, row_tokens.astype(jnp.float32), *params)
        row_grads = pullback(row_cot.astype(jnp.float32))
        new_totals = tuple((total_part + grad_part for total_part, grad_part in zip(totals, row_grads[1:])))
        return (new_totals, (result.astype(jnp.bfloat16), row_grads[0]))
    zero_grads = tuple((jnp.zeros(item.shape, jnp.float32) for item in params))
    row_items = (tokens.reshape(rows_all, ROW, D), segment.reshape(rows_all, ROW), live_token.reshape(rows_all, ROW), prompt_slot.reshape(rows_all, ROW), cotangent.reshape(rows_all, ROW, D))
    totals, stacked = lax.scan(one_row, zero_grads, row_items)
    output = stacked[0].reshape(rows_all * ROW, D)
    grad_tokens = stacked[1].reshape(rows_all * ROW, D)
    return (output, grad_tokens, totals[0], totals[1], totals[2], totals[3], totals[4], totals[5], totals[6], totals[7], totals[8], totals[9])
```

```python
import functools

import jax
import jax.numpy as jnp
from jax import lax
from jax.experimental import pallas as pl
from jax.experimental.pallas import tpu as pltpu
from jax.sharding import PartitionSpec as P

HEAD = 64
ROW = 2048
IMG = 247
IMGS_ROW = 8
PROMPTS = 50
SLOT = 272
CORE = 256
HALO = 48
EPSILON = 1e-06
AXES = ("rows", "heads")
F32 = jnp.float32
BF16 = jnp.bfloat16
VMEM_LIMIT = 56 * 1024 * 1024

NN = (((1,), (0,)), ((), ()))
NT = (((1,), (1,)), ((), ()))
TN = (((0,), (0,)), ((), ()))


def dot(left, right, dims=NN):
    return lax.dot_general(left, right, dims, preferred_element_type=F32)


def whole(shape):
    return pl.BlockSpec(shape, lambda *_: (0,) * len(shape))


def params(**more):
    return pltpu.CompilerParams(vmem_limit_bytes=VMEM_LIMIT, **more)


def cost(flops, moved, trans=0):
    return pl.CostEstimate(flops=int(flops), bytes_accessed=int(moved), transcendentals=int(trans))


SMEM = pl.BlockSpec(memory_space=pltpu.SMEM)
ANY = pl.BlockSpec(memory_space=pl.ANY)


def stats(values):
    center = values - jnp.mean(values, axis=-1, keepdims=True)
    inverse = lax.rsqrt(jnp.mean(center * center, axis=-1, keepdims=True) + EPSILON)
    return center * inverse, inverse


def norm_back(grad, hat, inverse, gain):
    inner = grad * gain
    first = jnp.mean(inner, axis=-1, keepdims=True)
    second = jnp.mean(inner * hat, axis=-1, keepdims=True)
    return inverse * (inner - first - hat * second)


def prep_kernel(
    place, own, other, halo, prom, gain, shift, x_out, n_out, cot_out, dest_own, dest_halo, d_oth
):
    step = pl.program_id(0)
    count = d_oth.shape[1]
    slots = pl.num_programs(0)
    y_at, c_at = place[2], place[3]

    @pl.when(step == 0)
    def _():
        big = 1 << 20
        spans = (
            (own[2 * count : 2 * count + 16, :count], 2 * count * y_at + count * c_at, True),
            (other[2 * count : 2 * count + 16, :count], 2 * count * y_at + count * (1 - c_at), True),
            (halo[2 * HALO : 2 * HALO + 16, :HALO], 2 * count - HALO * y_at, False),
        )
        parts = []
        for marks, base, home in spans:
            code = marks.astype(F32)[0:1].astype(jnp.int32)
            live = (code & 1) > 0
            slot = (code >> 1) - slots * y_at
            pos = base + lax.broadcasted_iota(jnp.int32, code.shape, 1)
            parts.append((live, slot, pos, home))
        starts = []
        for k in range(slots):
            low = None
            for live, slot, pos, home in parts:
                here = jnp.min(jnp.where(live & (slot == k), pos, big), axis=1, keepdims=True)
                low = here if low is None else jnp.minimum(low, here)
            starts.append(low)
        pads_own, pads_other = [
            jnp.sum(jnp.where(part[0], 0, 1), axis=1, keepdims=True) for part in parts[:2]
        ]
        befores = (c_at * pads_other, (1 - c_at) * pads_own, None)
        results = []
        for (live, slot, pos, home), before in zip(parts, befores):
            dest = jnp.full(pos.shape, -1, jnp.int32)
            for k in range(slots):
                dest = jnp.where(live & (slot == k), pos - starts[k] + k * SLOT, dest)
            if home:
                pads = jnp.where(live, 0.0, 1.0).astype(BF16)
                size = pads.shape[1]
                earlier = (
                    lax.broadcasted_iota(jnp.int32, (size, size), 0)
                    < lax.broadcasted_iota(jnp.int32, (size, size), 1)
                )
                wide = jnp.broadcast_to(pads, (16, size))
                rank = dot(wide, earlier.astype(BF16))[0:1].astype(jnp.int32) + before
                spare = (rank & (slots - 1)) * SLOT + IMG + (rank >> (slots.bit_length() - 1))
                dest = jnp.where(live, dest, spare)
            results.append(dest)
        dest_own[...] = results[0]
        d_oth[...] = results[1]
        dest_halo[...] = results[2]

    rows = step * SLOT
    tokens = cots = None
    for dest, ref, size in (
        (dest_own, own, count),
        (d_oth, other, count),
        (dest_halo, halo, HALO),
    ):
        at = rows + lax.broadcasted_iota(jnp.int32, (SLOT, size), 0)
        pick = (at == dest[...]).astype(BF16)
        one = dot(pick, ref[0:size])
        two = dot(pick, ref[size : 2 * size])
        tokens = one if tokens is None else tokens + one
        cots = two if cots is None else cots + two
    at = lax.broadcasted_iota(jnp.int32, (SLOT, 1), 0)
    inputs = jnp.where((at >= 1) & (at <= PROMPTS), prom[...].astype(F32), tokens)
    hat, _ = stats(inputs)
    x_out[...] = inputs.astype(BF16)
    n_out[...] = (hat * gain[...] + shift[...]).astype(BF16)
    cot_out[...] = cots.astype(BF16)


def prep(place, own, other, halo, prom, gain, shift, slots):
    count = own.shape[0] // 2 - 8
    wide = own.shape[1]
    rows = slots * SLOT
    tile = pl.BlockSpec((SLOT, wide), lambda t: (t, 0))
    array = jax.ShapeDtypeStruct((rows, wide), BF16)
    return pl.pallas_call(
        prep_kernel,
        grid=(slots,),
        in_specs=[SMEM] + [whole(v.shape) for v in (own, other, halo, prom, gain, shift)],
        out_specs=[tile, tile, tile, whole((1, count)), whole((1, HALO))],
        out_shape=[
            array,
            array,
            array,
            jax.ShapeDtypeStruct((1, count), jnp.int32),
            jax.ShapeDtypeStruct((1, HALO), jnp.int32),
        ],
        scratch_shapes=[pltpu.VMEM((1, count), jnp.int32)],
        compiler_params=params(),
        cost_estimate=cost(4 * rows * (2 * count + HALO) * wide, 12 * rows * wide),
        name="prep",
    )(place, own, other, halo, prom, gain, shift)


def attend_kernel(normed, weight, qkv_out, prob_out, att_out, part_out):
    third = weight.shape[2] // 4
    rows = lax.broadcasted_iota(jnp.int32, (CORE, CORE), 0)
    cols = lax.broadcasted_iota(jnp.int32, (CORE, CORE), 1)
    allowed = ((rows < IMG) & (cols < IMG)) | (rows == cols)
    total = None
    for group in range(weight.shape[0]):
        qkv_out[group] = dot(normed[...], weight[group, :, : 3 * third]).astype(BF16)
        for head in range(third // HEAD):
            at = head * HEAD
            queries = qkv_out[group, :CORE, at : at + HEAD]
            keys = qkv_out[group, :CORE, third + at : third + at + HEAD]
            values = qkv_out[group, :, 2 * third + at : 2 * third + at + HEAD]
            scores = jnp.where(allowed, dot(queries, keys, NT) * 0.125, -1e30)
            exp_scores = jnp.exp(scores - jnp.max(scores, axis=-1, keepdims=True))
            probs = (exp_scores / jnp.sum(exp_scores, axis=-1, keepdims=True)).astype(BF16)
            prob_out[0, group, head] = probs
            att_out[group, :CORE, at : at + HEAD] = dot(probs, values[:CORE]).astype(BF16)
            att_out[group, CORE:, at : at + HEAD] = values[CORE:]
        part = dot(att_out[group], weight[group, :, 3 * third :], NT)
        total = part if total is None else total + part
    part_out[...] = total.astype(BF16)


def attend(normed, weight, slots):
    groups, deep, wide = weight.shape
    third = wide // 4
    heads = third // HEAD
    rows = slots * SLOT
    return pl.pallas_call(
        attend_kernel,
        grid=(slots,),
        in_specs=[pl.BlockSpec((SLOT, deep), lambda t: (t, 0)), whole(weight.shape)],
        out_specs=[
            pl.BlockSpec((groups, SLOT, 3 * third), lambda t: (0, t, 0)),
            pl.BlockSpec((1, groups, heads, CORE, CORE), lambda t: (t, 0, 0, 0, 0)),
            pl.BlockSpec((groups, SLOT, third), lambda t: (0, t, 0)),
            pl.BlockSpec((SLOT, deep), lambda t: (t, 0)),
        ],
        out_shape=[
            jax.ShapeDtypeStruct((groups, rows, 3 * third), BF16),
            jax.ShapeDtypeStruct((slots, groups, heads, CORE, CORE), BF16),
            jax.ShapeDtypeStruct((groups, rows, third), BF16),
            jax.ShapeDtypeStruct((rows, deep), BF16),
        ],
        compiler_params=params(),
        cost_estimate=cost(2 * rows * deep * groups * wide * 1.6, 12 * rows * deep),
        name="attend",
    )(normed, weight)


def mid_kernel(x_in, one, two, gain, shift, middle_out, n_out):
    middle = x_in[...].astype(F32) + one[...].astype(F32) + two[...].astype(F32)
    middle_out[...] = middle
    hat, _ = stats(middle)
    n_out[...] = (hat * gain[...] + shift[...]).astype(BF16)


def mid(x_in, one, two, gain, shift, slots):
    rows, wide = x_in.shape
    tile = pl.BlockSpec((SLOT, wide), lambda t: (t, 0))
    return pl.pallas_call(
        mid_kernel,
        grid=(slots,),
        in_specs=[tile, tile, tile, whole(gain.shape), whole(shift.shape)],
        out_specs=[tile, tile],
        out_shape=[jax.ShapeDtypeStruct(x_in.shape, F32), jax.ShapeDtypeStruct(x_in.shape, BF16)],
        compiler_params=params(),
        cost_estimate=cost(20 * rows * wide, 12 * rows * wide),
        name="mid",
    )(x_in, one, two, gain, shift)


def mlp_kernel(more, *refs):
    if more:
        (a_in, b_in, normed, cot, bias, o_acc, g_acc, *refs) = refs
    else:
        (a_in, b_in, normed, cot, bias, *refs) = refs
    (o_out, g_out, a_out, b_out, bias_out, weight, act, grad, result, in_sem, out_sem) = refs
    step = pl.program_id(0)
    lead, count, _, span, _ = a_in.shape
    hidden = weight.shape[1]

    def pieces(first, second):
        for source, ref in enumerate((first, second)):
            for i in range(lead):
                for j in range(count):
                    for kind in range(2):
                        place = ((source * lead + i) * count + j) * span
                        index = ((source * lead + i) * count + j) * 2 + kind
                        yield ref.at[i, j, kind], kind, place, index

    @pl.when(step == 0)
    def _():
        copies = [
            pltpu.make_async_copy(ref, weight.at[kind, pl.ds(place, span)], in_sem.at[index])
            for ref, kind, place, index in pieces(a_in, b_in)
        ]
        for copy in copies:
            copy.start()
        bias_out[...] = jnp.zeros_like(bias_out)
        for copy in copies:
            copy.wait()

    rows = pl.ds(pl.multiple_of(step * SLOT, 16), SLOT)
    tile_n = normed[rows]
    tile_c = cot[rows]
    cut = 256
    o_sum = o_acc[...] if more else None
    g_sum = g_acc[...] if more else None
    for at in range(0, hidden, cut):
        up = weight[0, at : at + cut]
        down = weight[1, at : at + cut]
        pre = dot(tile_n, up, NT) + bias[:, at : at + cut]
        cdf = 0.5 * (1.0 + lax.erf(pre * 0.7071067811865476))
        pdf = jnp.exp(-0.5 * pre * pre) * 0.3989422804014327
        low = (pre * cdf).astype(BF16)
        grad_low = (dot(tile_c, down, NT) * (cdf + pre * pdf)).astype(BF16)
        act[rows, at : at + cut] = low
        grad[rows, at : at + cut] = grad_low
        bias_out[:, at : at + cut] += jnp.sum(grad_low.astype(F32), axis=0, keepdims=True)
        o_part = dot(low, down)
        g_part = dot(grad_low, up)
        o_sum = o_part if o_sum is None else o_sum + o_part
        g_sum = g_part if g_sum is None else g_sum + g_part
    o_out[...] = o_sum.astype(o_out.dtype)
    g_out[...] = g_sum.astype(g_out.dtype)

    @pl.when(step == pl.num_programs(0) - 1)
    def _():
        def tile(i, _):
            at = pl.ds(pl.multiple_of(i * cut, cut), cut)
            result[0, at] = dot(grad[:, at], normed[...], TN).astype(BF16)
            result[1, at] = dot(act[:, at], cot[...], TN).astype(BF16)
            return 0

        lax.fori_loop(0, hidden // cut, tile, 0)
        copies = [
            pltpu.make_async_copy(result.at[kind, pl.ds(place, span)], ref, out_sem.at[index])
            for ref, kind, place, index in pieces(a_out, b_out)
        ]
        for copy in copies:
            copy.start()
        for copy in copies:
            copy.wait()


def mlp(a_in, b_in, normed, cot, bias, slots, sums=None):
    rows, wide = normed.shape
    hidden = bias.shape[1]
    more = sums is not None
    tile = pl.BlockSpec((SLOT, wide), lambda t: (t, 0))
    kept = BF16 if more else F32
    count = 4 * a_in.shape[0] * a_in.shape[1]
    return pl.pallas_call(
        functools.partial(mlp_kernel, more),
        grid=(slots,),
        in_specs=[ANY, ANY, whole(normed.shape), whole(cot.shape), whole(bias.shape)]
        + ([tile, tile] if more else []),
        out_specs=[tile, tile, ANY, ANY, whole(bias.shape)],
        out_shape=[
            jax.ShapeDtypeStruct((rows, wide), kept),
            jax.ShapeDtypeStruct((rows, wide), kept),
            jax.ShapeDtypeStruct(a_in.shape, BF16),
            jax.ShapeDtypeStruct(b_in.shape, BF16),
            jax.ShapeDtypeStruct(bias.shape, F32),
        ],
        scratch_shapes=[
            pltpu.VMEM((2, hidden, wide), BF16),
            pltpu.VMEM((rows, hidden), BF16),
            pltpu.VMEM((rows, hidden), BF16),
            pltpu.VMEM((2, hidden, wide), BF16),
            pltpu.SemaphoreType.DMA((count,)),
            pltpu.SemaphoreType.DMA((count,)),
        ],
        compiler_params=params(),
        cost_estimate=cost(12 * rows * hidden * wide, 14 * rows * wide, 2 * rows * hidden),
        name="mlp",
    )(a_in, b_in, normed, cot, bias, *(sums or ()))


def finish_kernel(middle, one, two, dest_own, dest_halo, own_out, halo_out, total, total_halo):
    step = pl.program_id(0)
    value = middle[...] + one[...].astype(F32) + two[...].astype(F32)
    spread_rows(step, value.astype(BF16), dest_own, dest_halo, total, total_halo)

    @pl.when(step == pl.num_programs(0) - 1)
    def _():
        own_out[...] = total[...].astype(own_out.dtype)
        halo_out[...] = total_halo[...].astype(halo_out.dtype)


def spread_rows(step, value, dest_own, dest_halo, total, total_halo):
    for dest, sum_ref in ((dest_own, total), (dest_halo, total_halo)):
        at = step * SLOT + lax.broadcasted_iota(jnp.int32, (SLOT, dest.shape[1]), 0)
        part = dot((at == dest[...]).astype(BF16), value, TN)
        sum_ref[...] = jnp.where(step == 0, part, sum_ref[...] + part)


def finish(middle, one, two, dest_own, dest_halo, slots):
    rows, wide = middle.shape
    count = dest_own.shape[1]
    tile = pl.BlockSpec((SLOT, wide), lambda t: (t, 0))
    return pl.pallas_call(
        finish_kernel,
        grid=(slots,),
        in_specs=[tile, tile, tile, whole(dest_own.shape), whole(dest_halo.shape)],
        out_specs=[whole((count, wide)), whole((HALO, wide))],
        out_shape=[
            jax.ShapeDtypeStruct((count, wide), BF16),
            jax.ShapeDtypeStruct((HALO, wide), BF16),
        ],
        scratch_shapes=[pltpu.VMEM((count, wide), F32), pltpu.VMEM((HALO, wide), F32)],
        compiler_params=params(),
        cost_estimate=cost(2 * rows * (count + HALO) * wide, 10 * rows * wide),
        name="finish",
    )(middle, one, two, dest_own, dest_halo)


def back_kernel(
    middle, one, two, cot, gain, weight, qkv, prob, gm_out, gp_out, dq_out, part_out, sums_out
):
    step = pl.program_id(0)
    third = weight.shape[2] // 4

    @pl.when(step == 0)
    def _():
        sums_out[...] = jnp.zeros_like(sums_out)

    grad = one[...].astype(F32) + two[...].astype(F32)
    hat, inverse = stats(middle[...])
    sums_out[0:1] += jnp.sum(grad * hat, axis=0, keepdims=True)
    sums_out[1:2] += jnp.sum(grad, axis=0, keepdims=True)
    grad_middle = cot[...].astype(F32) + norm_back(grad, hat, inverse, gain[...])
    gm_out[...] = grad_middle
    grad_proj = grad_middle.astype(BF16)
    gp_out[...] = grad_proj
    total = None
    for group in range(weight.shape[0]):
        grad_att = dot(grad_proj, weight[group, :, 3 * third :]).astype(BF16)
        for head in range(third // HEAD):
            at = head * HEAD
            queries = qkv[group, :CORE, at : at + HEAD]
            keys = qkv[group, :CORE, third + at : third + at + HEAD]
            values = qkv[group, :CORE, 2 * third + at : 2 * third + at + HEAD]
            grad_head = grad_att[:, at : at + HEAD]
            grad_core = grad_head[:CORE]
            probs = prob[0, group, head]
            probs_wide = probs.astype(F32)
            grad_probs = dot(grad_core, values, NT)
            center = jnp.sum(probs_wide * grad_probs, axis=-1, keepdims=True)
            grad_scores = (probs_wide * (grad_probs - center)).astype(BF16)
            grad_q = (dot(grad_scores, keys) * 0.125).astype(BF16)
            grad_k = (dot(grad_scores, queries, TN) * 0.125).astype(BF16)
            grad_v = dot(probs, grad_core, TN).astype(BF16)
            blank = jnp.zeros((SLOT - CORE, HEAD), BF16)
            dq_out[group, :CORE, at : at + HEAD] = grad_q
            dq_out[group, CORE:, at : at + HEAD] = blank
            dq_out[group, :CORE, third + at : third + at + HEAD] = grad_k
            dq_out[group, CORE:, third + at : third + at + HEAD] = blank
            dq_out[group, :CORE, 2 * third + at : 2 * third + at + HEAD] = grad_v
            dq_out[group, CORE:, 2 * third + at : 2 * third + at + HEAD] = grad_head[CORE:]
        part = dot(dq_out[group], weight[group, :, : 3 * third], NT)
        total = part if total is None else total + part
    part_out[...] = total.astype(BF16)


def back(middle, one, two, cot, gain, weight, qkv, prob, slots):
    rows, wide = middle.shape
    groups, third = weight.shape[0], weight.shape[2] // 4
    tile = pl.BlockSpec((SLOT, wide), lambda t: (t, 0))
    tile_q = pl.BlockSpec((groups, SLOT, 3 * third), lambda t: (0, t, 0))
    return pl.pallas_call(
        back_kernel,
        grid=(slots,),
        in_specs=[
            tile,
            tile,
            tile,
            tile,
            whole(gain.shape),
            whole(weight.shape),
            tile_q,
            pl.BlockSpec((1,) + prob.shape[1:], lambda t: (t, 0, 0, 0, 0)),
        ],
        out_specs=[tile, tile, tile_q, tile, whole((8, wide))],
        out_shape=[
            jax.ShapeDtypeStruct((rows, wide), F32),
            jax.ShapeDtypeStruct((rows, wide), BF16),
            jax.ShapeDtypeStruct(qkv.shape, BF16),
            jax.ShapeDtypeStruct((rows, wide), BF16),
            jax.ShapeDtypeStruct((8, wide), F32),
        ],
        compiler_params=params(),
        cost_estimate=cost(2 * rows * wide * groups * 4 * third * 2, 24 * rows * wide),
        name="back",
    )(middle, one, two, cot, gain, weight, qkv, prob)


def weight_kernel(normed, grad_proj, grad_qkv, att, out):
    third = att.shape[2]
    out[0, :, : 3 * third] = dot(normed[...], grad_qkv[0], TN).astype(BF16)
    out[0, :, 3 * third :] = dot(grad_proj[...], att[0], TN).astype(BF16)


def weight_grads(normed, grad_proj, grad_qkv, att):
    rows, wide = normed.shape
    groups, _, third = att.shape
    cut = 256
    tall = pl.BlockSpec((rows, cut), lambda d, g: (0, d))
    return pl.pallas_call(
        weight_kernel,
        grid=(wide // cut, groups),
        in_specs=[
            tall,
            tall,
            pl.BlockSpec((1, rows, 3 * third), lambda d, g: (g, 0, 0)),
            pl.BlockSpec((1, rows, third), lambda d, g: (g, 0, 0)),
        ],
        out_specs=pl.BlockSpec((1, cut, 4 * third), lambda d, g: (g, d, 0)),
        out_shape=jax.ShapeDtypeStruct((groups, wide, 4 * third), BF16),
        compiler_params=params(),
        cost_estimate=cost(2 * rows * wide * groups * 4 * third, 20 * rows * wide),
        name="weight_grads",
    )(normed, grad_proj, grad_qkv, att)


def last_kernel(
    x_in, gm, one, two, gain, dest_own, dest_halo, own_out, halo_out, prompt_out, sums_out, halo_sum
):
    step = pl.program_id(0)

    @pl.when(step == 0)
    def _():
        sums_out[...] = jnp.zeros_like(sums_out)
        prompt_out[...] = jnp.zeros_like(prompt_out)

    grad = one[...].astype(F32) + two[...].astype(F32)
    hat, inverse = stats(x_in[...].astype(F32))
    sums_out[0:1] += jnp.sum(grad * hat, axis=0, keepdims=True)
    sums_out[1:2] += jnp.sum(grad, axis=0, keepdims=True)
    grad_in = gm[...] + norm_back(grad, hat, inverse, gain[...])
    prompt_out[...] += grad_in[: prompt_out.shape[0]]
    at = lax.broadcasted_iota(jnp.int32, (SLOT, 1), 0)
    value = jnp.where((at >= 1) & (at <= PROMPTS), 0.0, grad_in).astype(BF16)
    spread_rows(step, value, dest_own, dest_halo, own_out, halo_sum)

    @pl.when(step == pl.num_programs(0) - 1)
    def _():
        halo_out[...] = halo_sum[...].astype(BF16)


def last(x_in, gm, one, two, gain, dest_own, dest_halo, slots):
    rows, wide = x_in.shape
    count = dest_own.shape[1]
    tile = pl.BlockSpec((SLOT, wide), lambda t: (t, 0))
    return pl.pallas_call(
        last_kernel,
        grid=(slots,),
        in_specs=[tile] * 4 + [whole(gain.shape), whole(dest_own.shape), whole(dest_halo.shape)],
        out_specs=[whole((count, wide)), whole((HALO, wide)), whole((56, wide)), whole((8, wide))],
        out_shape=[
            jax.ShapeDtypeStruct((count, wide), F32),
            jax.ShapeDtypeStruct((HALO, wide), BF16),
            jax.ShapeDtypeStruct((56, wide), F32),
            jax.ShapeDtypeStruct((8, wide), F32),
        ],
        scratch_shapes=[pltpu.VMEM((HALO, wide), F32)],
        compiler_params=params(),
        cost_estimate=cost(2 * rows * (count + HALO) * wide, 10 * rows * wide),
        name="last",
    )(x_in, gm, one, two, gain, dest_own, dest_halo)


class Grid:
    def __init__(self, rows, heads):
        self.deep = rows // 2
        self.size = rows * heads
        row = lax.axis_index("rows")
        col = lax.axis_index("heads")
        self.z = row // 2
        self.x = row % 2
        self.y = col // 2
        self.c = col % 2

    def send(self, value, move):
        pairs = []
        for i in range(self.size):
            z, x, y, c = move(i // 8, (i // 4) % 2, (i // 2) % 2, i % 2)
            pairs.append((i, ((z * 2 + x) * 2 + y) * 2 + c))
        return lax.ppermute(value, AXES, pairs)

    def by_x(self, value):
        return self.send(value, lambda z, x, y, c: (z, 1 - x, y, c))

    def by_y(self, value):
        return self.send(value, lambda z, x, y, c: (z, x, 1 - y, c))

    def by_core(self, value):
        return self.send(value, lambda z, x, y, c: (z, x, y, 1 - c))

    def by_z(self, value, shift):
        return self.send(value, lambda z, x, y, c: ((z + shift) % self.deep, x, y, c))

    def gather_z(self, value):
        return [value] + [self.by_z(value, k) for k in range(1, self.deep)]

    def scatter_z(self, values):
        got = [self.by_z(values[k], self.deep - k) for k in range(1, self.deep)]
        total = values[0].astype(F32)
        for item in got:
            total = total + item.astype(F32)
        return total

    def spread(self, first, second):
        a_next, b_next = tie(self.by_y(first), self.by_x(second))
        a_zero = jnp.stack([first, a_next])
        b_zero = jnp.stack([second, b_next])
        return a_zero, b_zero

    def spread_more(self, a_zero, b_zero):
        return self.by_x(a_zero), self.by_y(b_zero)

    def fold(self, a_zero, b_zero, a_one, b_one):
        a_got, b_got = tie(self.by_x(a_one), self.by_y(b_one))
        a_last, b_last = tie(
            self.by_y(plus(a_zero[1], a_got[1])), self.by_x(plus(b_zero[1], b_got[1]))
        )
        return plus(a_zero[0], a_got[0], a_last), plus(b_zero[0], b_got[0], b_last)

    def to_absolute(self, blocks, z_axis, x_axis):
        size = self.deep
        turned = jnp.take(blocks, jnp.asarray([-m % size for m in range(size)]), axis=z_axis)
        turned = jnp.roll(turned, self.z, axis=z_axis)
        return jnp.where(self.x == 0, turned, jnp.flip(turned, axis=x_axis))

    def to_relative(self, blocks, z_axis, x_axis):
        size = self.deep
        turned = jnp.where(self.x == 0, blocks, jnp.flip(blocks, axis=x_axis))
        turned = jnp.roll(turned, -self.z, axis=z_axis)
        return jnp.take(turned, jnp.asarray([-m % size for m in range(size)]), axis=z_axis)


def tie(*values):
    return lax.optimization_barrier(values)


def plus(*values):
    total = values[0].astype(F32)
    for item in values[1:]:
        total = total + item.astype(F32)
    return total.astype(values[0].dtype)


def local(
    rows,
    heads,
    tokens,
    segment,
    live_token,
    prompt_slot,
    prompts,
    attn_gain,
    attn_shift,
    qkv_weight,
    out_weight,
    mlp_gain,
    mlp_shift,
    up_weight,
    up_bias,
    down_weight,
    cotangent,
):
    grid = Grid(rows, heads)
    deep = grid.deep
    count, wide = tokens.shape
    slots = IMGS_ROW * 2 * count // ROW
    place = jnp.stack([grid.z, grid.x, grid.y, grid.c]).astype(jnp.int32)

    def row_of(vec):
        return vec.astype(F32).reshape(1, -1)

    depth = qkv_weight.shape[0]
    third = qkv_weight.shape[2]
    shard = jnp.concatenate(
        [qkv_weight.reshape(depth, 3 * third), out_weight.swapaxes(0, 1)], axis=1
    ).reshape(2, depth // 2, 4 * third)
    got = grid.gather_z(shard)
    got = list(tie(*got))
    a_zero, b_zero = grid.spread(jnp.stack([g[0] for g in got]), jnp.stack([g[1] for g in got]))
    a_one, b_one = grid.spread_more(a_zero, b_zero)

    code = ((segment % IMGS_ROW) * 2 + live_token).astype(BF16)
    marks = jnp.pad(code[None], ((0, 15), (0, wide - count)))
    own = jnp.concatenate([tokens, cotangent, marks])
    other = grid.by_core(own)
    edge_source = jnp.where(grid.c == 1 - grid.y, 1, 0)
    first_row = jnp.where(grid.y == 0, count - HALO, 0)
    edge_parts = []
    for base, size in ((0, HALO), (count, HALO)):
        mine = lax.dynamic_slice_in_dim(own, base + first_row, size)
        theirs = lax.dynamic_slice_in_dim(other, base + first_row, size)
        edge_parts.append(jnp.where(edge_source == 1, mine, theirs))
    code_source = jnp.where(edge_source == 1, own[2 * count], other[2 * count])
    edge_code = lax.dynamic_slice_in_dim(code_source, first_row, HALO)
    edge_parts.append(jnp.pad(edge_code[None], ((0, 15), (0, wide - HALO))))
    halo = grid.by_y(jnp.concatenate(edge_parts))
    prom = jnp.pad(prompts, ((1, SLOT - PROMPTS - 1), (0, 0)))
    x_in, normed, cot, dest_own, dest_halo = prep(
        place, own, other, halo, prom, row_of(attn_gain), row_of(attn_shift), slots
    )

    hidden = up_weight.shape[1]
    span = hidden // 2
    shard = jnp.stack(
        [up_weight.swapaxes(0, 1).reshape(2, span, wide), down_weight.reshape(2, span, wide)],
        axis=1,
    )
    shard, got[0] = tie(shard, got[0])
    held = grid.gather_z(shard)
    bias = jnp.stack(grid.gather_z(up_bias.reshape(2, span)))
    bias = jnp.stack([bias, grid.by_x(bias)])
    bias = jnp.stack([bias, grid.by_y(bias)])
    mlp_a0, mlp_b0 = grid.spread(jnp.stack([h[0] for h in held]), jnp.stack([h[1] for h in held]))
    mlp_a1, mlp_b1 = grid.spread_more(mlp_a0, mlp_b0)
    bias_a = jnp.stack([bias[0, 0, :, 0], bias[1, 0, :, 0], bias[0, 0, :, 1], bias[0, 1, :, 1]])
    bias_b = jnp.stack([bias[0, 1, :, 0], bias[1, 1, :, 0], bias[1, 0, :, 1], bias[1, 1, :, 1]])

    blocks = jnp.stack(
        [
            jnp.concatenate(
                [(a_zero, a_one)[dx][dy], (b_zero, b_one)[dy][dx]], axis=1
            )
            for dy in range(2)
            for dx in range(2)
        ]
    ).reshape(2, 2, deep, depth, 4 * third)
    blocks = grid.to_absolute(blocks, 2, 1).swapaxes(1, 2)
    weight = blocks.reshape(2, 2 * deep * depth, 4 * third)
    qkv, prob, att, part = attend(normed, weight, slots)
    middle, normed_two = mid(
        x_in, part, grid.by_core(part), row_of(mlp_gain), row_of(mlp_shift), slots
    )

    fine = span % 16 == 0

    def enter(value):
        if fine:
            return value
        return value.swapaxes(1, 2).reshape(2, 1, 2, deep * span, wide)

    def leave(value):
        if fine:
            return value
        return value.reshape(2, 2, deep, span, wide).swapaxes(1, 2)

    o_sum, g_sum, grad_a0, grad_b0, grad_bias_a = mlp(
        enter(mlp_a0), enter(mlp_b0), normed_two, cot, row_of(bias_a), slots
    )
    o_part, g_part, grad_a1, grad_b1, grad_bias_b = mlp(
        enter(mlp_a1), enter(mlp_b1), normed_two, cot, row_of(bias_b), slots, (o_sum, g_sum)
    )
    g_other = grid.by_core(g_part)
    grad_a, grad_b = grid.fold(leave(grad_a0), leave(grad_b0), leave(grad_a1), leave(grad_b1))
    grad_shard = grid.scatter_z([jnp.stack([grad_a[k], grad_b[k]]) for k in range(deep)])
    grad_up = grad_shard[:, 0].reshape(hidden, wide).swapaxes(0, 1)
    grad_down = grad_shard[:, 1].reshape(hidden, wide)
    o_other = grid.by_core(o_part)
    out_own, out_halo = finish(middle, o_part, o_other, dest_own, dest_halo, slots)
    out_edge = grid.by_y(out_halo)

    grad_middle, grad_proj, grad_qkv, g_one, sums_two = back(
        middle, g_part, g_other, cot, row_of(mlp_gain), weight, qkv, prob, slots
    )
    g_one_other = grid.by_core(g_one)
    grad_weight = weight_grads(normed, grad_proj, grad_qkv, att)
    blocks = grad_weight.reshape(2, deep, 2, depth, 4 * third).swapaxes(1, 2)
    blocks = grid.to_relative(blocks, 2, 1)
    blocks = blocks.reshape(2, 2, deep, 2, depth // 2, 4 * third)
    att_a, att_b = grid.fold(
        blocks[:, 0, :, 0], blocks[0, :, :, 1], blocks[:, 1, :, 0], blocks[1, :, :, 1]
    )
    att_shard = grid.scatter_z([jnp.stack([att_a[k], att_b[k]]) for k in range(deep)])
    att_shard = att_shard.reshape(depth, 4 * third)
    grad_qkv_weight = att_shard[:, : 3 * third].reshape(depth, 3, third)
    grad_out_weight = att_shard[:, 3 * third :].swapaxes(0, 1)

    tok_own, tok_halo, prompt_sum, sums_one = last(
        x_in, grad_middle, g_one, g_one_other, row_of(attn_gain), dest_own, dest_halo, slots
    )
    tok_edge = grid.by_y(tok_halo)

    def merge(value, edge):
        edge = edge.astype(value.dtype)
        ends = jnp.where((grid.y == 0) & (grid.c == 1), edge, 0)
        begins = jnp.where((grid.y == 1) & (grid.c == 0), edge, 0)
        value = value.at[count - HALO :].add(ends)
        return value.at[:HALO].add(begins)

    g_a = grad_bias_a.reshape(4, deep, span)
    g_b = grad_bias_b.reshape(4, deep, span)
    bias_blocks = jnp.stack(
        [
            jnp.stack([jnp.stack([g_a[0], g_a[2]], 1), jnp.stack([g_b[0], g_a[3]], 1)]),
            jnp.stack([jnp.stack([g_a[1], g_b[2]], 1), jnp.stack([g_b[1], g_b[3]], 1)]),
        ]
    )
    bias_blocks = grid.to_absolute(bias_blocks, 2, 1)
    bias_blocks = jnp.where(grid.y == 0, bias_blocks, jnp.flip(bias_blocks, axis=0))
    small = jnp.concatenate(
        [prompt_sum, sums_one[:2], sums_two[:2], bias_blocks.reshape(-1, wide)]
    )
    small = small + grid.by_x(small)
    small = small + grid.by_y(small)
    stride = 1
    while stride < deep:
        small = small + grid.send(
            small, lambda z, x, y, c, stride=stride: (z ^ stride, x, y, c)
        )
        stride *= 2
    bias_all = small[60:].reshape(2, 2, deep, hidden)
    grad_bias = lax.dynamic_slice(
        bias_all, (grid.y, grid.x, grid.z, jnp.int32(0)), (1, 1, 1, hidden)
    ).reshape(hidden)
    return (
        merge(out_own, out_edge),
        merge(tok_own, tok_edge),
        small[1 : 1 + PROMPTS],
        small[56],
        small[57],
        grad_qkv_weight,
        grad_out_weight,
        small[58],
        small[59],
        grad_up,
        grad_bias,
        grad_down,
    )


def solution(mesh):
    both = P(AXES)
    lead = P(AXES, None)
    return jax.shard_map(
        functools.partial(local, mesh.shape["rows"], mesh.shape["heads"]),
        mesh=mesh,
        in_specs=(
            lead,
            both,
            both,
            both,
            P(),
            P(),
            P(),
            P("rows", None, "heads"),
            P("heads", "rows"),
            P(),
            P(),
            P(None, AXES),
            both,
            lead,
            lead,
        ),
        out_specs=(
            lead,
            lead,
            P(),
            P(),
            P(),
            P("rows", None, "heads"),
            P("heads", "rows"),
            P(),
            P(),
            P(None, AXES),
            both,
            lead,
        ),
        check_vma=False,
    )
```

```python
import functools

import jax
import jax.numpy as jnp
from jax import lax
from jax.experimental import pallas as pl
from jax.experimental.pallas import tpu as pltpu
from jax.sharding import PartitionSpec as P

HEAD = 64
ROW = 2048
IMG = 247
IMGS_ROW = 8
PROMPTS = 50
SLOT = 272
CORE = 256
HALO = 48
EPSILON = 1e-06
AXES = ("rows", "heads")
F32 = jnp.float32
BF16 = jnp.bfloat16
VMEM_LIMIT = 56 * 1024 * 1024

NN = (((1,), (0,)), ((), ()))
NT = (((1,), (1,)), ((), ()))
TN = (((0,), (0,)), ((), ()))


def dot(left, right, dims=NN):
    return lax.dot_general(left, right, dims, preferred_element_type=F32)


def whole(shape):
    return pl.BlockSpec(shape, lambda *_: (0,) * len(shape))


def params(**more):
    return pltpu.CompilerParams(vmem_limit_bytes=VMEM_LIMIT, **more)


COST = pl.CostEstimate(flops=1, bytes_accessed=1, transcendentals=0)


SMEM = pl.BlockSpec(memory_space=pltpu.SMEM)
ANY = pl.BlockSpec(memory_space=pl.ANY)


def stats(values):
    center = values - jnp.mean(values, axis=-1, keepdims=True)
    inverse = lax.rsqrt(jnp.mean(center * center, axis=-1, keepdims=True) + EPSILON)
    return center * inverse, inverse


def norm_back(grad, hat, inverse, gain):
    inner = grad * gain
    first = jnp.mean(inner, axis=-1, keepdims=True)
    second = jnp.mean(inner * hat, axis=-1, keepdims=True)
    return inverse * (inner - first - hat * second)


def prep_kernel(
    place, own, other, halo, prom, norms, x_out, n_out, cot_out, dest_own, dest_halo, d_oth
):
    step = pl.program_id(0)
    count = d_oth.shape[1]
    slots = pl.num_programs(0)
    y_at, c_at = place[2], place[3]

    @pl.when(step == 0)
    def _():
        big = 1 << 20
        spans = (
            (own[2 * count : 2 * count + 16, :count], 2 * count * y_at + count * c_at, True),
            (other[2 * count : 2 * count + 16, :count], 2 * count * y_at + count * (1 - c_at), True),
            (halo[2 * HALO : 2 * HALO + 16, :HALO], 2 * count - HALO * y_at, False),
        )
        parts = []
        for marks, base, home in spans:
            code = marks.astype(F32)[0:1].astype(jnp.int32)
            live = (code & 1) > 0
            slot = (code >> 1) - slots * y_at
            pos = base + lax.broadcasted_iota(jnp.int32, code.shape, 1)
            parts.append((live, slot, pos, home))
        starts = []
        for k in range(slots):
            low = None
            for live, slot, pos, home in parts:
                here = jnp.min(jnp.where(live & (slot == k), pos, big), axis=1, keepdims=True)
                low = here if low is None else jnp.minimum(low, here)
            starts.append(low)
        pads_own, pads_other = [
            jnp.sum(jnp.where(part[0], 0, 1), axis=1, keepdims=True) for part in parts[:2]
        ]
        befores = (c_at * pads_other, (1 - c_at) * pads_own, None)
        results = []
        for (live, slot, pos, home), before in zip(parts, befores):
            dest = jnp.full(pos.shape, -1, jnp.int32)
            for k in range(slots):
                dest = jnp.where(live & (slot == k), pos - starts[k] + k * SLOT, dest)
            if home:
                pads = jnp.where(live, 0.0, 1.0).astype(BF16)
                size = pads.shape[1]
                earlier = (
                    lax.broadcasted_iota(jnp.int32, (size, size), 0)
                    < lax.broadcasted_iota(jnp.int32, (size, size), 1)
                )
                wide = jnp.broadcast_to(pads, (16, size))
                rank = dot(wide, earlier.astype(BF16))[0:1].astype(jnp.int32) + before
                spare = (rank & (slots - 1)) * SLOT + IMG + (rank >> (slots.bit_length() - 1))
                dest = jnp.where(live, dest, spare)
            results.append(dest)
        dest_own[...] = results[0]
        d_oth[...] = results[1]
        dest_halo[...] = results[2]

    rows = step * SLOT
    tokens = cots = None
    for dest, ref, size in (
        (dest_own, own, count),
        (d_oth, other, count),
        (dest_halo, halo, HALO),
    ):
        at = rows + lax.broadcasted_iota(jnp.int32, (SLOT, size), 0)
        pick = (at == dest[...]).astype(BF16)
        one = dot(pick, ref[0:size])
        two = dot(pick, ref[size : 2 * size])
        tokens = one if tokens is None else tokens + one
        cots = two if cots is None else cots + two
    at = lax.broadcasted_iota(jnp.int32, (SLOT, 1), 0)
    slot_row = lax.broadcasted_iota(jnp.int32, (SLOT, PROMPTS), 0)
    which = lax.broadcasted_iota(jnp.int32, (SLOT, PROMPTS), 1)
    prompted = dot((slot_row == which + 1).astype(BF16), prom[...])
    inputs = jnp.where((at >= 1) & (at <= PROMPTS), prompted, tokens)
    hat, _ = stats(inputs)
    x_out[...] = inputs.astype(BF16)
    n_out[...] = (hat * norms[0:1] + norms[1:2]).astype(BF16)
    cot_out[...] = cots.astype(BF16)


def prep(place, own, other, halo, prom, norms, slots):
    count = own.shape[0] // 2 - 8
    wide = own.shape[1]
    rows = slots * SLOT
    tile = pl.BlockSpec((SLOT, wide), lambda t: (t, 0))
    array = jax.ShapeDtypeStruct((rows, wide), BF16)
    return pl.pallas_call(
        prep_kernel,
        grid=(slots,),
        in_specs=[SMEM] + [whole(v.shape) for v in (own, other, halo, prom, norms)],
        out_specs=[tile, tile, tile, whole((1, count)), whole((1, HALO))],
        out_shape=[
            array,
            array,
            array,
            jax.ShapeDtypeStruct((1, count), jnp.int32),
            jax.ShapeDtypeStruct((1, HALO), jnp.int32),
        ],
        scratch_shapes=[pltpu.VMEM((1, count), jnp.int32)],
        compiler_params=params(),
        cost_estimate=COST,
        name="prep",
    )(place, own, other, halo, prom, norms)


def weight_pieces(place, refs):
    if len(refs) == 1:
        for group in range(2):
            yield refs[0].at[group], group, 0, refs[0].shape[1]
        return
    a_zero, a_one, b_zero, b_one = refs
    deep, half = a_zero.shape[1], a_zero.shape[2]
    for dx in range(2):
        col = place[1] if dx == 0 else 1 - place[1]
        for dy in range(2):
            for k in range(deep):
                row = lax.rem(place[0] + deep - k, deep)
                for part in range(2):
                    ref = ((a_zero, a_one)[dx].at[dy, k], (b_zero, b_one)[dy].at[dx, k])[part]
                    first = ((row * 2 + col) * 2 + part) * half
                    yield ref, dy, pl.multiple_of(first, 16), half


def piece_count(held):
    return 2 if len(held) == 1 else 8 * held[0].shape[1]


def load_weight(place, held, weight, sem):
    copies = [
        pltpu.make_async_copy(ref, weight.at[group, pl.ds(first, size)], sem.at[i])
        for i, (ref, group, first, size) in enumerate(weight_pieces(place, held))
    ]
    for copy in copies:
        copy.start()
    for copy in copies:
        copy.wait()


def attend_kernel(held_count, place, normed, *refs):
    held = refs[:held_count]
    qkv_out, prob_out, att_out, part_out, weight, sem = refs[held_count:]

    @pl.when(pl.program_id(0) == 0)
    def _():
        load_weight(place, held, weight, sem)

    third = weight.shape[2] // 4
    rows = lax.broadcasted_iota(jnp.int32, (CORE, CORE), 0)
    cols = lax.broadcasted_iota(jnp.int32, (CORE, CORE), 1)
    allowed = ((rows < IMG) & (cols < IMG)) | (rows == cols)
    total = None
    for group in range(weight.shape[0]):
        qkv_out[group] = dot(normed[...], weight[group, :, : 3 * third]).astype(BF16)
        for head in range(third // HEAD):
            at = head * HEAD
            queries = qkv_out[group, :CORE, at : at + HEAD]
            keys = qkv_out[group, :CORE, third + at : third + at + HEAD]
            values = qkv_out[group, :, 2 * third + at : 2 * third + at + HEAD]
            scores = jnp.where(allowed, dot(queries, keys, NT) * 0.125, -1e30)
            exp_scores = jnp.exp(scores - jnp.max(scores, axis=-1, keepdims=True))
            probs = (exp_scores / jnp.sum(exp_scores, axis=-1, keepdims=True)).astype(BF16)
            prob_out[0, group, head] = probs
            att_out[group, :CORE, at : at + HEAD] = dot(probs, values[:CORE]).astype(BF16)
            att_out[group, CORE:, at : at + HEAD] = values[CORE:]
        part = dot(att_out[group], weight[group, :, 3 * third :], NT)
        total = part if total is None else total + part
    part_out[...] = total.astype(BF16)


def attend(place, normed, held, slots):
    rows, deep = normed.shape
    groups, wide = 2, held[0].shape[-1]
    third = wide // 4
    heads = third // HEAD
    return pl.pallas_call(
        functools.partial(attend_kernel, len(held)),
        grid=(slots,),
        in_specs=[SMEM, pl.BlockSpec((SLOT, deep), lambda t: (t, 0))] + [ANY] * len(held),
        out_specs=[
            pl.BlockSpec((groups, SLOT, 3 * third), lambda t: (0, t, 0)),
            pl.BlockSpec((1, groups, heads, CORE, CORE), lambda t: (t, 0, 0, 0, 0)),
            pl.BlockSpec((groups, SLOT, third), lambda t: (0, t, 0)),
            pl.BlockSpec((SLOT, deep), lambda t: (t, 0)),
        ],
        out_shape=[
            jax.ShapeDtypeStruct((groups, rows, 3 * third), BF16),
            jax.ShapeDtypeStruct((slots, groups, heads, CORE, CORE), BF16),
            jax.ShapeDtypeStruct((groups, rows, third), BF16),
            jax.ShapeDtypeStruct((rows, deep), BF16),
        ],
        scratch_shapes=[
            pltpu.VMEM((groups, deep, wide), BF16),
            pltpu.SemaphoreType.DMA((piece_count(held),)),
        ],
        compiler_params=params(),
        cost_estimate=COST,
        name="attend",
    )(place, normed, *held)


def mlp_kernel(more, *refs):
    if more:
        (a_in, b_in, normed, cot, bias, o_acc, g_acc, *refs) = refs
    else:
        (a_in, b_in, x_in, one, two, norms, cot, bias, middle_out, normed, *refs) = refs
    (o_out, g_out, a_out, b_out, bias_out, weight, act, grad, result, in_sem, out_sem) = refs
    step = pl.program_id(0)
    lead, count, _, span, _ = a_in.shape
    hidden = weight.shape[1]

    def pieces(first, second):
        for source, ref in enumerate((first, second)):
            for i in range(lead):
                for j in range(count):
                    for kind in range(2):
                        place = ((source * lead + i) * count + j) * span
                        index = ((source * lead + i) * count + j) * 2 + kind
                        yield ref.at[i, j, kind], kind, place, index

    @pl.when(step == 0)
    def _():
        copies = [
            pltpu.make_async_copy(ref, weight.at[kind, pl.ds(place, span)], in_sem.at[index])
            for ref, kind, place, index in pieces(a_in, b_in)
        ]
        for copy in copies:
            copy.start()
        bias_out[...] = jnp.zeros_like(bias_out)
        for copy in copies:
            copy.wait()

    rows = pl.ds(pl.multiple_of(step * SLOT, 16), SLOT)
    if not more:
        middle = x_in[...].astype(F32) + one[...].astype(F32) + two[...].astype(F32)
        middle_out[...] = middle
        hat, _ = stats(middle)
        normed[rows] = (hat * norms[2:3] + norms[3:4]).astype(BF16)
    tile_n = normed[rows]
    tile_c = cot[rows]
    cut = 256
    o_sum = o_acc[...] if more else None
    g_sum = g_acc[...] if more else None
    for at in range(0, hidden, cut):
        up = weight[0, at : at + cut]
        down = weight[1, at : at + cut]
        pre = dot(tile_n, up, NT) + bias[:, at : at + cut]
        cdf = 0.5 * (1.0 + lax.erf(pre * 0.7071067811865476))
        pdf = jnp.exp(-0.5 * pre * pre) * 0.3989422804014327
        low = (pre * cdf).astype(BF16)
        grad_low = (dot(tile_c, down, NT) * (cdf + pre * pdf)).astype(BF16)
        act[rows, at : at + cut] = low
        grad[rows, at : at + cut] = grad_low
        bias_out[:, at : at + cut] += jnp.sum(grad_low.astype(F32), axis=0, keepdims=True)
        o_part = dot(low, down)
        g_part = dot(grad_low, up)
        o_sum = o_part if o_sum is None else o_sum + o_part
        g_sum = g_part if g_sum is None else g_sum + g_part
    o_out[...] = o_sum.astype(o_out.dtype)
    g_out[...] = g_sum.astype(g_out.dtype)

    @pl.when(step == pl.num_programs(0) - 1)
    def _():
        def tile(i, _):
            at = pl.ds(pl.multiple_of(i * cut, cut), cut)
            result[0, at] = dot(grad[:, at], normed[...], TN).astype(BF16)
            result[1, at] = dot(act[:, at], cot[...], TN).astype(BF16)
            return 0

        lax.fori_loop(0, hidden // cut, tile, 0)
        copies = [
            pltpu.make_async_copy(result.at[kind, pl.ds(place, span)], ref, out_sem.at[index])
            for ref, kind, place, index in pieces(a_out, b_out)
        ]
        for copy in copies:
            copy.start()
        for copy in copies:
            copy.wait()


def mlp(a_in, b_in, cot, bias, slots, start=None, sums=None):
    rows, wide = cot.shape
    hidden = bias.shape[1]
    more = sums is not None
    tile = pl.BlockSpec((SLOT, wide), lambda t: (t, 0))
    wide_f32, wide_bf16 = (jax.ShapeDtypeStruct((rows, wide), kind) for kind in (F32, BF16))
    kept = wide_bf16 if more else wide_f32
    count = 4 * a_in.shape[0] * a_in.shape[1]
    full = whole(cot.shape)
    if more:
        operands = (a_in, b_in, start, cot, bias, *sums)
        specs = [ANY, ANY, full, full, whole(bias.shape), tile, tile]
    else:
        x_in, one, two, norms = start
        operands = (a_in, b_in, x_in, one, two, norms, cot, bias)
        specs = [ANY, ANY, tile, tile, tile, whole(norms.shape), full, whole(bias.shape)]
    return pl.pallas_call(
        functools.partial(mlp_kernel, more),
        grid=(slots,),
        in_specs=specs,
        out_specs=([] if more else [tile, full]) + [tile, tile, ANY, ANY, whole(bias.shape)],
        out_shape=([] if more else [wide_f32, wide_bf16])
        + [
            kept,
            kept,
            jax.ShapeDtypeStruct(a_in.shape, BF16),
            jax.ShapeDtypeStruct(b_in.shape, BF16),
            jax.ShapeDtypeStruct(bias.shape, F32),
        ],
        scratch_shapes=[
            pltpu.VMEM((2, hidden, wide), BF16),
            pltpu.VMEM((rows, hidden), BF16),
            pltpu.VMEM((rows, hidden), BF16),
            pltpu.VMEM((2, hidden, wide), BF16),
            pltpu.SemaphoreType.DMA((count,)),
            pltpu.SemaphoreType.DMA((count,)),
        ],
        compiler_params=params(),
        cost_estimate=COST,
        name="mlp",
    )(*operands)


def add_kernel(a_zero, a_got, b_zero, b_got, a_out, b_out):
    for zero, got, out in ((a_zero, a_got, a_out), (b_zero, b_got, b_out)):
        out[...] = (zero[0].astype(F32) + got[0].astype(F32)).astype(BF16)


def add_second(a_zero, a_got, b_zero, b_got):
    shape = a_zero.shape[1:]
    block = pl.BlockSpec((1, 1) + shape[1:], lambda k: (1, k) + (0,) * (len(shape) - 1))
    out = pl.BlockSpec((1,) + shape[1:], lambda k: (k,) + (0,) * (len(shape) - 1))
    return pl.pallas_call(
        add_kernel,
        grid=(shape[0],),
        in_specs=[block] * 4,
        out_specs=[out] * 2,
        out_shape=[jax.ShapeDtypeStruct(shape, BF16)] * 2,
        compiler_params=params(),
        cost_estimate=COST,
        name="add_second",
    )(a_zero, a_got, b_zero, b_got)


def fold_kernel(a_zero, a_got, a_last, b_zero, b_got, b_last, *outs):
    for part, (zero, got, last_got) in enumerate(((a_zero, a_got, a_last), (b_zero, b_got, b_last))):
        for k, out in enumerate(outs):
            total = zero[0, k].astype(F32) + got[0, k].astype(F32) + last_got[k].astype(F32)
            out[part] = total.astype(BF16)


def fold_first(a_zero, a_got, a_last, b_zero, b_got, b_last):
    shape = a_last.shape
    first = whole((1,) + shape)
    out = (2,) + shape[1:]
    return pl.pallas_call(
        fold_kernel,
        grid=(1,),
        in_specs=[first, first, whole(shape)] * 2,
        out_specs=[whole(out)] * shape[0],
        out_shape=[jax.ShapeDtypeStruct(out, BF16)] * shape[0],
        compiler_params=params(),
        cost_estimate=COST,
        name="fold_first",
    )(a_zero, a_got, a_last, b_zero, b_got, b_last)


def finish_kernel(middle, one, two, dest_own, dest_halo, own_out, halo_out, total, total_halo):
    step = pl.program_id(0)
    value = middle[...] + one[...].astype(F32) + two[...].astype(F32)
    spread_rows(step, value.astype(BF16), dest_own, dest_halo, total, total_halo)

    @pl.when(step == pl.num_programs(0) - 1)
    def _():
        own_out[...] = total[...].astype(own_out.dtype)
        halo_out[...] = total_halo[...].astype(halo_out.dtype)


def spread_rows(step, value, dest_own, dest_halo, total, total_halo):
    for dest, sum_ref in ((dest_own, total), (dest_halo, total_halo)):
        at = step * SLOT + lax.broadcasted_iota(jnp.int32, (SLOT, dest.shape[1]), 0)
        part = dot((at == dest[...]).astype(BF16), value, TN)
        sum_ref[...] = jnp.where(step == 0, part, sum_ref[...] + part)


def finish(middle, one, two, dest_own, dest_halo, slots):
    rows, wide = middle.shape
    count = dest_own.shape[1]
    tile = pl.BlockSpec((SLOT, wide), lambda t: (t, 0))
    return pl.pallas_call(
        finish_kernel,
        grid=(slots,),
        in_specs=[tile, tile, tile, whole(dest_own.shape), whole(dest_halo.shape)],
        out_specs=[whole((count, wide)), whole((HALO, wide))],
        out_shape=[
            jax.ShapeDtypeStruct((count, wide), BF16),
            jax.ShapeDtypeStruct((HALO, wide), BF16),
        ],
        scratch_shapes=[pltpu.VMEM((count, wide), F32), pltpu.VMEM((HALO, wide), F32)],
        compiler_params=params(),
        cost_estimate=COST,
        name="finish",
    )(middle, one, two, dest_own, dest_halo)


def back_kernel(held_count, place, middle, one, two, cot, norms, qkv, prob, *refs):
    held = refs[:held_count]
    gm_out, gp_out, dq_out, part_out, sums_out, weight, sem = refs[held_count:]
    step = pl.program_id(0)
    third = weight.shape[2] // 4

    @pl.when(step == 0)
    def _():
        sums_out[...] = jnp.zeros_like(sums_out)
        load_weight(place, held, weight, sem)

    grad = one[...].astype(F32) + two[...].astype(F32)
    hat, inverse = stats(middle[...])
    sums_out[0:1] += jnp.sum(grad * hat, axis=0, keepdims=True)
    sums_out[1:2] += jnp.sum(grad, axis=0, keepdims=True)
    grad_middle = cot[...].astype(F32) + norm_back(grad, hat, inverse, norms[2:3])
    gm_out[...] = grad_middle
    grad_proj = grad_middle.astype(BF16)
    gp_out[...] = grad_proj
    total = None
    for group in range(weight.shape[0]):
        grad_att = dot(grad_proj, weight[group, :, 3 * third :]).astype(BF16)
        for head in range(third // HEAD):
            at = head * HEAD
            queries = qkv[group, :CORE, at : at + HEAD]
            keys = qkv[group, :CORE, third + at : third + at + HEAD]
            values = qkv[group, :CORE, 2 * third + at : 2 * third + at + HEAD]
            grad_head = grad_att[:, at : at + HEAD]
            grad_core = grad_head[:CORE]
            probs = prob[0, group, head]
            probs_wide = probs.astype(F32)
            grad_probs = dot(grad_core, values, NT)
            center = jnp.sum(probs_wide * grad_probs, axis=-1, keepdims=True)
            grad_scores = (probs_wide * (grad_probs - center)).astype(BF16)
            grad_q = (dot(grad_scores, keys) * 0.125).astype(BF16)
            grad_k = (dot(grad_scores, queries, TN) * 0.125).astype(BF16)
            grad_v = dot(probs, grad_core, TN).astype(BF16)
            blank = jnp.zeros((SLOT - CORE, HEAD), BF16)
            dq_out[group, :CORE, at : at + HEAD] = grad_q
            dq_out[group, CORE:, at : at + HEAD] = blank
            dq_out[group, :CORE, third + at : third + at + HEAD] = grad_k
            dq_out[group, CORE:, third + at : third + at + HEAD] = blank
            dq_out[group, :CORE, 2 * third + at : 2 * third + at + HEAD] = grad_v
            dq_out[group, CORE:, 2 * third + at : 2 * third + at + HEAD] = grad_head[CORE:]
        part = dot(dq_out[group], weight[group, :, : 3 * third], NT)
        total = part if total is None else total + part
    part_out[...] = total.astype(BF16)


def back(place, middle, one, two, cot, norms, held, qkv, prob, slots):
    rows, wide = middle.shape
    groups, third = qkv.shape[0], qkv.shape[2] // 3
    tile = pl.BlockSpec((SLOT, wide), lambda t: (t, 0))
    tile_q = pl.BlockSpec((groups, SLOT, 3 * third), lambda t: (0, t, 0))
    return pl.pallas_call(
        functools.partial(back_kernel, len(held)),
        grid=(slots,),
        in_specs=[
            SMEM,
            tile,
            tile,
            tile,
            tile,
            whole(norms.shape),
            tile_q,
            pl.BlockSpec((1,) + prob.shape[1:], lambda t: (t, 0, 0, 0, 0)),
        ]
        + [ANY] * len(held),
        out_specs=[tile, tile, tile_q, tile, whole((8, wide))],
        out_shape=[
            jax.ShapeDtypeStruct((rows, wide), F32),
            jax.ShapeDtypeStruct((rows, wide), BF16),
            jax.ShapeDtypeStruct(qkv.shape, BF16),
            jax.ShapeDtypeStruct((rows, wide), BF16),
            jax.ShapeDtypeStruct((8, wide), F32),
        ],
        scratch_shapes=[
            pltpu.VMEM((groups, wide, 4 * third), BF16),
            pltpu.SemaphoreType.DMA((piece_count(held),)),
        ],
        compiler_params=params(),
        cost_estimate=COST,
        name="back",
    )(place, middle, one, two, cot, norms, qkv, prob, *held)


def weight_kernel(held_count, place, normed, grad_proj, grad_qkv, att, *refs):
    held = refs[:held_count]
    result, sem = refs[held_count:]
    third = att.shape[2]
    cut = normed.shape[1]
    at = pl.ds(pl.multiple_of(pl.program_id(0) * cut, cut), cut)
    for group in range(2):
        result[group, at, : 3 * third] = dot(normed[...], grad_qkv[group], TN).astype(BF16)
        result[group, at, 3 * third :] = dot(grad_proj[...], att[group], TN).astype(BF16)

    @pl.when(pl.program_id(0) == pl.num_programs(0) - 1)
    def _():
        copies = [
            pltpu.make_async_copy(result.at[group, pl.ds(first, size)], ref, sem.at[i])
            for i, (ref, group, first, size) in enumerate(weight_pieces(place, held))
        ]
        for copy in copies:
            copy.start()
        for copy in copies:
            copy.wait()


def weight_grads(place, normed, grad_proj, grad_qkv, att, held):
    rows, wide = normed.shape
    groups, _, third = att.shape
    cut = 256
    tall = pl.BlockSpec((rows, cut), lambda d: (0, d))
    return pl.pallas_call(
        functools.partial(weight_kernel, len(held)),
        grid=(wide // cut,),
        in_specs=[SMEM, tall, tall, whole(grad_qkv.shape), whole(att.shape)],
        out_specs=[ANY] * len(held),
        out_shape=[jax.ShapeDtypeStruct(v.shape, BF16) for v in held],
        scratch_shapes=[
            pltpu.VMEM((groups, wide, 4 * third), BF16),
            pltpu.SemaphoreType.DMA((piece_count(held),)),
        ],
        compiler_params=params(),
        cost_estimate=COST,
        name="weight_grads",
    )(place, normed, grad_proj, grad_qkv, att)


def last_kernel(
    x_in, gm, one, two, norms, dest_own, dest_halo, own_out, halo_out, prompt_out, sums_out, halo_sum
):
    step = pl.program_id(0)

    @pl.when(step == 0)
    def _():
        sums_out[...] = jnp.zeros_like(sums_out)
        prompt_out[...] = jnp.zeros_like(prompt_out)

    grad = one[...].astype(F32) + two[...].astype(F32)
    hat, inverse = stats(x_in[...].astype(F32))
    sums_out[0:1] += jnp.sum(grad * hat, axis=0, keepdims=True)
    sums_out[1:2] += jnp.sum(grad, axis=0, keepdims=True)
    grad_in = gm[...] + norm_back(grad, hat, inverse, norms[0:1])
    prompt_out[...] += grad_in[: prompt_out.shape[0]]
    at = lax.broadcasted_iota(jnp.int32, (SLOT, 1), 0)
    value = jnp.where((at >= 1) & (at <= PROMPTS), 0.0, grad_in).astype(BF16)
    spread_rows(step, value, dest_own, dest_halo, own_out, halo_sum)

    @pl.when(step == pl.num_programs(0) - 1)
    def _():
        halo_out[...] = halo_sum[...].astype(BF16)


def last(x_in, gm, one, two, norms, dest_own, dest_halo, slots):
    rows, wide = x_in.shape
    count = dest_own.shape[1]
    tile = pl.BlockSpec((SLOT, wide), lambda t: (t, 0))
    return pl.pallas_call(
        last_kernel,
        grid=(slots,),
        in_specs=[tile] * 4 + [whole(norms.shape), whole(dest_own.shape), whole(dest_halo.shape)],
        out_specs=[whole((count, wide)), whole((HALO, wide)), whole((56, wide)), whole((8, wide))],
        out_shape=[
            jax.ShapeDtypeStruct((count, wide), F32),
            jax.ShapeDtypeStruct((HALO, wide), BF16),
            jax.ShapeDtypeStruct((56, wide), F32),
            jax.ShapeDtypeStruct((8, wide), F32),
        ],
        scratch_shapes=[pltpu.VMEM((HALO, wide), F32)],
        compiler_params=params(),
        cost_estimate=COST,
        name="last",
    )(x_in, gm, one, two, norms, dest_own, dest_halo)


class Grid:
    def __init__(self, rows, heads):
        self.deep = rows // 2
        self.size = rows * heads
        row = lax.axis_index("rows")
        col = lax.axis_index("heads")
        self.z = row // 2
        self.x = row % 2
        self.y = col // 2
        self.c = col % 2

    def send(self, value, move):
        pairs = []
        for i in range(self.size):
            z, x, y, c = move(i // 8, (i // 4) % 2, (i // 2) % 2, i % 2)
            pairs.append((i, ((z * 2 + x) * 2 + y) * 2 + c))
        return lax.ppermute(value, AXES, pairs)

    def by_x(self, value):
        return self.send(value, lambda z, x, y, c: (z, 1 - x, y, c))

    def by_y(self, value):
        return self.send(value, lambda z, x, y, c: (z, x, 1 - y, c))

    def by_core(self, value):
        return self.send(value, lambda z, x, y, c: (z, x, y, 1 - c))

    def by_z(self, value, shift):
        return self.send(value, lambda z, x, y, c: ((z + shift) % self.deep, x, y, c))

    def gather_z(self, value):
        return [value] + [self.by_z(value, k) for k in range(1, self.deep)]

    def scatter_z(self, values, earlier):
        got = [self.by_z(values[k], self.deep - k) for k in range(1, self.deep)]
        got = tie(*got, earlier)[:-1]
        total = values[0].astype(F32)
        for item in got:
            total = total + item.astype(F32)
        return total

    def spread(self, first, second):
        a_next, b_next = tie(self.by_y(first), self.by_x(second))
        a_zero = jnp.stack([first, a_next])
        b_zero = jnp.stack([second, b_next])
        return a_zero, b_zero

    def spread_more(self, a_zero, b_zero):
        return self.by_x(a_zero), self.by_y(b_zero)

    def to_absolute(self, blocks, z_axis, x_axis):
        size = self.deep
        turned = jnp.take(blocks, jnp.asarray([-m % size for m in range(size)]), axis=z_axis)
        turned = jnp.roll(turned, self.z, axis=z_axis)
        return jnp.where(self.x == 0, turned, jnp.flip(turned, axis=x_axis))

    def to_relative(self, blocks, z_axis, x_axis):
        size = self.deep
        turned = jnp.where(self.x == 0, blocks, jnp.flip(blocks, axis=x_axis))
        turned = jnp.roll(turned, -self.z, axis=z_axis)
        return jnp.take(turned, jnp.asarray([-m % size for m in range(size)]), axis=z_axis)


def tie(*values):
    return lax.optimization_barrier(values)


def after(value, *earlier):
    return lax.optimization_barrier((value, *earlier))[0]


def local(
    rows,
    heads,
    tokens,
    segment,
    live_token,
    prompt_slot,
    prompts,
    attn_gain,
    attn_shift,
    qkv_weight,
    out_weight,
    mlp_gain,
    mlp_shift,
    up_weight,
    up_bias,
    down_weight,
    cotangent,
):
    grid = Grid(rows, heads)
    deep = grid.deep
    count, wide = tokens.shape
    slots = IMGS_ROW * 2 * count // ROW
    place = jnp.stack([grid.z, grid.x, grid.y, grid.c]).astype(jnp.int32)

    def row_of(vec):
        return vec.astype(F32).reshape(1, -1)

    norms = jnp.stack([attn_gain, attn_shift, mlp_gain, mlp_shift]).astype(F32)

    depth = qkv_weight.shape[0]
    third = qkv_weight.shape[2]
    shard = jnp.concatenate(
        [qkv_weight.reshape(depth, 3 * third), out_weight.swapaxes(0, 1)], axis=1
    ).reshape(2, depth // 2, 4 * third)
    hidden = up_weight.shape[1]
    span = hidden // 2
    bias = jnp.stack(grid.gather_z(up_bias.reshape(2, span)))
    bias = jnp.stack([bias, grid.by_x(bias)])
    bias = jnp.stack([bias, grid.by_y(bias)])
    *got, bias = tie(*grid.gather_z(shard), bias)

    code = ((segment % IMGS_ROW) * 2 + live_token).astype(BF16)
    marks = jnp.pad(code[None], ((0, 15), (0, wide - count)))
    own = after(jnp.concatenate([tokens, cotangent, marks]), shard)
    other = grid.by_core(own)
    mine = grid.c == 1 - grid.y
    first_row = jnp.where(grid.y == 0, count - HALO, 0)
    edge_parts = []
    for base in (0, count):
        edge_parts.append(
            jnp.where(
                mine,
                lax.dynamic_slice_in_dim(own, base + first_row, HALO),
                lax.dynamic_slice_in_dim(other, base + first_row, HALO),
            )
        )
    edge_code = jnp.where(mine, own[2 * count :], other[2 * count :])
    edge_code = jnp.where(grid.y == 0, edge_code[:, count - HALO : count], edge_code[:, :HALO])
    edge_parts.append(jnp.pad(edge_code, ((0, 0), (0, wide - HALO))))
    edge = jnp.concatenate(edge_parts)
    halo = grid.by_y(edge)

    a_zero, b_zero = grid.spread(jnp.stack([g[0] for g in got]), jnp.stack([g[1] for g in got]))
    a_zero, b_zero, _ = tie(a_zero, b_zero, edge)
    a_one, b_one = grid.spread_more(a_zero, b_zero)
    x_in, normed, cot, dest_own, dest_halo = prep(place, own, other, halo, prompts, norms, slots)

    shard = jnp.stack(
        [up_weight.swapaxes(0, 1).reshape(2, span, wide), down_weight.reshape(2, span, wide)],
        axis=1,
    )
    shard = after(shard, got[0])
    held = tie(*grid.gather_z(shard), normed)[:deep]
    mlp_a = jnp.stack([h[0] for h in held])
    mlp_b = jnp.stack([h[1] for h in held])
    mlp_a0, mlp_b0 = grid.spread(mlp_a, mlp_b)
    mlp_a1, mlp_b1 = grid.spread_more(mlp_a0, mlp_b0)
    bias_a = jnp.stack([bias[0, 0, :, 0], bias[1, 0, :, 0], bias[0, 0, :, 1], bias[0, 1, :, 1]])
    bias_b = jnp.stack([bias[0, 1, :, 0], bias[1, 1, :, 0], bias[1, 0, :, 1], bias[1, 1, :, 1]])

    weights = [a_zero, a_one, b_zero, b_one]
    if (depth // 2) % 16:
        blocks = jnp.stack(
            [
                jnp.concatenate([(a_zero, a_one)[dx][dy], (b_zero, b_one)[dy][dx]], axis=1)
                for dy in range(2)
                for dx in range(2)
            ]
        ).reshape(2, 2, deep, depth, 4 * third)
        blocks = grid.to_absolute(blocks, 2, 1).swapaxes(1, 2)
        weights = [blocks.reshape(2, 2 * deep * depth, 4 * third)]
    qkv, prob, att, part = attend(place, normed, weights, slots)

    fine = span % 16 == 0

    def enter(value):
        if fine:
            return value
        return value.swapaxes(1, 2).reshape(2, 1, 2, deep * span, wide)

    def leave(value):
        if fine:
            return value
        return value.reshape(2, 2, deep, span, wide).swapaxes(1, 2)

    start = (x_in, part, grid.by_core(part), norms)
    middle, normed_two, o_sum, g_sum, grad_a0, grad_b0, grad_bias_a = mlp(
        enter(mlp_a0), enter(mlp_b0), cot, row_of(bias_a), slots, start
    )
    o_part, g_part, grad_a1, grad_b1, grad_bias_b = mlp(
        enter(mlp_a1), enter(mlp_b1), cot, row_of(bias_b), slots, normed_two, (o_sum, g_sum)
    )
    grad_a0, grad_b0 = leave(grad_a0), leave(grad_b0)
    a_got, b_got = grid.by_x(leave(grad_a1)), grid.by_y(leave(grad_b1))
    g_other = grid.by_core(g_part)
    o_other = grid.by_core(after(o_part, g_other))

    grad_middle, grad_proj, grad_qkv, g_one, sums_two = back(
        place, middle, g_part, g_other, cot, norms, weights, qkv, prob, slots
    )
    g_one_other = grid.by_core(g_one)
    a_got, b_got, _ = tie(a_got, b_got, g_one)
    a_send, b_send = add_second(grad_a0, a_got, grad_b0, b_got)
    a_last, b_last = grid.by_y(a_send), grid.by_x(b_send)
    weight_blocks = weight_grads(
        place, after(normed, a_send), grad_proj, grad_qkv, att, weights
    )
    if len(weight_blocks) == 1:
        blocks = weight_blocks[0].reshape(2, deep, 2, depth, 4 * third).swapaxes(1, 2)
        blocks = grid.to_relative(blocks, 2, 1)
        blocks = blocks.reshape(2, 2, deep, 2, depth // 2, 4 * third)
        weight_blocks = [
            blocks[:, 0, :, 0],
            blocks[:, 1, :, 0],
            blocks[0, :, :, 1],
            blocks[1, :, :, 1],
        ]
    att_a0, att_a1, att_b0, att_b1 = weight_blocks
    att_a_got, att_b_got = grid.by_x(att_a1), grid.by_y(att_b1)
    a_last, b_last, _ = tie(a_last, b_last, att_a1)
    pieces = fold_first(grad_a0, a_got, a_last, grad_b0, b_got, b_last)

    att_a_got, att_b_got, _ = tie(att_a_got, att_b_got, pieces[0])
    a_send, b_send = add_second(att_a0, att_a_got, att_b0, att_b_got)
    att_a_last, att_b_last = grid.by_y(a_send), grid.by_x(b_send)
    tok_own, tok_halo, prompt_sum, sums_one = last(
        x_in, grad_middle, g_one, after(g_one_other, a_send), norms, dest_own, dest_halo, slots
    )
    tok_edge = grid.by_y(tok_halo)
    att_a_last, att_b_last, _ = tie(att_a_last, att_b_last, tok_halo)
    att_pieces = fold_first(att_a0, att_a_got, att_a_last, att_b0, att_b_got, att_b_last)
    out_own, out_halo = finish(
        middle, o_part, after(o_other, att_pieces[0]), dest_own, dest_halo, slots
    )
    out_edge = grid.by_y(out_halo)
    grad_shard = grid.scatter_z(pieces, out_halo)
    grad_up = grad_shard[:, 0].reshape(hidden, wide).swapaxes(0, 1)
    grad_down = grad_shard[:, 1].reshape(hidden, wide)
    att_shard = grid.scatter_z(att_pieces, out_halo)
    att_shard = att_shard.reshape(depth, 4 * third)
    grad_qkv_weight = att_shard[:, : 3 * third].reshape(depth, 3, third)
    grad_out_weight = att_shard[:, 3 * third :].swapaxes(0, 1)

    def merge(value, edge):
        edge = edge.astype(value.dtype)
        ends = jnp.where((grid.y == 0) & (grid.c == 1), edge, 0)
        begins = jnp.where((grid.y == 1) & (grid.c == 0), edge, 0)
        value = value.at[count - HALO :].add(ends)
        return value.at[:HALO].add(begins)

    g_a = grad_bias_a.reshape(4, deep, span)
    g_b = grad_bias_b.reshape(4, deep, span)
    bias_blocks = jnp.stack(
        [
            jnp.stack([jnp.stack([g_a[0], g_a[2]], 1), jnp.stack([g_b[0], g_a[3]], 1)]),
            jnp.stack([jnp.stack([g_a[1], g_b[2]], 1), jnp.stack([g_b[1], g_b[3]], 1)]),
        ]
    )
    bias_blocks = grid.to_absolute(bias_blocks, 2, 1)
    bias_blocks = jnp.where(grid.y == 0, bias_blocks, jnp.flip(bias_blocks, axis=0))
    small = jnp.concatenate(
        [prompt_sum, sums_one[:2], sums_two[:2], bias_blocks.reshape(-1, wide)]
    )
    small = small + grid.by_x(small)
    small = small + grid.by_y(small)
    stride = 1
    while stride < deep:
        small = small + grid.send(
            small, lambda z, x, y, c, stride=stride: (z ^ stride, x, y, c)
        )
        stride *= 2
    bias_all = small[60:].reshape(2, 2, deep, hidden)
    grad_bias = lax.dynamic_slice(
        bias_all, (grid.y, grid.x, grid.z, jnp.int32(0)), (1, 1, 1, hidden)
    ).reshape(hidden)
    return (
        merge(out_own, out_edge),
        merge(tok_own, tok_edge),
        small[1 : 1 + PROMPTS],
        small[56],
        small[57],
        grad_qkv_weight,
        grad_out_weight,
        small[58],
        small[59],
        grad_up,
        grad_bias,
        grad_down,
    )


def solution(mesh):
    both = P(AXES)
    lead = P(AXES, None)
    return jax.shard_map(
        functools.partial(local, mesh.shape["rows"], mesh.shape["heads"]),
        mesh=mesh,
        in_specs=(
            lead,
            both,
            both,
            both,
            P(),
            P(),
            P(),
            P("rows", None, "heads"),
            P("heads", "rows"),
            P(),
            P(),
            P(None, AXES),
            both,
            lead,
            lead,
        ),
        out_specs=(
            lead,
            lead,
            P(),
            P(),
            P(),
            P("rows", None, "heads"),
            P("heads", "rows"),
            P(),
            P(),
            P(None, AXES),
            both,
            lead,
        ),
        check_vma=False,
    )
```

```python
import functools

import jax
import jax.numpy as jnp
from jax import lax
from jax.experimental import pallas as pl
from jax.experimental.pallas import tpu as pltpu
from jax.sharding import PartitionSpec as P

HEAD = 64
ROW = 2048
IMG = 247
IMGS_ROW = 8
PROMPTS = 50
SLOT = 272
CORE = 256
TAIL = 16
HALO = 48
EPSILON = 1e-06
AXES = ("rows", "heads")
F32 = jnp.float32
BF16 = jnp.bfloat16
VMEM_LIMIT = 56 * 1024 * 1024

NN = (((1,), (0,)), ((), ()))
NT = (((1,), (1,)), ((), ()))
TN = (((0,), (0,)), ((), ()))


def dot(left, right, dims=NN):
    return lax.dot_general(left, right, dims, preferred_element_type=F32)


def whole(shape):
    return pl.BlockSpec(shape, lambda *_: (0,) * len(shape))


def params(**more):
    return pltpu.CompilerParams(vmem_limit_bytes=VMEM_LIMIT, **more)


SCALE = 0.15


def cost(time):
    return pl.CostEstimate(flops=int(time * SCALE * 1.15e9), bytes_accessed=1, transcendentals=0)


SMEM = pl.BlockSpec(memory_space=pltpu.SMEM)
ANY = pl.BlockSpec(memory_space=pl.ANY)


def stats(values):
    center = values - jnp.mean(values, axis=-1, keepdims=True)
    inverse = lax.rsqrt(jnp.mean(center * center, axis=-1, keepdims=True) + EPSILON)
    return center * inverse, inverse


def norm_back(grad, hat, inverse, gain):
    inner = grad * gain
    first = jnp.mean(inner, axis=-1, keepdims=True)
    second = jnp.mean(inner * hat, axis=-1, keepdims=True)
    return inverse * (inner - first - hat * second)


def prep_kernel(
    place, own, other, halo, prom, norms, x_out, n_out, cot_out, dest_own, dest_halo, d_oth
):
    step = pl.program_id(0)
    count = d_oth.shape[1]
    slots = pl.num_programs(0)
    y_at, c_at = place[2], place[3]

    @pl.when(step == 0)
    def _():
        big = 1 << 20
        spans = (
            (own[2 * count : 2 * count + 16, :count], 2 * count * y_at + count * c_at, True),
            (other[2 * count : 2 * count + 16, :count], 2 * count * y_at + count * (1 - c_at), True),
            (halo[2 * HALO : 2 * HALO + 16, :HALO], 2 * count - HALO * y_at, False),
        )
        parts = []
        for marks, base, home in spans:
            code = marks.astype(F32)[0:1].astype(jnp.int32)
            live = (code & 1) > 0
            slot = (code >> 1) - slots * y_at
            pos = base + lax.broadcasted_iota(jnp.int32, code.shape, 1)
            parts.append((live, slot, pos, home))
        starts = []
        for k in range(slots):
            low = None
            for live, slot, pos, home in parts:
                here = jnp.min(jnp.where(live & (slot == k), pos, big), axis=1, keepdims=True)
                low = here if low is None else jnp.minimum(low, here)
            starts.append(low)
        pads_own, pads_other = [
            jnp.sum(jnp.where(part[0], 0, 1), axis=1, keepdims=True) for part in parts[:2]
        ]
        befores = (c_at * pads_other, (1 - c_at) * pads_own, None)
        results = []
        for (live, slot, pos, home), before in zip(parts, befores):
            dest = jnp.full(pos.shape, -1, jnp.int32)
            for k in range(slots):
                dest = jnp.where(live & (slot == k), pos - starts[k] + k * SLOT, dest)
            if home:
                pads = jnp.where(live, 0.0, 1.0).astype(BF16)
                size = pads.shape[1]
                earlier = (
                    lax.broadcasted_iota(jnp.int32, (size, size), 0)
                    < lax.broadcasted_iota(jnp.int32, (size, size), 1)
                )
                wide = jnp.broadcast_to(pads, (16, size))
                rank = dot(wide, earlier.astype(BF16))[0:1].astype(jnp.int32) + before
                spare = (rank & (slots - 1)) * SLOT + IMG + (rank >> (slots.bit_length() - 1))
                dest = jnp.where(live, dest, spare)
            results.append(dest)
        dest_own[...] = results[0]
        d_oth[...] = results[1]
        dest_halo[...] = results[2]

    rows = step * SLOT
    tokens = cots = None
    for dest, ref, size in (
        (dest_own, own, count),
        (d_oth, other, count),
        (dest_halo, halo, HALO),
    ):
        at = rows + lax.broadcasted_iota(jnp.int32, (SLOT, size), 0)
        pick = (at == dest[...]).astype(BF16)
        one = dot(pick, ref[0:size])
        two = dot(pick, ref[size : 2 * size])
        tokens = one if tokens is None else tokens + one
        cots = two if cots is None else cots + two
    at = lax.broadcasted_iota(jnp.int32, (SLOT, 1), 0)
    slot_row = lax.broadcasted_iota(jnp.int32, (SLOT, PROMPTS), 0)
    which = lax.broadcasted_iota(jnp.int32, (SLOT, PROMPTS), 1)
    prompted = dot((slot_row == which + 1).astype(BF16), prom[...])
    inputs = jnp.where((at >= 1) & (at <= PROMPTS), prompted, tokens)
    hat, _ = stats(inputs)
    x_out[...] = inputs.astype(BF16)
    n_out[...] = (hat * norms[0:1] + norms[1:2]).astype(BF16)
    cot_out[...] = cots.astype(BF16)


def prep(place, own, other, halo, prom, norms, slots):
    count = own.shape[0] // 2 - 8
    wide = own.shape[1]
    rows = slots * SLOT
    tile = pl.BlockSpec((SLOT, wide), lambda t: (t, 0))
    array = jax.ShapeDtypeStruct((rows, wide), BF16)
    return pl.pallas_call(
        prep_kernel,
        grid=(slots,),
        in_specs=[SMEM] + [whole(v.shape) for v in (own, other, halo, prom, norms)],
        out_specs=[tile, tile, tile, whole((1, count)), whole((1, HALO))],
        out_shape=[
            array,
            array,
            array,
            jax.ShapeDtypeStruct((1, count), jnp.int32),
            jax.ShapeDtypeStruct((1, HALO), jnp.int32),
        ],
        scratch_shapes=[pltpu.VMEM((1, count), jnp.int32)],
        compiler_params=params(),
        cost_estimate=cost(8),
        name="prep",
    )(place, own, other, halo, prom, norms)


def reverse_bits(index, size):
    return sum(((index >> i) & 1) * (size >> (i + 1)) for i in range(size.bit_length() - 1))


def weight_pieces(place, refs):
    if len(refs) == 1:
        for group in range(2):
            yield refs[0].at[group], group, 0, refs[0].shape[1]
        return
    a_zero, a_one, b_zero, b_one = refs
    deep, half = a_zero.shape[1], a_zero.shape[2]
    for dx in range(2):
        col = place[1] if dx == 0 else 1 - place[1]
        for dy in range(2):
            for k in range(deep):
                row = place[0] ^ reverse_bits(k, deep)
                for part in range(2):
                    ref = ((a_zero, a_one)[dx].at[dy, k], (b_zero, b_one)[dy].at[dx, k])[part]
                    first = ((row * 2 + col) * 2 + part) * half
                    yield ref, dy, pl.multiple_of(first, 16), half


def piece_count(held):
    return 2 if len(held) == 1 else 8 * held[0].shape[1]


def weight_copies(place, held, weight, sem):
    return [
        pltpu.make_async_copy(ref, weight.at[group, pl.ds(first, size)], sem.at[i])
        for i, (ref, group, first, size) in enumerate(weight_pieces(place, held))
    ]


def load_weight(copies):
    for copy in copies:
        copy.start()
    for copy in copies:
        copy.wait()


def attend_kernel(held_count, place, normed, *refs):
    held = refs[:held_count]
    qkv_out, prob_out, att_out, part_out, weight, sem = refs[held_count:]
    copies = weight_copies(place, held, weight, sem)

    @pl.when(pl.program_id(0) == 0)
    def _():
        load_weight(copies)

    third = weight.shape[2] // 4
    live = lax.broadcasted_iota(jnp.int32, (TAIL, 1), 0) < IMG - (CORE - TAIL)
    groups, heads = weight.shape[0], third // HEAD
    pairs = [(group, head) for group in range(groups) for head in range(heads)]
    for group in range(groups):
        qkv_out[group] = dot(normed[...], weight[group, :, : 3 * third]).astype(BF16)

    def part_of(which, group, head):
        at = which * third + head * HEAD
        return qkv_out[group, :CORE, at : at + HEAD]

    scores = [dot(part_of(1, *pair), part_of(0, *pair) * 0.125, NT) for pair in pairs]
    for (group, head), score in zip(pairs, scores):
        score = jnp.concatenate(
            [score[: CORE - TAIL], jnp.where(live, score[CORE - TAIL :], -1e30)]
        )
        exp_scores = jnp.exp(score - jnp.max(score, axis=0, keepdims=True))
        shrink = 1.0 / jnp.sum(exp_scores, axis=0, keepdims=True)
        prob_out[0, group, head] = (exp_scores * shrink).astype(BF16)
    mixed = [dot(part_of(2, *pair), prob_out[(0, *pair)], TN) for pair in pairs]
    total = None
    for group in range(groups):
        mix = jnp.concatenate(mixed[group * heads : (group + 1) * heads]).T.astype(BF16)
        att_out[group, : CORE - TAIL] = mix[: CORE - TAIL]
        att_out[group, CORE - TAIL : CORE] = jnp.where(
            live, mix[CORE - TAIL :], qkv_out[group, CORE - TAIL : CORE, 2 * third :]
        )
        att_out[group, CORE:] = qkv_out[group, CORE:, 2 * third :]
        part = dot(att_out[group], weight[group, :, 3 * third :], NT)
        total = part if total is None else total + part
    part_out[...] = total.astype(BF16)


def attend(place, normed, held, slots):
    rows, deep = normed.shape
    groups, wide = 2, held[0].shape[-1]
    third = wide // 4
    heads = third // HEAD
    return pl.pallas_call(
        functools.partial(attend_kernel, len(held)),
        grid=(slots,),
        in_specs=[SMEM, pl.BlockSpec((SLOT, deep), lambda t: (t, 0))] + [ANY] * len(held),
        out_specs=[
            pl.BlockSpec((groups, SLOT, 3 * third), lambda t: (0, t, 0)),
            pl.BlockSpec((1, groups, heads, CORE, CORE), lambda t: (t, 0, 0, 0, 0)),
            pl.BlockSpec((groups, SLOT, third), lambda t: (0, t, 0)),
            pl.BlockSpec((SLOT, deep), lambda t: (t, 0)),
        ],
        out_shape=[
            jax.ShapeDtypeStruct((groups, rows, 3 * third), BF16),
            jax.ShapeDtypeStruct((slots, groups, heads, CORE, CORE), BF16),
            jax.ShapeDtypeStruct((groups, rows, third), BF16),
            jax.ShapeDtypeStruct((rows, deep), BF16),
        ],
        scratch_shapes=[
            pltpu.VMEM((groups, deep, wide), BF16),
            pltpu.SemaphoreType.DMA((piece_count(held),)),
        ],
        compiler_params=params(),
        cost_estimate=cost(13),
        name="attend",
    )(place, normed, *held)


def mlp_kernel(more, count, *refs):
    parts, refs = refs[:count], refs[count:]
    if more:
        (normed, cot, bias, o_acc, g_acc, *refs) = refs
    else:
        (x_in, one, two, norms, cot, bias, middle_out, normed, *refs) = refs
    (o_out, g_out), grads, refs = refs[:2], refs[2 : 2 + count], refs[2 + count :]
    (bias_out, weight, act, grad, result, in_sem, out_sem) = refs
    step = pl.program_id(0)
    _, pieces, span, wide = weight.shape
    hidden = pieces * span
    cut = 384
    spots = []
    for ref in parts:
        spots.append(sum(size for _, size in spots))
        spots[-1] = (spots[-1], ref.shape[0])
    loads = [
        pltpu.make_async_copy(
            parts[i].at[:, kind], weight.at[kind, pl.ds(first, size)], in_sem.at[2 * i + kind]
        )
        for i, (first, size) in enumerate(spots)
        for kind in range(2)
    ]
    stores = [
        pltpu.make_async_copy(
            result.at[kind, pl.ds(first, size)], grads[i].at[:, kind], out_sem.at[2 * i + kind]
        )
        for i, (first, size) in enumerate(spots)
        for kind in range(2)
    ]

    @pl.when(step == 0)
    def _():
        for copy in loads:
            copy.start()
        bias_out[...] = jnp.zeros_like(bias_out)
        for copy in loads:
            copy.wait()

    rows = pl.ds(pl.multiple_of(step * SLOT, 16), SLOT)
    if not more:
        middle = x_in[...].astype(F32) + (one[...].astype(F32) + two[...].astype(F32))
        middle_out[...] = middle
        hat, _ = stats(middle)
        normed[rows] = (hat * norms[2:3] + norms[3:4]).astype(BF16)
    tile_n = normed[rows]
    tile_c = cot[rows]
    for at in range(0, hidden, cut):
        up = weight[0, at // span : (at + cut) // span].reshape(cut, wide)
        down = weight[1, at // span : (at + cut) // span].reshape(cut, wide)
        pre = dot(tile_n, up, NT) + bias[:, at : at + cut]
        cdf = 0.5 * (1.0 + lax.erf(pre * 0.7071067811865476))
        pdf = jnp.exp(-0.5 * pre * pre) * 0.3989422804014327
        act[rows, at : at + cut] = (pre * cdf).astype(BF16)
        grad_low = (dot(tile_c, down, NT) * (cdf + pre * pdf)).astype(BF16)
        grad[rows, at : at + cut] = grad_low
        bias_out[:, at : at + cut] += jnp.sum(grad_low.astype(F32), axis=0, keepdims=True)
    o_sum = dot(act[rows], weight[1].reshape(hidden, wide))
    g_sum = dot(grad[rows], weight[0].reshape(hidden, wide))
    if more:
        o_sum = o_sum + o_acc[...].astype(F32)
        g_sum = g_sum + g_acc[...].astype(F32)
    o_out[...] = o_sum.astype(o_out.dtype)
    g_out[...] = g_sum.astype(g_out.dtype)

    @pl.when(step == pl.num_programs(0) - 1)
    def _():
        sent = 0
        for at in range(0, hidden, cut):
            own = pl.ds(at // span, cut // span)
            shape = (cut // span, span, wide)
            result[0, own] = dot(grad[:, at : at + cut], normed[...], TN).astype(BF16).reshape(shape)
            result[1, own] = dot(act[:, at : at + cut], cot[...], TN).astype(BF16).reshape(shape)
            done = sum((first + size) * span <= at + cut for first, size in spots)
            for copy in stores[2 * sent : 2 * done]:
                copy.start()
            sent = done
        for copy in stores:
            copy.wait()


def mlp(parts, cot, bias, slots, start=None, sums=None):
    rows, wide = cot.shape
    hidden = bias.shape[1]
    span = parts[0].shape[2]
    more = sums is not None
    tile = pl.BlockSpec((SLOT, wide), lambda t: (t, 0))
    wide_f32, wide_bf16 = (jax.ShapeDtypeStruct((rows, wide), kind) for kind in (F32, BF16))
    full = whole(cot.shape)
    count = len(parts)
    if more:
        operands = (*parts, start, cot, bias, *sums)
        specs = [ANY] * count + [full, full, whole(bias.shape), tile, tile]
    else:
        x_in, one, two, norms = start
        operands = (*parts, x_in, one, two, norms, cot, bias)
        specs = [ANY] * count + [tile, tile, tile, whole(norms.shape), full, whole(bias.shape)]
    return pl.pallas_call(
        functools.partial(mlp_kernel, more, count),
        grid=(slots,),
        in_specs=specs,
        out_specs=([] if more else [tile, full])
        + [tile, tile]
        + [ANY] * count
        + [whole(bias.shape)],
        out_shape=([] if more else [wide_f32, wide_bf16])
        + [wide_bf16, wide_bf16]
        + [jax.ShapeDtypeStruct(v.shape, BF16) for v in parts]
        + [jax.ShapeDtypeStruct(bias.shape, F32)],
        scratch_shapes=[
            pltpu.VMEM((2, hidden // span, span, wide), BF16),
            pltpu.VMEM((rows, hidden), BF16),
            pltpu.VMEM((rows, hidden), BF16),
            pltpu.VMEM((2, hidden // span, span, wide), BF16),
            pltpu.SemaphoreType.DMA((2 * count,)),
            pltpu.SemaphoreType.DMA((2 * count,)),
        ],
        compiler_params=params(),
        cost_estimate=cost(17),
        name="mlp",
    )(*operands)


def add_kernel(a_zero, a_got, b_zero, b_got, a_out, b_out):
    for zero, got, out in ((a_zero, a_got, a_out), (b_zero, b_got, b_out)):
        out[...] = (zero[0].astype(F32) + got[0].astype(F32)).astype(BF16)


def add_second(a_zero, a_got, b_zero, b_got):
    shape = a_zero.shape[1:]
    block = pl.BlockSpec((1, 1) + shape[1:], lambda k: (1, k) + (0,) * (len(shape) - 1))
    out = pl.BlockSpec((1,) + shape[1:], lambda k: (k,) + (0,) * (len(shape) - 1))
    return pl.pallas_call(
        add_kernel,
        grid=(shape[0],),
        in_specs=[block] * 4,
        out_specs=[out] * 2,
        out_shape=[jax.ShapeDtypeStruct(shape, BF16)] * 2,
        compiler_params=params(),
        cost_estimate=cost(3.4),
        name="add_second",
    )(a_zero, a_got, b_zero, b_got)


def split_kernel(count, *refs):
    total = refs[0][...].astype(F32)
    for ref in refs[1:count]:
        total = total + ref[...].astype(F32)
    low = total.astype(BF16)
    half = low.shape[0] // 2
    refs[count][...] = low[:half]
    refs[count + 1][...] = low[half:]


def sum_split(values):
    shape = values[0].shape
    half = (shape[0] // 2,) + shape[1:]
    return pl.pallas_call(
        functools.partial(split_kernel, len(values)),
        grid=(1,),
        in_specs=[whole(shape)] * len(values),
        out_specs=[whole(half)] * 2,
        out_shape=[jax.ShapeDtypeStruct(half, BF16)] * 2,
        compiler_params=params(),
        cost_estimate=cost(2),
        name="sum_split",
    )(*values)


def fold_kernel(a_zero, a_got, a_last, b_zero, b_got, b_last, keep, send):
    half = keep.shape[0]
    for part, (zero, got, last_got) in enumerate(((a_zero, a_got, a_last), (b_zero, b_got, b_last))):
        total = zero[0].astype(F32) + got[0].astype(F32) + last_got[...].astype(F32)
        total = total.astype(BF16)
        keep[:, part] = total[:half]
        send[:, part] = total[half:]


def fold_first(a_zero, a_got, a_last, b_zero, b_got, b_last):
    shape = a_last.shape
    first = whole((1,) + shape)
    out = (shape[0] // 2, 2) + shape[1:]
    return pl.pallas_call(
        fold_kernel,
        grid=(1,),
        in_specs=[first, first, whole(shape)] * 2,
        out_specs=[whole(out)] * 2,
        out_shape=[jax.ShapeDtypeStruct(out, BF16)] * 2,
        compiler_params=params(),
        cost_estimate=cost(3),
        name="fold_first",
    )(a_zero, a_got, a_last, b_zero, b_got, b_last)


def finish_kernel(middle, one, two, dest_own, dest_halo, own_out, halo_out, values):
    step = pl.program_id(0)
    value = middle[...] + (one[...].astype(F32) + two[...].astype(F32))
    values[pl.ds(pl.multiple_of(step * SLOT, 16), SLOT)] = value.astype(BF16)
    spread_rows(values, dest_own, dest_halo, own_out, halo_out)


def spread_rows(values, dest_own, dest_halo, own_out, halo_out):
    @pl.when(pl.program_id(0) == pl.num_programs(0) - 1)
    def _():
        for dest, out in ((dest_own, own_out), (dest_halo, halo_out)):
            shape = (dest.shape[1], values.shape[0])
            at = lax.broadcasted_iota(jnp.int32, shape, 1)
            pick = (at == dest[...].reshape(dest.shape[1], 1)).astype(BF16)
            out[...] = dot(pick, values[...]).astype(out.dtype)


def finish(middle, one, two, dest_own, dest_halo, slots):
    rows, wide = middle.shape
    count = dest_own.shape[1]
    tile = pl.BlockSpec((SLOT, wide), lambda t: (t, 0))
    return pl.pallas_call(
        finish_kernel,
        grid=(slots,),
        in_specs=[tile, tile, tile, whole(dest_own.shape), whole(dest_halo.shape)],
        out_specs=[whole((count, wide)), whole((HALO, wide))],
        out_shape=[
            jax.ShapeDtypeStruct((count, wide), BF16),
            jax.ShapeDtypeStruct((HALO, wide), BF16),
        ],
        scratch_shapes=[pltpu.VMEM((rows, wide), BF16)],
        compiler_params=params(),
        cost_estimate=cost(5),
        name="finish",
    )(middle, one, two, dest_own, dest_halo)


def back_kernel(held_count, place, middle, one, two, cot, norms, qkv, prob, *refs):
    held = refs[:held_count]
    gm_out, gp_out, dq_out, part_out, sums_out, weight, scored, sem = refs[held_count:]
    step = pl.program_id(0)
    third = weight.shape[2] // 4
    copies = weight_copies(place, held, weight, sem)

    @pl.when(step == 0)
    def _():
        load_weight(copies)
        sums_out[...] = jnp.zeros_like(sums_out)

    grad = one[...].astype(F32) + two[...].astype(F32)
    hat, inverse = stats(middle[...])
    sums_out[0:1] += jnp.sum(grad * hat, axis=0, keepdims=True)
    sums_out[1:2] += jnp.sum(grad, axis=0, keepdims=True)
    grad_middle = cot[...].astype(F32) + norm_back(grad, hat, inverse, norms[2:3])
    gm_out[...] = grad_middle
    grad_proj = grad_middle.astype(BF16)
    gp_out[...] = grad_proj
    live = lax.broadcasted_iota(jnp.int32, (TAIL, 1), 0) < IMG - (CORE - TAIL)
    groups, heads = weight.shape[0], third // HEAD
    pairs = [(group, head) for group in range(groups) for head in range(heads)]

    def part_of(which, group, head):
        at = which * third + head * HEAD
        return qkv[group, :CORE, at : at + HEAD]

    grad_atts, grad_cores = [], []
    for group in range(groups):
        grad_att = dot(grad_proj, weight[group, :, 3 * third :]).astype(BF16)
        tail = grad_att[CORE - TAIL : CORE]
        tail = jnp.where(live, tail, jnp.zeros_like(tail))
        grad_atts.append(grad_att)
        grad_cores.append(jnp.concatenate([grad_att[: CORE - TAIL], tail]))
    grad_heads = [grad_cores[group][:, head * HEAD : (head + 1) * HEAD] for group, head in pairs]
    grad_probs = [dot(part_of(2, *pair), grad, NT) for pair, grad in zip(pairs, grad_heads)]
    grads_v = [dot(prob[(0, *pair)], grad) for pair, grad in zip(pairs, grad_heads)]
    for (group, head), grad_prob in zip(pairs, grad_probs):
        probs = prob[0, group, head].astype(F32)
        center = jnp.sum(probs * grad_prob, axis=0, keepdims=True)
        scored[group * heads + head] = (probs * (grad_prob - center)).astype(BF16)
    grads_q, grads_k = [], []
    for group, head in pairs:
        at = group * heads + head
        grads_q.append(dot(part_of(1, group, head) * 0.125, scored[at], TN))
        grads_k.append(dot(scored[at], part_of(0, group, head) * 0.125))
    total = None
    for group in range(groups):
        own = slice(group * heads, (group + 1) * heads)
        grad_q = jnp.concatenate(grads_q[own]).T.astype(BF16)
        grad_k = jnp.concatenate(grads_k[own], axis=1).astype(BF16)
        grad_v = jnp.concatenate(grads_v[own], axis=1).astype(BF16)
        tail = grad_atts[group][CORE - TAIL : CORE]
        dq_out[group, :CORE, : 3 * third] = jnp.concatenate([grad_q, grad_k, grad_v], axis=1)
        dq_out[group, CORE - TAIL : CORE, 2 * third :] = jnp.where(live, grad_v[CORE - TAIL :], tail)
        dq_out[group, CORE:, : 2 * third] = jnp.zeros((SLOT - CORE, 2 * third), BF16)
        dq_out[group, CORE:, 2 * third :] = grad_atts[group][CORE:]
        part = dot(dq_out[group], weight[group, :, : 3 * third], NT)
        total = part if total is None else total + part
    part_out[...] = total.astype(BF16)


def back(place, middle, one, two, cot, norms, held, qkv, prob, slots):
    rows, wide = middle.shape
    groups, third = qkv.shape[0], qkv.shape[2] // 3
    tile = pl.BlockSpec((SLOT, wide), lambda t: (t, 0))
    tile_q = pl.BlockSpec((groups, SLOT, 3 * third), lambda t: (0, t, 0))
    return pl.pallas_call(
        functools.partial(back_kernel, len(held)),
        grid=(slots,),
        in_specs=[
            SMEM,
            tile,
            tile,
            tile,
            tile,
            whole(norms.shape),
            tile_q,
            pl.BlockSpec((1,) + prob.shape[1:], lambda t: (t, 0, 0, 0, 0)),
        ]
        + [ANY] * len(held),
        out_specs=[tile, tile, tile_q, tile, whole((8, wide))],
        out_shape=[
            jax.ShapeDtypeStruct((rows, wide), F32),
            jax.ShapeDtypeStruct((rows, wide), BF16),
            jax.ShapeDtypeStruct(qkv.shape, BF16),
            jax.ShapeDtypeStruct((rows, wide), BF16),
            jax.ShapeDtypeStruct((8, wide), F32),
        ],
        scratch_shapes=[
            pltpu.VMEM((groups, wide, 4 * third), BF16),
            pltpu.VMEM((groups * (third // HEAD), CORE, CORE), BF16),
            pltpu.SemaphoreType.DMA((piece_count(held),)),
        ],
        compiler_params=params(),
        cost_estimate=cost(19),
        name="back",
    )(place, middle, one, two, cot, norms, qkv, prob, *held)


def weight_kernel(held_count, place, normed, grad_proj, grad_qkv, att, *refs):
    held = refs[:held_count]
    result, sem = refs[held_count:]
    third = att.shape[2]
    cut = normed.shape[1]
    at = pl.ds(pl.multiple_of(pl.program_id(0) * cut, cut), cut)
    for group in range(2):
        result[group, at, : 3 * third] = dot(normed[...], grad_qkv[group], TN).astype(BF16)
        result[group, at, 3 * third :] = dot(grad_proj[...], att[group], TN).astype(BF16)

    @pl.when(pl.program_id(0) == pl.num_programs(0) - 1)
    def _():
        copies = [
            pltpu.make_async_copy(result.at[group, pl.ds(first, size)], ref, sem.at[i])
            for i, (ref, group, first, size) in enumerate(weight_pieces(place, held))
        ]
        for copy in copies:
            copy.start()
        for copy in copies:
            copy.wait()


def weight_grads(place, normed, grad_proj, grad_qkv, att, held):
    rows, wide = normed.shape
    groups, _, third = att.shape
    cut = 256
    tall = pl.BlockSpec((rows, cut), lambda d: (0, d))
    return pl.pallas_call(
        functools.partial(weight_kernel, len(held)),
        grid=(wide // cut,),
        in_specs=[SMEM, tall, tall, whole(grad_qkv.shape), whole(att.shape)],
        out_specs=[ANY] * len(held),
        out_shape=[jax.ShapeDtypeStruct(v.shape, BF16) for v in held],
        scratch_shapes=[
            pltpu.VMEM((groups, wide, 4 * third), BF16),
            pltpu.SemaphoreType.DMA((piece_count(held),)),
        ],
        compiler_params=params(),
        cost_estimate=cost(9),
        name="weight_grads",
    )(place, normed, grad_proj, grad_qkv, att)


def last_kernel(
    x_in, gm, one, two, norms, dest_own, dest_halo, own_out, halo_out, prompt_out, sums_out, values
):
    step = pl.program_id(0)

    @pl.when(step == 0)
    def _():
        sums_out[...] = jnp.zeros_like(sums_out)
        prompt_out[...] = jnp.zeros_like(prompt_out)

    grad = one[...].astype(F32) + two[...].astype(F32)
    hat, inverse = stats(x_in[...].astype(F32))
    sums_out[0:1] += jnp.sum(grad * hat, axis=0, keepdims=True)
    sums_out[1:2] += jnp.sum(grad, axis=0, keepdims=True)
    grad_in = gm[...] + norm_back(grad, hat, inverse, norms[0:1])
    prompt_out[...] += grad_in[: prompt_out.shape[0]]
    at = lax.broadcasted_iota(jnp.int32, (SLOT, 1), 0)
    value = jnp.where((at >= 1) & (at <= PROMPTS), 0.0, grad_in).astype(BF16)
    values[pl.ds(pl.multiple_of(step * SLOT, 16), SLOT)] = value
    spread_rows(values, dest_own, dest_halo, own_out, halo_out)


def last(x_in, gm, one, two, norms, dest_own, dest_halo, slots):
    rows, wide = x_in.shape
    count = dest_own.shape[1]
    tile = pl.BlockSpec((SLOT, wide), lambda t: (t, 0))
    return pl.pallas_call(
        last_kernel,
        grid=(slots,),
        in_specs=[tile] * 4 + [whole(norms.shape), whole(dest_own.shape), whole(dest_halo.shape)],
        out_specs=[whole((count, wide)), whole((HALO, wide)), whole((56, wide)), whole((8, wide))],
        out_shape=[
            jax.ShapeDtypeStruct((count, wide), F32),
            jax.ShapeDtypeStruct((HALO, wide), BF16),
            jax.ShapeDtypeStruct((56, wide), F32),
            jax.ShapeDtypeStruct((8, wide), F32),
        ],
        scratch_shapes=[pltpu.VMEM((rows, wide), BF16)],
        compiler_params=params(),
        cost_estimate=cost(7),
        name="last",
    )(x_in, gm, one, two, norms, dest_own, dest_halo)


class Grid:
    def __init__(self, rows, heads):
        self.deep = rows // 2
        self.size = rows * heads
        row = lax.axis_index("rows")
        col = lax.axis_index("heads")
        self.z = row // 2
        self.x = row % 2
        self.y = col // 2
        self.c = col % 2

    def send(self, value, move):
        pairs = []
        for i in range(self.size):
            z, x, y, c = move(i // 8, (i // 4) % 2, (i // 2) % 2, i % 2)
            pairs.append((i, ((z * 2 + x) * 2 + y) * 2 + c))
        return lax.ppermute(value, AXES, pairs)

    def by_x(self, value):
        return self.send(value, lambda z, x, y, c: (z, 1 - x, y, c))

    def by_y(self, value):
        return self.send(value, lambda z, x, y, c: (z, x, 1 - y, c))

    def by_core(self, value):
        return self.send(value, lambda z, x, y, c: (z, x, y, 1 - c))

    def by_z(self, value, bit):
        return self.send(value, lambda z, x, y, c: (z ^ bit, x, y, c))

    def gather_z(self, value, axis, *between):
        first = None
        bit = self.deep // 2
        while bit:
            got = self.by_z(value, bit)
            if first is None:
                got = first = after(got, *between)
            value = jnp.concatenate([value, got], axis=axis)
            bit //= 2
        return value, first

    def spread(self, first, second):
        a_next, b_next = tie(self.by_y(first), self.by_x(second))
        a_zero = jnp.stack([first, a_next])
        b_zero = jnp.stack([second, b_next])
        return a_zero, b_zero

    def spread_more(self, a_zero, b_zero):
        return self.by_x(a_zero), self.by_y(b_zero)

    def fold_z(self, keep, got):
        bit, first = 2, got
        while bit < self.deep:
            keep, send = sum_split([keep, got])
            got = self.by_z(send, bit)
            first = send if bit == 2 else first
            bit *= 2
        return keep, got, first

    def to_absolute(self, blocks, z_axis, x_axis):
        return self.turn(jnp.where(self.x == 0, blocks, jnp.flip(blocks, axis=x_axis)), z_axis, False)

    def to_relative(self, blocks, z_axis, x_axis):
        return self.turn(jnp.where(self.x == 0, blocks, jnp.flip(blocks, axis=x_axis)), z_axis, True)

    def turn(self, blocks, z_axis, back):
        shape = blocks.shape
        bits = self.deep.bit_length() - 1
        blocks = blocks.reshape(shape[:z_axis] + (2,) * bits + shape[z_axis + 1 :])
        order = list(range(blocks.ndim))
        order[z_axis : z_axis + bits] = order[z_axis : z_axis + bits][::-1]
        if back:
            blocks = blocks.transpose(order)
        for i in range(bits):
            flipped = jnp.flip(blocks, axis=z_axis + i)
            blocks = jnp.where((self.z >> i) & 1 == 0, blocks, flipped)
        if not back:
            blocks = blocks.transpose(order)
        return blocks.reshape(shape)


def exchange(value, send):
    low = value.astype(BF16)
    return low.astype(F32) + send(low).astype(F32)


def tie(*values):
    return lax.optimization_barrier(values)


def after(value, *earlier):
    return lax.optimization_barrier((value, *earlier))[0]


def local(
    rows,
    heads,
    tokens,
    segment,
    live_token,
    prompt_slot,
    prompts,
    attn_gain,
    attn_shift,
    qkv_weight,
    out_weight,
    mlp_gain,
    mlp_shift,
    up_weight,
    up_bias,
    down_weight,
    cotangent,
):
    grid = Grid(rows, heads)
    deep = grid.deep
    count, wide = tokens.shape
    slots = IMGS_ROW * 2 * count // ROW
    place = jnp.stack([grid.z, grid.x, grid.y, grid.c]).astype(jnp.int32)

    def row_of(vec):
        return vec.astype(F32).reshape(1, -1)

    norms = jnp.stack([attn_gain, attn_shift, mlp_gain, mlp_shift]).astype(F32)

    depth = qkv_weight.shape[0]
    third = qkv_weight.shape[2]
    shard = jnp.concatenate(
        [qkv_weight.reshape(depth, 3 * third), out_weight.swapaxes(0, 1)], axis=1
    ).reshape(2, 1, depth // 2, 4 * third)

    hidden = up_weight.shape[1]
    span = hidden // 2
    halves = jnp.stack(
        [up_weight.swapaxes(0, 1).reshape(2, span, wide), down_weight.reshape(2, span, wide)],
        axis=1,
    )
    bias, first = grid.gather_z(up_bias.reshape(1, hidden), 0)
    shard = after(shard, first)
    got, first = grid.gather_z(shard, 1, bias)
    bias = jnp.stack([bias, grid.by_x(bias)])
    bias = jnp.stack([bias, grid.by_y(bias)])

    code = ((segment % IMGS_ROW) * 2 + live_token).astype(BF16)
    marks = jnp.pad(code[None], ((0, 15), (0, wide - count)))
    own = after(jnp.concatenate([tokens, cotangent, marks]), shard)
    other = grid.by_core(own)
    mine = grid.c == 1 - grid.y
    first_row = jnp.where(grid.y == 0, count - HALO, 0)
    edge_parts = []
    for base in (0, count):
        edge_parts.append(
            jnp.where(
                mine,
                lax.dynamic_slice_in_dim(own, base + first_row, HALO),
                lax.dynamic_slice_in_dim(other, base + first_row, HALO),
            )
        )
    edge_code = jnp.where(mine, own[2 * count :], other[2 * count :])
    edge_code = jnp.where(grid.y == 0, edge_code[:, count - HALO : count], edge_code[:, :HALO])
    edge_parts.append(jnp.pad(edge_code, ((0, 0), (0, wide - HALO))))
    edge = jnp.concatenate(edge_parts)
    halo = grid.by_y(edge)

    got, bias, halo = tie(got, bias, halo)
    a_zero, b_zero = grid.spread(got[0], got[1])
    a_one, b_one = grid.spread_more(a_zero, b_zero)
    x_in, normed, cot, dest_own, dest_halo = prep(place, own, other, halo, prompts, norms, slots)

    held, _ = grid.gather_z(after(halves, first)[:, None], 1, normed)
    mlp_a, mlp_b = held[0], held[1]
    mlp_a0, mlp_b0 = grid.spread(mlp_a, mlp_b)
    mlp_a1, mlp_b1 = grid.spread_more(mlp_a0, mlp_b0)
    bias_a = jnp.stack([bias[:, 0, :, :span], bias[0, :, :, span:]])
    bias_b = jnp.stack([bias[:, 1, :, :span], bias[1, :, :, span:]])

    weights = [a_zero, a_one, b_zero, b_one]
    if (depth // 2) % 16:
        blocks = jnp.stack(
            [
                jnp.concatenate([(a_zero, a_one)[dx][dy], (b_zero, b_one)[dy][dx]], axis=1)
                for dy in range(2)
                for dx in range(2)
            ]
        ).reshape(2, 2, deep, depth, 4 * third)
        blocks = grid.to_absolute(blocks, 2, 1).swapaxes(1, 2)
        weights = [blocks.reshape(2, 2 * deep * depth, 4 * third)]
    qkv, prob, att, part = attend(place, normed, weights, slots)

    fine = span % 16 == 0

    def enter(value):
        value = value.reshape(-1, 2, span, wide)
        if fine:
            return value
        return value.swapaxes(0, 1).reshape(2, -1, 48, wide).swapaxes(0, 1)

    def leave(value):
        if fine:
            return value
        return value.swapaxes(0, 1).reshape(2, -1, span, wide).swapaxes(0, 1)

    start = (x_in, part, grid.by_core(part), norms)
    middle, normed_two, o_sum, g_sum, *grads, grad_bias_a = mlp(
        [enter(mlp_a0), enter(mlp_b0)], cot, row_of(bias_a), slots, start
    )
    grad_a0, grad_b0 = [leave(v).reshape(2, deep, 2, span, wide) for v in grads]
    o_part, g_part, *grads, grad_bias_b = mlp(
        [enter(mlp_a1), enter(mlp_b1)],
        cot,
        row_of(bias_b),
        slots,
        normed_two,
        (o_sum, g_sum),
    )
    grad_a1, grad_b1 = [leave(v).reshape(2, deep, 2, span, wide) for v in grads]
    a_got, b_got = grid.by_x(grad_a1), grid.by_y(grad_b1)
    g_other = grid.by_core(g_part)

    grad_middle, grad_proj, grad_qkv, g_one, sums_two = back(
        place, middle, g_part, g_other, cot, norms, weights, qkv, prob, slots
    )
    g_one_other = grid.by_core(g_one)
    o_other = grid.by_core(after(o_part, g_one))
    a_got, b_got, _ = tie(a_got, b_got, g_one)
    a_send, b_send = add_second(grad_a0, a_got, grad_b0, b_got)
    a_last, b_last = grid.by_y(a_send), grid.by_x(b_send)
    weight_blocks = weight_grads(
        place, after(normed, a_send), grad_proj, grad_qkv, att, weights
    )
    if len(weight_blocks) == 1:
        blocks = weight_blocks[0].reshape(2, deep, 2, depth, 4 * third).swapaxes(1, 2)
        blocks = grid.to_relative(blocks, 2, 1)
        blocks = blocks.reshape(2, 2, deep, 2, depth // 2, 4 * third)
        weight_blocks = [
            blocks[:, 0, :, 0],
            blocks[:, 1, :, 0],
            blocks[0, :, :, 1],
            blocks[1, :, :, 1],
        ]
    att_a0, att_a1, att_b0, att_b1 = weight_blocks
    att_a_got, att_b_got = grid.by_x(att_a1), grid.by_y(att_b1)
    a_last, b_last, o_other, g_one_other, _ = tie(a_last, b_last, o_other, g_one_other, att_a1)
    grad_keep, grad_send = fold_first(grad_a0, a_got, a_last, grad_b0, b_got, b_last)
    grad_got = grid.by_z(grad_send, 1)

    tok_own, tok_halo, prompt_sum, sums_one = last(
        x_in, grad_middle, g_one, after(g_one_other, grad_send), norms, dest_own, dest_halo, slots
    )
    tok_edge = grid.by_y(tok_halo)

    g_a = grad_bias_a.reshape(2, 2, deep, span)
    g_b = grad_bias_b.reshape(2, 2, deep, span)
    bias_blocks = jnp.stack(
        [jnp.stack([g_a[0], g_b[0]], axis=1), jnp.stack([g_a[1], g_b[1]], axis=0)], axis=3
    )
    bias_blocks = grid.to_absolute(bias_blocks, 2, 1)
    bias_blocks = jnp.where(grid.y == 0, bias_blocks, jnp.flip(bias_blocks, axis=0))
    small = jnp.concatenate(
        [prompt_sum, sums_one[:2], sums_two[:2], bias_blocks.reshape(-1, wide)]
    )
    small = exchange(small, grid.by_x)
    att_a_got, att_b_got, _ = tie(att_a_got, att_b_got, tok_halo)
    a_send, b_send = add_second(att_a0, att_a_got, att_b0, att_b_got)
    att_a_last, att_b_last = grid.by_y(a_send), grid.by_x(b_send)
    grad_got, small, _ = tie(grad_got, small, a_send)
    grad_keep, grad_got, grad_send = grid.fold_z(grad_keep, grad_got)
    small = exchange(small, grid.by_y)
    out_own, out_halo = finish(
        middle, o_part, after(o_other, grad_send), dest_own, dest_halo, slots
    )
    out_edge = grid.by_y(out_halo)
    att_a_last, att_b_last, small, _ = tie(att_a_last, att_b_last, small, out_halo)
    att_keep, att_send = fold_first(att_a0, att_a_got, att_a_last, att_b0, att_b_got, att_b_last)
    att_got = grid.by_z(att_send, 1)
    small = exchange(small, lambda v: grid.by_z(v, 1))
    att_got, small = tie(att_got, small)
    att_keep, att_got, _ = grid.fold_z(att_keep, att_got)
    grad_got = after(grad_got, att_keep)
    grad_shard = (grad_keep.astype(F32) + grad_got.astype(F32))[0]
    grad_up = grad_shard[:, 0].reshape(hidden, wide).swapaxes(0, 1)
    grad_down = grad_shard[:, 1].reshape(hidden, wide)
    att_shard = att_keep.astype(F32) + att_got.astype(F32)
    att_shard = att_shard.reshape(depth, 4 * third)
    grad_qkv_weight = att_shard[:, : 3 * third].reshape(depth, 3, third)
    grad_out_weight = att_shard[:, 3 * third :].swapaxes(0, 1)

    def merge(value, edge):
        edge = edge.astype(value.dtype)
        ends = jnp.where((grid.y == 0) & (grid.c == 1), edge, 0)
        begins = jnp.where((grid.y == 1) & (grid.c == 0), edge, 0)
        value = value.at[count - HALO :].add(ends)
        return value.at[:HALO].add(begins)

    stride = 2
    while stride < deep:
        small = exchange(small, lambda v, stride=stride: grid.by_z(v, stride))
        stride *= 2
    bias_all = small[60:].reshape(2, 2, deep, hidden)
    grad_bias = lax.dynamic_slice(
        bias_all, (grid.y, grid.x, grid.z, jnp.int32(0)), (1, 1, 1, hidden)
    ).reshape(hidden)
    return (
        merge(out_own, out_edge),
        merge(tok_own, tok_edge),
        small[1 : 1 + PROMPTS],
        small[56],
        small[57],
        grad_qkv_weight,
        grad_out_weight,
        small[58],
        small[59],
        grad_up,
        grad_bias,
        grad_down,
    )


def solution(mesh):
    both = P(AXES)
    lead = P(AXES, None)
    return jax.shard_map(
        functools.partial(local, mesh.shape["rows"], mesh.shape["heads"]),
        mesh=mesh,
        in_specs=(
            lead,
            both,
            both,
            both,
            P(),
            P(),
            P(),
            P("rows", None, "heads"),
            P("heads", "rows"),
            P(),
            P(),
            P(None, AXES),
            both,
            lead,
            lead,
        ),
        out_specs=(
            lead,
            lead,
            P(),
            P(),
            P(),
            P("rows", None, "heads"),
            P("heads", "rows"),
            P(),
            P(),
            P(None, AXES),
            both,
            lead,
        ),
        check_vma=False,
    )
```

```python
import functools

import jax
import jax.numpy as jnp
from jax import lax
from jax.experimental import pallas as pl
from jax.experimental.pallas import tpu as pltpu
from jax.sharding import PartitionSpec as P

HEAD = 64
ROW = 2048
IMG = 247
IMGS_ROW = 8
PROMPTS = 50
SLOT = 272
CORE = 256
TAIL = 16
HALO = 48
EPSILON = 1e-06
AXES = ("rows", "heads")
F32 = jnp.float32
BF16 = jnp.bfloat16
VMEM_LIMIT = 56 * 1024 * 1024

NN = (((1,), (0,)), ((), ()))
NT = (((1,), (1,)), ((), ()))
TN = (((0,), (0,)), ((), ()))


def dot(left, right, dims=NN):
    return lax.dot_general(left, right, dims, preferred_element_type=F32)


def whole(shape):
    return pl.BlockSpec(shape, lambda *_: (0,) * len(shape))


def params(**more):
    return pltpu.CompilerParams(vmem_limit_bytes=VMEM_LIMIT, **more)


SCALE = 0.15


def cost(time):
    return pl.CostEstimate(flops=int(time * SCALE * 1.15e9), bytes_accessed=1, transcendentals=0)


SMEM = pl.BlockSpec(memory_space=pltpu.SMEM)
ANY = pl.BlockSpec(memory_space=pl.ANY)


def stats(values):
    center = values - jnp.mean(values, axis=-1, keepdims=True)
    inverse = lax.rsqrt(jnp.mean(center * center, axis=-1, keepdims=True) + EPSILON)
    return center * inverse, inverse


def norm_back(grad, hat, inverse, gain):
    inner = grad * gain
    first = jnp.mean(inner, axis=-1, keepdims=True)
    second = jnp.mean(inner * hat, axis=-1, keepdims=True)
    return inverse * (inner - first - hat * second)


def prep_kernel(
    place, own, other, halo, prom, norms, x_out, n_out, cot_out, dest_own, dest_halo, d_oth
):
    step = pl.program_id(0)
    count = d_oth.shape[1]
    slots = pl.num_programs(0)
    y_at, c_at = place[2], place[3]

    @pl.when(step == 0)
    def _():
        big = 1 << 20
        spans = (
            (own[2 * count : 2 * count + 16, :count], 2 * count * y_at + count * c_at, True),
            (other[2 * count : 2 * count + 16, :count], 2 * count * y_at + count * (1 - c_at), True),
            (halo[2 * HALO : 2 * HALO + 16, :HALO], 2 * count - HALO * y_at, False),
        )
        parts = []
        for marks, base, home in spans:
            code = marks.astype(F32)[0:1].astype(jnp.int32)
            live = (code & 1) > 0
            slot = (code >> 1) - slots * y_at
            pos = base + lax.broadcasted_iota(jnp.int32, code.shape, 1)
            parts.append((live, slot, pos, home))
        starts = []
        for k in range(slots):
            low = None
            for live, slot, pos, home in parts:
                here = jnp.min(jnp.where(live & (slot == k), pos, big), axis=1, keepdims=True)
                low = here if low is None else jnp.minimum(low, here)
            starts.append(low)
        pads_own, pads_other = [
            jnp.sum(jnp.where(part[0], 0, 1), axis=1, keepdims=True) for part in parts[:2]
        ]
        befores = (c_at * pads_other, (1 - c_at) * pads_own, None)
        results = []
        for (live, slot, pos, home), before in zip(parts, befores):
            dest = jnp.full(pos.shape, -1, jnp.int32)
            for k in range(slots):
                dest = jnp.where(live & (slot == k), pos - starts[k] + k * SLOT, dest)
            if home:
                pads = jnp.where(live, 0.0, 1.0).astype(BF16)
                size = pads.shape[1]
                earlier = (
                    lax.broadcasted_iota(jnp.int32, (size, size), 0)
                    < lax.broadcasted_iota(jnp.int32, (size, size), 1)
                )
                wide = jnp.broadcast_to(pads, (16, size))
                rank = dot(wide, earlier.astype(BF16))[0:1].astype(jnp.int32) + before
                spare = (rank & (slots - 1)) * SLOT + IMG + (rank >> (slots.bit_length() - 1))
                dest = jnp.where(live, dest, spare)
            results.append(dest)
        dest_own[...] = results[0]
        d_oth[...] = results[1]
        dest_halo[...] = results[2]

    rows = step * SLOT
    tokens = cots = None
    for dest, ref, size in (
        (dest_own, own, count),
        (d_oth, other, count),
        (dest_halo, halo, HALO),
    ):
        at = rows + lax.broadcasted_iota(jnp.int32, (SLOT, size), 0)
        pick = (at == dest[...]).astype(BF16)
        one = dot(pick, ref[0:size])
        two = dot(pick, ref[size : 2 * size])
        tokens = one if tokens is None else tokens + one
        cots = two if cots is None else cots + two
    at = lax.broadcasted_iota(jnp.int32, (SLOT, 1), 0)
    slot_row = lax.broadcasted_iota(jnp.int32, (SLOT, PROMPTS), 0)
    which = lax.broadcasted_iota(jnp.int32, (SLOT, PROMPTS), 1)
    prompted = dot((slot_row == which + 1).astype(BF16), prom[...])
    inputs = jnp.where((at >= 1) & (at <= PROMPTS), prompted, tokens)
    hat, _ = stats(inputs)
    x_out[...] = inputs.astype(BF16)
    n_out[...] = (hat * norms[0:1] + norms[1:2]).astype(BF16)
    cot_out[...] = cots.astype(BF16)


def prep(place, own, other, halo, prom, norms, slots):
    count = own.shape[0] // 2 - 8
    wide = own.shape[1]
    rows = slots * SLOT
    tile = pl.BlockSpec((SLOT, wide), lambda t: (t, 0))
    array = jax.ShapeDtypeStruct((rows, wide), BF16)
    return pl.pallas_call(
        prep_kernel,
        grid=(slots,),
        in_specs=[SMEM] + [whole(v.shape) for v in (own, other, halo, prom, norms)],
        out_specs=[tile, tile, tile, whole((1, count)), whole((1, HALO))],
        out_shape=[
            array,
            array,
            array,
            jax.ShapeDtypeStruct((1, count), jnp.int32),
            jax.ShapeDtypeStruct((1, HALO), jnp.int32),
        ],
        scratch_shapes=[pltpu.VMEM((1, count), jnp.int32)],
        compiler_params=params(),
        cost_estimate=cost(8),
        name="prep",
    )(place, own, other, halo, prom, norms)


def reverse_bits(index, size):
    return sum(((index >> i) & 1) * (size >> (i + 1)) for i in range(size.bit_length() - 1))


def weight_pieces(place, refs):
    if len(refs) == 1:
        for group in range(2):
            yield refs[0].at[group], group, 0, refs[0].shape[1]
        return
    a_zero, a_one, b_zero, b_one = refs
    deep, half = a_zero.shape[1], a_zero.shape[2]
    for dx in range(2):
        col = place[1] if dx == 0 else 1 - place[1]
        for dy in range(2):
            for k in range(deep):
                row = place[0] ^ reverse_bits(k, deep)
                for part in range(2):
                    ref = ((a_zero, a_one)[dx].at[dy, k], (b_zero, b_one)[dy].at[dx, k])[part]
                    first = ((row * 2 + col) * 2 + part) * half
                    yield ref, dy, pl.multiple_of(first, 16), half


def piece_count(held):
    return 2 if len(held) == 1 else 8 * held[0].shape[1]


def weight_copies(place, held, weight, sem):
    return [
        pltpu.make_async_copy(ref, weight.at[group, pl.ds(first, size)], sem.at[i])
        for i, (ref, group, first, size) in enumerate(weight_pieces(place, held))
    ]


def load_weight(copies):
    for copy in copies:
        copy.start()
    for copy in copies:
        copy.wait()


def attend_kernel(held_count, place, normed, *refs):
    held = refs[:held_count]
    qkv_out, prob_out, att_out, part_out, weight, sem = refs[held_count:]
    copies = weight_copies(place, held, weight, sem)

    @pl.when(pl.program_id(0) == 0)
    def _():
        load_weight(copies)

    third = weight.shape[2] // 4
    live = lax.broadcasted_iota(jnp.int32, (TAIL, 1), 0) < IMG - (CORE - TAIL)
    groups, heads = weight.shape[0], third // HEAD
    pairs = [(group, head) for group in range(groups) for head in range(heads)]
    for group in range(groups):
        qkv_out[group] = dot(normed[...], weight[group, :, : 3 * third]).astype(BF16)

    def part_of(which, group, head):
        at = which * third + head * HEAD
        return qkv_out[group, :CORE, at : at + HEAD]

    scores = [dot(part_of(1, *pair), part_of(0, *pair) * 0.125, NT) for pair in pairs]
    for (group, head), score in zip(pairs, scores):
        score = jnp.concatenate(
            [score[: CORE - TAIL], jnp.where(live, score[CORE - TAIL :], -1e30)]
        )
        exp_scores = jnp.exp(score - jnp.max(score, axis=0, keepdims=True))
        shrink = 1.0 / jnp.sum(exp_scores, axis=0, keepdims=True)
        prob_out[0, group, head] = (exp_scores * shrink).astype(BF16)
    mixed = [dot(part_of(2, *pair), prob_out[(0, *pair)], TN) for pair in pairs]
    total = None
    for group in range(groups):
        mix = jnp.concatenate(mixed[group * heads : (group + 1) * heads]).T.astype(BF16)
        att_out[group, : CORE - TAIL] = mix[: CORE - TAIL]
        att_out[group, CORE - TAIL : CORE] = jnp.where(
            live, mix[CORE - TAIL :], qkv_out[group, CORE - TAIL : CORE, 2 * third :]
        )
        att_out[group, CORE:] = qkv_out[group, CORE:, 2 * third :]
        part = dot(att_out[group], weight[group, :, 3 * third :], NT)
        total = part if total is None else total + part
    part_out[...] = total.astype(BF16)


def attend(place, normed, held, slots):
    rows, deep = normed.shape
    groups, wide = 2, held[0].shape[-1]
    third = wide // 4
    heads = third // HEAD
    return pl.pallas_call(
        functools.partial(attend_kernel, len(held)),
        grid=(slots,),
        in_specs=[SMEM, pl.BlockSpec((SLOT, deep), lambda t: (t, 0))] + [ANY] * len(held),
        out_specs=[
            pl.BlockSpec((groups, SLOT, 3 * third), lambda t: (0, t, 0)),
            pl.BlockSpec((1, groups, heads, CORE, CORE), lambda t: (t, 0, 0, 0, 0)),
            pl.BlockSpec((groups, SLOT, third), lambda t: (0, t, 0)),
            pl.BlockSpec((SLOT, deep), lambda t: (t, 0)),
        ],
        out_shape=[
            jax.ShapeDtypeStruct((groups, rows, 3 * third), BF16),
            jax.ShapeDtypeStruct((slots, groups, heads, CORE, CORE), BF16),
            jax.ShapeDtypeStruct((groups, rows, third), BF16),
            jax.ShapeDtypeStruct((rows, deep), BF16),
        ],
        scratch_shapes=[
            pltpu.VMEM((groups, deep, wide), BF16),
            pltpu.SemaphoreType.DMA((piece_count(held),)),
        ],
        compiler_params=params(),
        cost_estimate=cost(13),
        name="attend",
    )(place, normed, *held)


def mlp_kernel(more, count, *refs):
    parts, refs = refs[:count], refs[count:]
    if more:
        (normed, cot, bias, o_acc, g_acc, *refs) = refs
    else:
        (x_in, one, two, norms, cot, bias, middle_out, normed, *refs) = refs
    (o_out, g_out), grads, refs = refs[:2], refs[2 : 2 + count], refs[2 + count :]
    (bias_out, weight, act, grad, result, in_sem, out_sem) = refs
    step = pl.program_id(0)
    _, pieces, span, wide = weight.shape
    hidden = pieces * span
    cut = 384
    spots = []
    for ref in parts:
        spots.append(sum(size for _, size in spots))
        spots[-1] = (spots[-1], ref.shape[0])
    loads = [
        pltpu.make_async_copy(
            parts[i].at[:, kind], weight.at[kind, pl.ds(first, size)], in_sem.at[2 * i + kind]
        )
        for i, (first, size) in enumerate(spots)
        for kind in range(2)
    ]
    stores = [
        pltpu.make_async_copy(
            result.at[kind, pl.ds(first, size)], grads[i].at[:, kind], out_sem.at[2 * i + kind]
        )
        for i, (first, size) in enumerate(spots)
        for kind in range(2)
    ]

    @pl.when(step == 0)
    def _():
        for copy in loads:
            copy.start()
        bias_out[...] = jnp.zeros_like(bias_out)
        for copy in loads:
            copy.wait()

    rows = pl.ds(pl.multiple_of(step * SLOT, 16), SLOT)
    if not more:
        middle = x_in[...].astype(F32) + (one[...].astype(F32) + two[...].astype(F32))
        middle_out[...] = middle.astype(BF16)
        hat, _ = stats(middle)
        normed[rows] = (hat * norms[2:3] + norms[3:4]).astype(BF16)
    tile_n = normed[rows]
    tile_c = cot[rows]
    for at in range(0, hidden, cut):
        up = weight[0, at // span : (at + cut) // span].reshape(cut, wide)
        down = weight[1, at // span : (at + cut) // span].reshape(cut, wide)
        pre = dot(tile_n, up, NT) + bias[:, at : at + cut]
        cdf = 0.5 * (1.0 + lax.erf(pre * 0.7071067811865476))
        pdf = jnp.exp(-0.5 * pre * pre) * 0.3989422804014327
        act[rows, at : at + cut] = (pre * cdf).astype(BF16)
        grad_low = (dot(tile_c, down, NT) * (cdf + pre * pdf)).astype(BF16)
        grad[rows, at : at + cut] = grad_low
        bias_out[:, at : at + cut] += jnp.sum(grad_low.astype(F32), axis=0, keepdims=True)
    o_sum = dot(act[rows], weight[1].reshape(hidden, wide))
    g_sum = dot(grad[rows], weight[0].reshape(hidden, wide))
    if more:
        o_sum = o_sum + o_acc[...].astype(F32)
        g_sum = g_sum + g_acc[...].astype(F32)
    o_out[...] = o_sum.astype(o_out.dtype)
    g_out[...] = g_sum.astype(g_out.dtype)

    @pl.when(step == pl.num_programs(0) - 1)
    def _():
        sent = 0
        for at in range(0, hidden, cut):
            own = pl.ds(at // span, cut // span)
            shape = (cut // span, span, wide)
            result[0, own] = dot(grad[:, at : at + cut], normed[...], TN).astype(BF16).reshape(shape)
            result[1, own] = dot(act[:, at : at + cut], cot[...], TN).astype(BF16).reshape(shape)
            done = sum((first + size) * span <= at + cut for first, size in spots)
            for copy in stores[2 * sent : 2 * done]:
                copy.start()
            sent = done
        for copy in stores:
            copy.wait()


def mlp(parts, cot, bias, slots, start=None, sums=None):
    rows, wide = cot.shape
    hidden = bias.shape[1]
    span = parts[0].shape[2]
    more = sums is not None
    tile = pl.BlockSpec((SLOT, wide), lambda t: (t, 0))
    wide_bf16 = jax.ShapeDtypeStruct((rows, wide), BF16)
    full = whole(cot.shape)
    count = len(parts)
    if more:
        operands = (*parts, start, cot, bias, *sums)
        specs = [ANY] * count + [full, full, whole(bias.shape), tile, tile]
    else:
        x_in, one, two, norms = start
        operands = (*parts, x_in, one, two, norms, cot, bias)
        specs = [ANY] * count + [tile, tile, tile, whole(norms.shape), full, whole(bias.shape)]
    return pl.pallas_call(
        functools.partial(mlp_kernel, more, count),
        grid=(slots,),
        in_specs=specs,
        out_specs=([] if more else [tile, full])
        + [tile, tile]
        + [ANY] * count
        + [whole(bias.shape)],
        out_shape=([] if more else [wide_bf16, wide_bf16])
        + [wide_bf16, wide_bf16]
        + [jax.ShapeDtypeStruct(v.shape, BF16) for v in parts]
        + [jax.ShapeDtypeStruct(bias.shape, F32)],
        scratch_shapes=[
            pltpu.VMEM((2, hidden // span, span, wide), BF16),
            pltpu.VMEM((rows, hidden), BF16),
            pltpu.VMEM((rows, hidden), BF16),
            pltpu.VMEM((2, hidden // span, span, wide), BF16),
            pltpu.SemaphoreType.DMA((2 * count,)),
            pltpu.SemaphoreType.DMA((2 * count,)),
        ],
        compiler_params=params(),
        cost_estimate=cost(17),
        name="mlp",
    )(*operands)


def add_kernel(a_zero, a_got, b_zero, b_got, a_out, b_out):
    for zero, got, out in ((a_zero, a_got, a_out), (b_zero, b_got, b_out)):
        out[...] = (zero[0].astype(F32) + got[0].astype(F32)).astype(BF16)


def add_second(a_zero, a_got, b_zero, b_got, time):
    shape = a_zero.shape[1:]
    block = pl.BlockSpec((1, 1) + shape[1:], lambda k: (1, k) + (0,) * (len(shape) - 1))
    out = pl.BlockSpec((1,) + shape[1:], lambda k: (k,) + (0,) * (len(shape) - 1))
    return pl.pallas_call(
        add_kernel,
        grid=(shape[0],),
        in_specs=[block] * 4,
        out_specs=[out] * 2,
        out_shape=[jax.ShapeDtypeStruct(shape, BF16)] * 2,
        compiler_params=params(),
        cost_estimate=cost(time),
        name="add_second",
    )(a_zero, a_got, b_zero, b_got)


def split_kernel(count, *refs):
    total = refs[0][...].astype(F32)
    for ref in refs[1:count]:
        total = total + ref[...].astype(F32)
    low = total.astype(BF16)
    half = low.shape[0] // 2
    refs[count][...] = low[:half]
    refs[count + 1][...] = low[half:]


def sum_split(values):
    shape = values[0].shape
    half = (shape[0] // 2,) + shape[1:]
    return pl.pallas_call(
        functools.partial(split_kernel, len(values)),
        grid=(1,),
        in_specs=[whole(shape)] * len(values),
        out_specs=[whole(half)] * 2,
        out_shape=[jax.ShapeDtypeStruct(half, BF16)] * 2,
        compiler_params=params(),
        cost_estimate=cost(2),
        name="sum_split",
    )(*values)


def fold_kernel(a_zero, a_got, a_last, b_zero, b_got, b_last, keep, send):
    half = keep.shape[0]
    for part, (zero, got, last_got) in enumerate(((a_zero, a_got, a_last), (b_zero, b_got, b_last))):
        total = zero[0].astype(F32) + got[0].astype(F32) + last_got[...].astype(F32)
        total = total.astype(BF16)
        keep[:, part] = total[:half]
        send[:, part] = total[half:]


def fold_first(a_zero, a_got, a_last, b_zero, b_got, b_last):
    shape = a_last.shape
    first = whole((1,) + shape)
    out = (shape[0] // 2, 2) + shape[1:]
    return pl.pallas_call(
        fold_kernel,
        grid=(1,),
        in_specs=[first, first, whole(shape)] * 2,
        out_specs=[whole(out)] * 2,
        out_shape=[jax.ShapeDtypeStruct(out, BF16)] * 2,
        compiler_params=params(),
        cost_estimate=cost(3),
        name="fold_first",
    )(a_zero, a_got, a_last, b_zero, b_got, b_last)


def finish_kernel(middle, one, two, dest_own, dest_halo, own_out, halo_out, values):
    step = pl.program_id(0)
    value = middle[...].astype(F32) + (one[...].astype(F32) + two[...].astype(F32))
    values[pl.ds(pl.multiple_of(step * SLOT, 16), SLOT)] = value.astype(BF16)
    spread_rows(values, dest_own, dest_halo, own_out, halo_out)


def spread_rows(values, dest_own, dest_halo, own_out, halo_out):
    @pl.when(pl.program_id(0) == pl.num_programs(0) - 1)
    def _():
        for dest, out in ((dest_own, own_out), (dest_halo, halo_out)):
            shape = (dest.shape[1], values.shape[0])
            at = lax.broadcasted_iota(jnp.int32, shape, 1)
            pick = (at == dest[...].reshape(dest.shape[1], 1)).astype(BF16)
            out[...] = dot(pick, values[...]).astype(out.dtype)


def finish(middle, one, two, dest_own, dest_halo, slots):
    rows, wide = middle.shape
    count = dest_own.shape[1]
    tile = pl.BlockSpec((SLOT, wide), lambda t: (t, 0))
    return pl.pallas_call(
        finish_kernel,
        grid=(slots,),
        in_specs=[tile, tile, tile, whole(dest_own.shape), whole(dest_halo.shape)],
        out_specs=[whole((count, wide)), whole((HALO, wide))],
        out_shape=[
            jax.ShapeDtypeStruct((count, wide), BF16),
            jax.ShapeDtypeStruct((HALO, wide), BF16),
        ],
        scratch_shapes=[pltpu.VMEM((rows, wide), BF16)],
        compiler_params=params(),
        cost_estimate=cost(5),
        name="finish",
    )(middle, one, two, dest_own, dest_halo)


def back_kernel(held_count, place, middle, one, two, cot, norms, qkv, prob, *refs):
    held = refs[:held_count]
    gp_out, dq_out, part_out, sums_out, weight, scored, sem = refs[held_count:]
    step = pl.program_id(0)
    third = weight.shape[2] // 4
    copies = weight_copies(place, held, weight, sem)

    @pl.when(step == 0)
    def _():
        load_weight(copies)
        sums_out[...] = jnp.zeros_like(sums_out)

    grad = one[...].astype(F32) + two[...].astype(F32)
    hat, inverse = stats(middle[...].astype(F32))
    sums_out[0:1] += jnp.sum(grad * hat, axis=0, keepdims=True)
    sums_out[1:2] += jnp.sum(grad, axis=0, keepdims=True)
    grad_middle = cot[...].astype(F32) + norm_back(grad, hat, inverse, norms[2:3])
    grad_proj = grad_middle.astype(BF16)
    gp_out[...] = grad_proj
    live = lax.broadcasted_iota(jnp.int32, (TAIL, 1), 0) < IMG - (CORE - TAIL)
    groups, heads = weight.shape[0], third // HEAD
    pairs = [(group, head) for group in range(groups) for head in range(heads)]

    def part_of(which, group, head):
        at = which * third + head * HEAD
        return qkv[group, :CORE, at : at + HEAD]

    grad_atts, grad_cores = [], []
    for group in range(groups):
        grad_att = dot(grad_proj, weight[group, :, 3 * third :]).astype(BF16)
        tail = grad_att[CORE - TAIL : CORE]
        tail = jnp.where(live, tail, jnp.zeros_like(tail))
        grad_atts.append(grad_att)
        grad_cores.append(jnp.concatenate([grad_att[: CORE - TAIL], tail]))
    grad_heads = [grad_cores[group][:, head * HEAD : (head + 1) * HEAD] for group, head in pairs]
    grad_probs = [dot(part_of(2, *pair), grad, NT) for pair, grad in zip(pairs, grad_heads)]
    grads_v = [dot(prob[(0, *pair)], grad) for pair, grad in zip(pairs, grad_heads)]
    for (group, head), grad_prob in zip(pairs, grad_probs):
        probs = prob[0, group, head].astype(F32)
        center = jnp.sum(probs * grad_prob, axis=0, keepdims=True)
        scored[group * heads + head] = (probs * (grad_prob - center)).astype(BF16)
    grads_q, grads_k = [], []
    for group, head in pairs:
        at = group * heads + head
        grads_q.append(dot(part_of(1, group, head) * 0.125, scored[at], TN))
        grads_k.append(dot(scored[at], part_of(0, group, head) * 0.125))
    total = None
    for group in range(groups):
        own = slice(group * heads, (group + 1) * heads)
        grad_q = jnp.concatenate(grads_q[own]).T.astype(BF16)
        grad_k = jnp.concatenate(grads_k[own], axis=1).astype(BF16)
        grad_v = jnp.concatenate(grads_v[own], axis=1).astype(BF16)
        tail = grad_atts[group][CORE - TAIL : CORE]
        dq_out[group, :CORE, : 3 * third] = jnp.concatenate([grad_q, grad_k, grad_v], axis=1)
        dq_out[group, CORE - TAIL : CORE, 2 * third :] = jnp.where(live, grad_v[CORE - TAIL :], tail)
        dq_out[group, CORE:, : 2 * third] = jnp.zeros((SLOT - CORE, 2 * third), BF16)
        dq_out[group, CORE:, 2 * third :] = grad_atts[group][CORE:]
        part = dot(dq_out[group], weight[group, :, : 3 * third], NT)
        total = part if total is None else total + part
    part_out[...] = total.astype(BF16)


def back(place, middle, one, two, cot, norms, held, qkv, prob, slots):
    rows, wide = middle.shape
    groups, third = qkv.shape[0], qkv.shape[2] // 3
    tile = pl.BlockSpec((SLOT, wide), lambda t: (t, 0))
    tile_q = pl.BlockSpec((groups, SLOT, 3 * third), lambda t: (0, t, 0))
    return pl.pallas_call(
        functools.partial(back_kernel, len(held)),
        grid=(slots,),
        in_specs=[
            SMEM,
            tile,
            tile,
            tile,
            tile,
            whole(norms.shape),
            tile_q,
            pl.BlockSpec((1,) + prob.shape[1:], lambda t: (t, 0, 0, 0, 0)),
        ]
        + [ANY] * len(held),
        out_specs=[tile, tile_q, tile, whole((8, wide))],
        out_shape=[
            jax.ShapeDtypeStruct((rows, wide), BF16),
            jax.ShapeDtypeStruct(qkv.shape, BF16),
            jax.ShapeDtypeStruct((rows, wide), BF16),
            jax.ShapeDtypeStruct((8, wide), F32),
        ],
        scratch_shapes=[
            pltpu.VMEM((groups, wide, 4 * third), BF16),
            pltpu.VMEM((groups * (third // HEAD), CORE, CORE), BF16),
            pltpu.SemaphoreType.DMA((piece_count(held),)),
        ],
        compiler_params=params(),
        cost_estimate=cost(19),
        name="back",
    )(place, middle, one, two, cot, norms, qkv, prob, *held)


def weight_kernel(held_count, place, normed, grad_proj, grad_qkv, att, *refs):
    held = refs[:held_count]
    result, sem = refs[held_count:]
    third = att.shape[2]
    cut = normed.shape[1]
    at = pl.ds(pl.multiple_of(pl.program_id(0) * cut, cut), cut)
    for group in range(2):
        result[group, at, : 3 * third] = dot(normed[...], grad_qkv[group], TN).astype(BF16)
        result[group, at, 3 * third :] = dot(grad_proj[...], att[group], TN).astype(BF16)

    @pl.when(pl.program_id(0) == pl.num_programs(0) - 1)
    def _():
        copies = [
            pltpu.make_async_copy(result.at[group, pl.ds(first, size)], ref, sem.at[i])
            for i, (ref, group, first, size) in enumerate(weight_pieces(place, held))
        ]
        for copy in copies:
            copy.start()
        for copy in copies:
            copy.wait()


def weight_grads(place, normed, grad_proj, grad_qkv, att, held):
    rows, wide = normed.shape
    groups, _, third = att.shape
    cut = 256
    tall = pl.BlockSpec((rows, cut), lambda d: (0, d))
    return pl.pallas_call(
        functools.partial(weight_kernel, len(held)),
        grid=(wide // cut,),
        in_specs=[SMEM, tall, tall, whole(grad_qkv.shape), whole(att.shape)],
        out_specs=[ANY] * len(held),
        out_shape=[jax.ShapeDtypeStruct(v.shape, BF16) for v in held],
        scratch_shapes=[
            pltpu.VMEM((groups, wide, 4 * third), BF16),
            pltpu.SemaphoreType.DMA((piece_count(held),)),
        ],
        compiler_params=params(),
        cost_estimate=cost(9),
        name="weight_grads",
    )(place, normed, grad_proj, grad_qkv, att)


def last_kernel(
    x_in, gm, one, two, norms, dest_own, dest_halo, own_out, halo_out, prompt_out, sums_out, values
):
    step = pl.program_id(0)

    @pl.when(step == 0)
    def _():
        sums_out[...] = jnp.zeros_like(sums_out)
        prompt_out[...] = jnp.zeros_like(prompt_out)

    grad = one[...].astype(F32) + two[...].astype(F32)
    hat, inverse = stats(x_in[...].astype(F32))
    sums_out[0:1] += jnp.sum(grad * hat, axis=0, keepdims=True)
    sums_out[1:2] += jnp.sum(grad, axis=0, keepdims=True)
    grad_in = gm[...].astype(F32) + norm_back(grad, hat, inverse, norms[0:1])
    prompt_out[...] += grad_in[: prompt_out.shape[0]]
    at = lax.broadcasted_iota(jnp.int32, (SLOT, 1), 0)
    value = jnp.where((at >= 1) & (at <= PROMPTS), 0.0, grad_in).astype(BF16)
    values[pl.ds(pl.multiple_of(step * SLOT, 16), SLOT)] = value
    spread_rows(values, dest_own, dest_halo, own_out, halo_out)


def last(x_in, gm, one, two, norms, dest_own, dest_halo, slots):
    rows, wide = x_in.shape
    count = dest_own.shape[1]
    tile = pl.BlockSpec((SLOT, wide), lambda t: (t, 0))
    return pl.pallas_call(
        last_kernel,
        grid=(slots,),
        in_specs=[tile] * 4 + [whole(norms.shape), whole(dest_own.shape), whole(dest_halo.shape)],
        out_specs=[whole((count, wide)), whole((HALO, wide)), whole((56, wide)), whole((8, wide))],
        out_shape=[
            jax.ShapeDtypeStruct((count, wide), F32),
            jax.ShapeDtypeStruct((HALO, wide), BF16),
            jax.ShapeDtypeStruct((56, wide), F32),
            jax.ShapeDtypeStruct((8, wide), F32),
        ],
        scratch_shapes=[pltpu.VMEM((rows, wide), BF16)],
        compiler_params=params(),
        cost_estimate=cost(7),
        name="last",
    )(x_in, gm, one, two, norms, dest_own, dest_halo)


class Grid:
    def __init__(self, rows, heads):
        self.deep = rows // 2
        self.size = rows * heads
        row = lax.axis_index("rows")
        col = lax.axis_index("heads")
        self.z = row // 2
        self.x = row % 2
        self.y = col // 2
        self.c = col % 2

    def send(self, value, move):
        pairs = []
        for i in range(self.size):
            z, x, y, c = move(i // 8, (i // 4) % 2, (i // 2) % 2, i % 2)
            pairs.append((i, ((z * 2 + x) * 2 + y) * 2 + c))
        return lax.ppermute(value, AXES, pairs)

    def by_x(self, value):
        return self.send(value, lambda z, x, y, c: (z, 1 - x, y, c))

    def by_y(self, value):
        return self.send(value, lambda z, x, y, c: (z, x, 1 - y, c))

    def by_core(self, value):
        return self.send(value, lambda z, x, y, c: (z, x, y, 1 - c))

    def by_z(self, value, bit):
        return self.send(value, lambda z, x, y, c: (z ^ bit, x, y, c))

    def gather_z(self, value, axis, *between):
        first = None
        bit = self.deep // 2
        while bit:
            got = self.by_z(value, bit)
            if first is None:
                got = first = after(got, *between)
            value = jnp.concatenate([value, got], axis=axis)
            bit //= 2
        return value, first

    def spread(self, first, second):
        a_next, b_next = tie(self.by_y(first), self.by_x(second))
        a_zero = jnp.stack([first, a_next])
        b_zero = jnp.stack([second, b_next])
        return a_zero, b_zero

    def spread_more(self, a_zero, b_zero):
        return self.by_x(a_zero), self.by_y(b_zero)

    def fold_z(self, keep, got):
        bit, first = 2, got
        while bit < self.deep:
            keep, send = sum_split([keep, got])
            got = self.by_z(send, bit)
            first = send if bit == 2 else first
            bit *= 2
        return keep, got, first

    def to_absolute(self, blocks, z_axis, x_axis):
        return self.turn(jnp.where(self.x == 0, blocks, jnp.flip(blocks, axis=x_axis)), z_axis, False)

    def to_relative(self, blocks, z_axis, x_axis):
        return self.turn(jnp.where(self.x == 0, blocks, jnp.flip(blocks, axis=x_axis)), z_axis, True)

    def turn(self, blocks, z_axis, back):
        shape = blocks.shape
        bits = self.deep.bit_length() - 1
        blocks = blocks.reshape(shape[:z_axis] + (2,) * bits + shape[z_axis + 1 :])
        order = list(range(blocks.ndim))
        order[z_axis : z_axis + bits] = order[z_axis : z_axis + bits][::-1]
        if back:
            blocks = blocks.transpose(order)
        for i in range(bits):
            flipped = jnp.flip(blocks, axis=z_axis + i)
            blocks = jnp.where((self.z >> i) & 1 == 0, blocks, flipped)
        if not back:
            blocks = blocks.transpose(order)
        return blocks.reshape(shape)


def exchange(value, send):
    low = value.astype(BF16)
    return low.astype(F32) + send(low).astype(F32)


def tie(*values):
    return lax.optimization_barrier(values)


def after(value, *earlier):
    return lax.optimization_barrier((value, *earlier))[0]


def local(
    rows,
    heads,
    tokens,
    segment,
    live_token,
    prompt_slot,
    prompts,
    attn_gain,
    attn_shift,
    qkv_weight,
    out_weight,
    mlp_gain,
    mlp_shift,
    up_weight,
    up_bias,
    down_weight,
    cotangent,
):
    grid = Grid(rows, heads)
    deep = grid.deep
    count, wide = tokens.shape
    slots = IMGS_ROW * 2 * count // ROW
    place = jnp.stack([grid.z, grid.x, grid.y, grid.c]).astype(jnp.int32)

    def row_of(vec):
        return vec.astype(F32).reshape(1, -1)

    norms = jnp.stack([attn_gain, attn_shift, mlp_gain, mlp_shift]).astype(F32)

    depth = qkv_weight.shape[0]
    third = qkv_weight.shape[2]
    shard = jnp.concatenate(
        [qkv_weight.reshape(depth, 3 * third), out_weight.swapaxes(0, 1)], axis=1
    ).reshape(2, 1, depth // 2, 4 * third)

    hidden = up_weight.shape[1]
    span = hidden // 2
    halves = jnp.stack(
        [up_weight.swapaxes(0, 1).reshape(2, span, wide), down_weight.reshape(2, span, wide)],
        axis=1,
    )
    bias, first = grid.gather_z(up_bias.reshape(1, hidden), 0)
    shard = after(shard, first)
    got, first = grid.gather_z(shard, 1, bias)
    bias = jnp.stack([bias, grid.by_x(bias)])
    bias = jnp.stack([bias, grid.by_y(bias)])

    code = ((segment % IMGS_ROW) * 2 + live_token).astype(BF16)
    marks = jnp.pad(code[None], ((0, 15), (0, wide - count)))
    own = after(jnp.concatenate([tokens, cotangent, marks]), shard)
    other = grid.by_core(own)
    mine = grid.c == 1 - grid.y
    first_row = jnp.where(grid.y == 0, count - HALO, 0)
    edge_parts = []
    for base in (0, count):
        edge_parts.append(
            jnp.where(
                mine,
                lax.dynamic_slice_in_dim(own, base + first_row, HALO),
                lax.dynamic_slice_in_dim(other, base + first_row, HALO),
            )
        )
    edge_code = jnp.where(mine, own[2 * count :], other[2 * count :])
    edge_code = jnp.where(grid.y == 0, edge_code[:, count - HALO : count], edge_code[:, :HALO])
    edge_parts.append(jnp.pad(edge_code, ((0, 0), (0, wide - HALO))))
    edge = jnp.concatenate(edge_parts)
    halo = grid.by_y(edge)

    got, bias, halo = tie(got, bias, halo)
    a_zero, b_zero = grid.spread(got[0], got[1])
    a_one, b_one = grid.spread_more(a_zero, b_zero)
    x_in, normed, cot, dest_own, dest_halo = prep(place, own, other, halo, prompts, norms, slots)

    held, _ = grid.gather_z(after(halves, first)[:, None], 1, normed)
    mlp_a, mlp_b = held[0], held[1]
    mlp_a0, mlp_b0 = grid.spread(mlp_a, mlp_b)
    mlp_a1, mlp_b1 = grid.spread_more(mlp_a0, mlp_b0)
    bias_a = jnp.stack([bias[:, 0, :, :span], bias[0, :, :, span:]])
    bias_b = jnp.stack([bias[:, 1, :, :span], bias[1, :, :, span:]])

    weights = [a_zero, a_one, b_zero, b_one]
    if (depth // 2) % 16:
        blocks = jnp.stack(
            [
                jnp.concatenate([(a_zero, a_one)[dx][dy], (b_zero, b_one)[dy][dx]], axis=1)
                for dy in range(2)
                for dx in range(2)
            ]
        ).reshape(2, 2, deep, depth, 4 * third)
        blocks = grid.to_absolute(blocks, 2, 1).swapaxes(1, 2)
        weights = [blocks.reshape(2, 2 * deep * depth, 4 * third)]
    qkv, prob, att, part = attend(place, normed, weights, slots)

    fine = span % 16 == 0

    def enter(value):
        value = value.reshape(-1, 2, span, wide)
        if fine:
            return value
        return value.swapaxes(0, 1).reshape(2, -1, 48, wide).swapaxes(0, 1)

    def leave(value):
        if fine:
            return value
        return value.swapaxes(0, 1).reshape(2, -1, span, wide).swapaxes(0, 1)

    start = (x_in, part, grid.by_core(part), norms)
    middle, normed_two, o_sum, g_sum, *grads, grad_bias_a = mlp(
        [enter(mlp_a0), enter(mlp_b0)], cot, row_of(bias_a), slots, start
    )
    grad_a0, grad_b0 = [leave(v).reshape(2, deep, 2, span, wide) for v in grads]
    o_part, g_part, *grads, grad_bias_b = mlp(
        [enter(mlp_a1), enter(mlp_b1)],
        cot,
        row_of(bias_b),
        slots,
        normed_two,
        (o_sum, g_sum),
    )
    grad_a1, grad_b1 = [leave(v).reshape(2, deep, 2, span, wide) for v in grads]
    a_got, b_got = grid.by_x(grad_a1), grid.by_y(grad_b1)
    g_other = grid.by_core(g_part)

    grad_proj, grad_qkv, g_one, sums_two = back(
        place, middle, g_part, g_other, cot, norms, weights, qkv, prob, slots
    )
    g_one_other = grid.by_core(g_one)
    o_other = grid.by_core(after(o_part, g_one))
    weight_blocks = weight_grads(place, normed, grad_proj, grad_qkv, att, weights)
    a_got, b_got, _ = tie(a_got, b_got, weight_blocks[0])
    a_send, b_send = add_second(grad_a0, a_got, grad_b0, b_got, 40)
    a_last, b_last = grid.by_y(a_send), grid.by_x(b_send)
    if len(weight_blocks) == 1:
        blocks = weight_blocks[0].reshape(2, deep, 2, depth, 4 * third).swapaxes(1, 2)
        blocks = grid.to_relative(blocks, 2, 1)
        blocks = blocks.reshape(2, 2, deep, 2, depth // 2, 4 * third)
        weight_blocks = [
            blocks[:, 0, :, 0],
            blocks[:, 1, :, 0],
            blocks[0, :, :, 1],
            blocks[1, :, :, 1],
        ]
    att_a0, att_a1, att_b0, att_b1 = weight_blocks
    att_a_got, att_b_got = grid.by_x(after(att_a1, a_send)), grid.by_y(after(att_b1, b_send))
    tok_own, tok_halo, prompt_sum, sums_one = last(
        x_in, grad_proj, g_one, after(g_one_other, a_send), norms, dest_own, dest_halo, slots
    )

    g_a = grad_bias_a.reshape(2, 2, deep, span)
    g_b = grad_bias_b.reshape(2, 2, deep, span)
    bias_blocks = jnp.stack(
        [jnp.stack([g_a[0], g_b[0]], axis=1), jnp.stack([g_a[1], g_b[1]], axis=0)], axis=3
    )
    bias_blocks = grid.to_absolute(bias_blocks, 2, 1)
    bias_blocks = jnp.where(grid.y == 0, bias_blocks, jnp.flip(bias_blocks, axis=0))
    small = jnp.concatenate(
        [prompt_sum, sums_one[:2], sums_two[:2], bias_blocks.reshape(-1, wide)]
    )
    out_own, out_halo = finish(
        middle, o_part, after(o_other, tok_halo), dest_own, dest_halo, slots
    )
    edges = grid.by_y(jnp.concatenate([out_halo, tok_halo]))
    small = exchange(small, lambda v: grid.by_z(v, 1))
    a_last, b_last, _ = tie(a_last, b_last, out_halo)
    grad_keep, grad_send = fold_first(grad_a0, a_got, a_last, grad_b0, b_got, b_last)
    grad_got = grid.by_z(grad_send, 1)
    att_a_got, att_b_got, small, _ = tie(att_a_got, att_b_got, small, grad_send)
    stride = 2
    while stride < deep:
        small = exchange(small, lambda v, stride=stride: grid.by_z(v, stride))
        stride *= 2
    a_send, b_send = add_second(att_a0, att_a_got, att_b0, att_b_got, 4)
    att_a_last, att_b_last = grid.by_y(a_send), grid.by_x(b_send)
    grad_got, _ = tie(grad_got, a_send)
    grad_keep, grad_got, grad_send = grid.fold_z(grad_keep, grad_got)
    att_a_last, att_b_last, small, edges, _ = tie(
        att_a_last, att_b_last, small, edges, grad_send
    )
    small = exchange(small, grid.by_x)
    att_keep, att_send = fold_first(att_a0, att_a_got, att_a_last, att_b0, att_b_got, att_b_last)
    att_got = grid.by_z(att_send, 1)
    att_got, small, grad_got = tie(att_got, small, grad_got)
    small = exchange(small, grid.by_y)
    att_keep, att_got, _ = grid.fold_z(att_keep, att_got)
    grad_shard = (grad_keep.astype(F32) + grad_got.astype(F32))[0]
    grad_up = grad_shard[:, 0].reshape(hidden, wide).swapaxes(0, 1)
    grad_down = grad_shard[:, 1].reshape(hidden, wide)
    att_shard = att_keep.astype(F32) + att_got.astype(F32)
    att_shard = att_shard.reshape(depth, 4 * third)
    grad_qkv_weight = att_shard[:, : 3 * third].reshape(depth, 3, third)
    grad_out_weight = att_shard[:, 3 * third :].swapaxes(0, 1)

    def merge(value, edge):
        edge = edge.astype(value.dtype)
        ends = jnp.where((grid.y == 0) & (grid.c == 1), edge, 0)
        begins = jnp.where((grid.y == 1) & (grid.c == 0), edge, 0)
        value = value.at[count - HALO :].add(ends)
        return value.at[:HALO].add(begins)

    bias_all = small[60:].reshape(2, 2, deep, hidden)
    grad_bias = lax.dynamic_slice(
        bias_all, (grid.y, grid.x, grid.z, jnp.int32(0)), (1, 1, 1, hidden)
    ).reshape(hidden)
    return (
        merge(out_own, edges[:HALO]),
        merge(tok_own, edges[HALO:]),
        small[1 : 1 + PROMPTS],
        small[56],
        small[57],
        grad_qkv_weight,
        grad_out_weight,
        small[58],
        small[59],
        grad_up,
        grad_bias,
        grad_down,
    )


def solution(mesh):
    both = P(AXES)
    lead = P(AXES, None)
    return jax.shard_map(
        functools.partial(local, mesh.shape["rows"], mesh.shape["heads"]),
        mesh=mesh,
        in_specs=(
            lead,
            both,
            both,
            both,
            P(),
            P(),
            P(),
            P("rows", None, "heads"),
            P("heads", "rows"),
            P(),
            P(),
            P(None, AXES),
            both,
            lead,
            lead,
        ),
        out_specs=(
            lead,
            lead,
            P(),
            P(),
            P(),
            P("rows", None, "heads"),
            P("heads", "rows"),
            P(),
            P(),
            P(None, AXES),
            both,
            lead,
        ),
        check_vma=False,
    )
```

```python
import functools

import jax
import jax.numpy as jnp
from jax import lax
from jax.experimental import pallas as pl
from jax.experimental.pallas import tpu as pltpu
from jax.sharding import PartitionSpec as P

HEAD = 64
ROW = 2048
IMG = 247
IMGS_ROW = 8
PROMPTS = 50
SLOT = 272
CORE = 256
TAIL = 16
HALO = 48
EPSILON = 1e-06
AXES = ("rows", "heads")
F32 = jnp.float32
BF16 = jnp.bfloat16
VMEM_LIMIT = 56 * 1024 * 1024

NN = (((1,), (0,)), ((), ()))
NT = (((1,), (1,)), ((), ()))
TN = (((0,), (0,)), ((), ()))


def dot(left, right, dims=NN):
    return lax.dot_general(left, right, dims, preferred_element_type=F32)


def whole(shape):
    return pl.BlockSpec(shape, lambda *_: (0,) * len(shape))


def params(**more):
    return pltpu.CompilerParams(vmem_limit_bytes=VMEM_LIMIT, **more)


SCALE = 0.15


def cost(time):
    return pl.CostEstimate(flops=int(time * SCALE * 1.15e9), bytes_accessed=1, transcendentals=0)


SMEM = pl.BlockSpec(memory_space=pltpu.SMEM)
ANY = pl.BlockSpec(memory_space=pl.ANY)


def stats(values):
    center = values - jnp.mean(values, axis=-1, keepdims=True)
    inverse = lax.rsqrt(jnp.mean(center * center, axis=-1, keepdims=True) + EPSILON)
    return center * inverse, inverse


def norm_back(grad, hat, inverse, gain):
    inner = grad * gain
    first = jnp.mean(inner, axis=-1, keepdims=True)
    second = jnp.mean(inner * hat, axis=-1, keepdims=True)
    return inverse * (inner - first - hat * second)


def prep_kernel(
    place, own, other, halo, prom, norms, x_out, n_out, cot_out, dest_own, dest_halo, d_oth
):
    step = pl.program_id(0)
    count = d_oth.shape[1]
    slots = pl.num_programs(0)
    y_at, c_at = place[2], place[3]

    @pl.when(step == 0)
    def _():
        big = 1 << 20
        spans = (
            (own[2 * count : 2 * count + 16, :count], 2 * count * y_at + count * c_at, True),
            (other[2 * count : 2 * count + 16, :count], 2 * count * y_at + count * (1 - c_at), True),
            (halo[2 * HALO : 2 * HALO + 16, :HALO], 2 * count - HALO * y_at, False),
        )
        parts = []
        for marks, base, home in spans:
            code = marks.astype(F32)[0:1].astype(jnp.int32)
            live = (code & 1) > 0
            slot = (code >> 1) - slots * y_at
            pos = base + lax.broadcasted_iota(jnp.int32, code.shape, 1)
            parts.append((live, slot, pos, home))
        starts = []
        for k in range(slots):
            low = None
            for live, slot, pos, home in parts:
                here = jnp.min(jnp.where(live & (slot == k), pos, big), axis=1, keepdims=True)
                low = here if low is None else jnp.minimum(low, here)
            starts.append(low)
        pads_own, pads_other = [
            jnp.sum(jnp.where(part[0], 0, 1), axis=1, keepdims=True) for part in parts[:2]
        ]
        befores = (c_at * pads_other, (1 - c_at) * pads_own, None)
        results = []
        for (live, slot, pos, home), before in zip(parts, befores):
            dest = jnp.full(pos.shape, -1, jnp.int32)
            for k in range(slots):
                dest = jnp.where(live & (slot == k), pos - starts[k] + k * SLOT, dest)
            if home:
                pads = jnp.where(live, 0.0, 1.0).astype(BF16)
                size = pads.shape[1]
                earlier = (
                    lax.broadcasted_iota(jnp.int32, (size, size), 0)
                    < lax.broadcasted_iota(jnp.int32, (size, size), 1)
                )
                wide = jnp.broadcast_to(pads, (16, size))
                rank = dot(wide, earlier.astype(BF16))[0:1].astype(jnp.int32) + before
                spare = (rank & (slots - 1)) * SLOT + IMG + (rank >> (slots.bit_length() - 1))
                dest = jnp.where(live, dest, spare)
            results.append(dest)
        dest_own[...] = results[0]
        d_oth[...] = results[1]
        dest_halo[...] = results[2]

    rows = step * SLOT
    tokens = cots = None
    for dest, ref, size in (
        (dest_own, own, count),
        (d_oth, other, count),
        (dest_halo, halo, HALO),
    ):
        at = rows + lax.broadcasted_iota(jnp.int32, (SLOT, size), 0)
        pick = (at == dest[...]).astype(BF16)
        one = dot(pick, ref[0:size])
        two = dot(pick, ref[size : 2 * size])
        tokens = one if tokens is None else tokens + one
        cots = two if cots is None else cots + two
    at = lax.broadcasted_iota(jnp.int32, (SLOT, 1), 0)
    slot_row = lax.broadcasted_iota(jnp.int32, (SLOT, PROMPTS), 0)
    which = lax.broadcasted_iota(jnp.int32, (SLOT, PROMPTS), 1)
    prompted = dot((slot_row == which + 1).astype(BF16), prom[...])
    inputs = jnp.where((at >= 1) & (at <= PROMPTS), prompted, tokens)
    hat, _ = stats(inputs)
    x_out[...] = inputs.astype(BF16)
    n_out[...] = (hat * norms[0:1] + norms[1:2]).astype(BF16)
    cot_out[...] = cots.astype(BF16)


def prep(place, own, other, halo, prom, norms, slots):
    count = own.shape[0] // 2 - 8
    wide = own.shape[1]
    rows = slots * SLOT
    tile = pl.BlockSpec((SLOT, wide), lambda t: (t, 0))
    array = jax.ShapeDtypeStruct((rows, wide), BF16)
    return pl.pallas_call(
        prep_kernel,
        grid=(slots,),
        in_specs=[SMEM] + [whole(v.shape) for v in (own, other, halo, prom, norms)],
        out_specs=[tile, tile, tile, whole((1, count)), whole((1, HALO))],
        out_shape=[
            array,
            array,
            array,
            jax.ShapeDtypeStruct((1, count), jnp.int32),
            jax.ShapeDtypeStruct((1, HALO), jnp.int32),
        ],
        scratch_shapes=[pltpu.VMEM((1, count), jnp.int32)],
        compiler_params=params(),
        cost_estimate=cost(8),
        name="prep",
    )(place, own, other, halo, prom, norms)


def reverse_bits(index, size):
    return sum(((index >> i) & 1) * (size >> (i + 1)) for i in range(size.bit_length() - 1))


def weight_pieces(place, refs):
    if len(refs) == 1:
        for group in range(2):
            yield refs[0].at[group], group, 0, refs[0].shape[1]
        return
    a_zero, a_one, b_zero, b_one = refs
    deep, half = a_zero.shape[1], a_zero.shape[2]
    for dx in range(2):
        col = place[1] if dx == 0 else 1 - place[1]
        for dy in range(2):
            for k in range(deep):
                row = place[0] ^ reverse_bits(k, deep)
                for part in range(2):
                    ref = ((a_zero, a_one)[dx].at[dy, k], (b_zero, b_one)[dy].at[dx, k])[part]
                    first = ((row * 2 + col) * 2 + part) * half
                    yield ref, dy, pl.multiple_of(first, 16), half


def piece_count(held):
    return 2 if len(held) == 1 else 8 * held[0].shape[1]


def weight_copies(place, held, weight, sem):
    return [
        pltpu.make_async_copy(ref, weight.at[group, pl.ds(first, size)], sem.at[i])
        for i, (ref, group, first, size) in enumerate(weight_pieces(place, held))
    ]


def load_weight(copies):
    for copy in copies:
        copy.start()
    for copy in copies:
        copy.wait()


def attend_kernel(held_count, place, normed, *refs):
    held = refs[:held_count]
    qkv_out, prob_out, att_out, part_out, weight, sem = refs[held_count:]
    copies = weight_copies(place, held, weight, sem)

    @pl.when(pl.program_id(0) == 0)
    def _():
        load_weight(copies)

    third = weight.shape[2] // 4
    live = lax.broadcasted_iota(jnp.int32, (TAIL, 1), 0) < IMG - (CORE - TAIL)
    groups, heads = weight.shape[0], third // HEAD
    pairs = [(group, head) for group in range(groups) for head in range(heads)]
    for group in range(groups):
        qkv_out[group] = dot(normed[...], weight[group, :, : 3 * third]).astype(BF16)

    def part_of(which, group, head):
        at = which * third + head * HEAD
        return qkv_out[group, :CORE, at : at + HEAD]

    scores = [dot(part_of(1, *pair), part_of(0, *pair) * 0.125, NT) for pair in pairs]
    for (group, head), score in zip(pairs, scores):
        score = jnp.concatenate(
            [score[: CORE - TAIL], jnp.where(live, score[CORE - TAIL :], -1e30)]
        )
        exp_scores = jnp.exp(score - jnp.max(score, axis=0, keepdims=True))
        shrink = 1.0 / jnp.sum(exp_scores, axis=0, keepdims=True)
        prob_out[0, group, head] = (exp_scores * shrink).astype(BF16)
    mixed = [dot(part_of(2, *pair), prob_out[(0, *pair)], TN) for pair in pairs]
    total = None
    for group in range(groups):
        mix = jnp.concatenate(mixed[group * heads : (group + 1) * heads]).T.astype(BF16)
        att_out[group, : CORE - TAIL] = mix[: CORE - TAIL]
        att_out[group, CORE - TAIL : CORE] = jnp.where(
            live, mix[CORE - TAIL :], qkv_out[group, CORE - TAIL : CORE, 2 * third :]
        )
        att_out[group, CORE:] = qkv_out[group, CORE:, 2 * third :]
        part = dot(att_out[group], weight[group, :, 3 * third :], NT)
        total = part if total is None else total + part
    part_out[...] = total.astype(BF16)


def attend(place, normed, held, slots):
    rows, deep = normed.shape
    groups, wide = 2, held[0].shape[-1]
    third = wide // 4
    heads = third // HEAD
    return pl.pallas_call(
        functools.partial(attend_kernel, len(held)),
        grid=(slots,),
        in_specs=[SMEM, pl.BlockSpec((SLOT, deep), lambda t: (t, 0))] + [ANY] * len(held),
        out_specs=[
            pl.BlockSpec((groups, SLOT, 3 * third), lambda t: (0, t, 0)),
            pl.BlockSpec((1, groups, heads, CORE, CORE), lambda t: (t, 0, 0, 0, 0)),
            pl.BlockSpec((groups, SLOT, third), lambda t: (0, t, 0)),
            pl.BlockSpec((SLOT, deep), lambda t: (t, 0)),
        ],
        out_shape=[
            jax.ShapeDtypeStruct((groups, rows, 3 * third), BF16),
            jax.ShapeDtypeStruct((slots, groups, heads, CORE, CORE), BF16),
            jax.ShapeDtypeStruct((groups, rows, third), BF16),
            jax.ShapeDtypeStruct((rows, deep), BF16),
        ],
        scratch_shapes=[
            pltpu.VMEM((groups, deep, wide), BF16),
            pltpu.SemaphoreType.DMA((piece_count(held),)),
        ],
        compiler_params=params(),
        cost_estimate=cost(13),
        name="attend",
    )(place, normed, *held)


def mlp_kernel(more, count, *refs):
    parts, refs = refs[:count], refs[count:]
    if more:
        (normed, cot, bias, o_acc, g_acc, *refs) = refs
    else:
        (x_in, one, two, norms, cot, bias, middle_out, normed, *refs) = refs
    (o_out, g_out), grads, refs = refs[:2], refs[2 : 2 + count], refs[2 + count :]
    (bias_out, weight, act, grad, result, in_sem, out_sem) = refs
    step = pl.program_id(0)
    _, pieces, span, wide = weight.shape
    hidden = pieces * span
    cut = 384
    spots = []
    for ref in parts:
        spots.append(sum(size for _, size in spots))
        spots[-1] = (spots[-1], ref.shape[0])
    loads = [
        pltpu.make_async_copy(
            parts[i].at[:, kind], weight.at[kind, pl.ds(first, size)], in_sem.at[2 * i + kind]
        )
        for i, (first, size) in enumerate(spots)
        for kind in range(2)
    ]
    stores = [
        pltpu.make_async_copy(
            result.at[kind, pl.ds(first, size)], grads[i].at[:, kind], out_sem.at[2 * i + kind]
        )
        for i, (first, size) in enumerate(spots)
        for kind in range(2)
    ]

    @pl.when(step == 0)
    def _():
        for copy in loads:
            copy.start()
        bias_out[...] = jnp.zeros_like(bias_out)
        for copy in loads:
            copy.wait()

    rows = pl.ds(pl.multiple_of(step * SLOT, 16), SLOT)
    if not more:
        middle = x_in[...].astype(F32) + (one[...].astype(F32) + two[...].astype(F32))
        middle_out[...] = middle.astype(BF16)
        hat, _ = stats(middle)
        normed[rows] = (hat * norms[2:3] + norms[3:4]).astype(BF16)
    tile_n = normed[rows]
    tile_c = cot[rows]
    for at in range(0, hidden, cut):
        up = weight[0, at // span : (at + cut) // span].reshape(cut, wide)
        down = weight[1, at // span : (at + cut) // span].reshape(cut, wide)
        pre = dot(tile_n, up, NT) + bias[:, at : at + cut]
        cdf = 0.5 * (1.0 + lax.erf(pre * 0.7071067811865476))
        pdf = jnp.exp(-0.5 * pre * pre) * 0.3989422804014327
        act[rows, at : at + cut] = (pre * cdf).astype(BF16)
        grad_low = (dot(tile_c, down, NT) * (cdf + pre * pdf)).astype(BF16)
        grad[rows, at : at + cut] = grad_low
        bias_out[:, at : at + cut] += jnp.sum(grad_low.astype(F32), axis=0, keepdims=True)
    o_sum = dot(act[rows], weight[1].reshape(hidden, wide))
    g_sum = dot(grad[rows], weight[0].reshape(hidden, wide))
    if more:
        o_sum = o_sum + o_acc[...].astype(F32)
        g_sum = g_sum + g_acc[...].astype(F32)
    o_out[...] = o_sum.astype(o_out.dtype)
    g_out[...] = g_sum.astype(g_out.dtype)

    @pl.when(step == pl.num_programs(0) - 1)
    def _():
        sent = 0
        for at in range(0, hidden, cut):
            own = pl.ds(at // span, cut // span)
            shape = (cut // span, span, wide)
            result[0, own] = dot(grad[:, at : at + cut], normed[...], TN).astype(BF16).reshape(shape)
            result[1, own] = dot(act[:, at : at + cut], cot[...], TN).astype(BF16).reshape(shape)
            done = sum((first + size) * span <= at + cut for first, size in spots)
            for copy in stores[2 * sent : 2 * done]:
                copy.start()
            sent = done
        for copy in stores:
            copy.wait()


def mlp(parts, cot, bias, slots, start=None, sums=None):
    rows, wide = cot.shape
    hidden = bias.shape[1]
    span = parts[0].shape[2]
    more = sums is not None
    tile = pl.BlockSpec((SLOT, wide), lambda t: (t, 0))
    wide_bf16 = jax.ShapeDtypeStruct((rows, wide), BF16)
    full = whole(cot.shape)
    count = len(parts)
    if more:
        operands = (*parts, start, cot, bias, *sums)
        specs = [ANY] * count + [full, full, whole(bias.shape), tile, tile]
    else:
        x_in, one, two, norms = start
        operands = (*parts, x_in, one, two, norms, cot, bias)
        specs = [ANY] * count + [tile, tile, tile, whole(norms.shape), full, whole(bias.shape)]
    return pl.pallas_call(
        functools.partial(mlp_kernel, more, count),
        grid=(slots,),
        in_specs=specs,
        out_specs=([] if more else [tile, full])
        + [tile, tile]
        + [ANY] * count
        + [whole(bias.shape)],
        out_shape=([] if more else [wide_bf16, wide_bf16])
        + [wide_bf16, wide_bf16]
        + [jax.ShapeDtypeStruct(v.shape, BF16) for v in parts]
        + [jax.ShapeDtypeStruct(bias.shape, F32)],
        scratch_shapes=[
            pltpu.VMEM((2, hidden // span, span, wide), BF16),
            pltpu.VMEM((rows, hidden), BF16),
            pltpu.VMEM((rows, hidden), BF16),
            pltpu.VMEM((2, hidden // span, span, wide), BF16),
            pltpu.SemaphoreType.DMA((2 * count,)),
            pltpu.SemaphoreType.DMA((2 * count,)),
        ],
        compiler_params=params(),
        cost_estimate=cost(17),
        name="mlp",
    )(*operands)


def add_kernel(a_zero, a_got, b_zero, b_got, a_out, b_out):
    for zero, got, out in ((a_zero, a_got, a_out), (b_zero, b_got, b_out)):
        out[...] = (zero[0].astype(F32) + got[0].astype(F32)).astype(BF16)


def add_second(a_zero, a_got, b_zero, b_got, time):
    shape = a_zero.shape[1:]
    size = shape[0] // 2
    block = pl.BlockSpec((1, size) + shape[1:], lambda k: (1, k) + (0,) * (len(shape) - 1))
    out = pl.BlockSpec((size,) + shape[1:], lambda k: (k,) + (0,) * (len(shape) - 1))
    return pl.pallas_call(
        add_kernel,
        grid=(2,),
        in_specs=[block] * 4,
        out_specs=[out] * 2,
        out_shape=[jax.ShapeDtypeStruct(shape, BF16)] * 2,
        compiler_params=params(),
        cost_estimate=cost(time),
        name="add_second",
    )(a_zero, a_got, b_zero, b_got)


def split_kernel(count, *refs):
    total = refs[0][...].astype(F32)
    for ref in refs[1:count]:
        total = total + ref[...].astype(F32)
    low = total.astype(BF16)
    half = low.shape[0] // 2
    refs[count][...] = low[:half]
    refs[count + 1][...] = low[half:]


def sum_split(values):
    shape = values[0].shape
    half = (shape[0] // 2,) + shape[1:]
    return pl.pallas_call(
        functools.partial(split_kernel, len(values)),
        grid=(1,),
        in_specs=[whole(shape)] * len(values),
        out_specs=[whole(half)] * 2,
        out_shape=[jax.ShapeDtypeStruct(half, BF16)] * 2,
        compiler_params=params(),
        cost_estimate=cost(2),
        name="sum_split",
    )(*values)


def fold_kernel(a_zero, a_got, a_last, b_zero, b_got, b_last, keep, send):
    half = keep.shape[0]
    for part, (zero, got, last_got) in enumerate(((a_zero, a_got, a_last), (b_zero, b_got, b_last))):
        total = zero[0].astype(F32) + got[0].astype(F32) + last_got[...].astype(F32)
        total = total.astype(BF16)
        keep[:, part] = total[:half]
        send[:, part] = total[half:]


def fold_first(a_zero, a_got, a_last, b_zero, b_got, b_last):
    shape = a_last.shape
    first = whole((1,) + shape)
    out = (shape[0] // 2, 2) + shape[1:]
    return pl.pallas_call(
        fold_kernel,
        grid=(1,),
        in_specs=[first, first, whole(shape)] * 2,
        out_specs=[whole(out)] * 2,
        out_shape=[jax.ShapeDtypeStruct(out, BF16)] * 2,
        compiler_params=params(),
        cost_estimate=cost(3),
        name="fold_first",
    )(a_zero, a_got, a_last, b_zero, b_got, b_last)


def finish_kernel(middle, one, two, dest_own, dest_halo, own_out, halo_out, values):
    step = pl.program_id(0)
    value = middle[...].astype(F32) + (one[...].astype(F32) + two[...].astype(F32))
    values[pl.ds(pl.multiple_of(step * SLOT, 16), SLOT)] = value.astype(BF16)
    spread_rows(values, dest_own, dest_halo, own_out, halo_out)


def spread_rows(values, dest_own, dest_halo, own_out, halo_out):
    @pl.when(pl.program_id(0) == pl.num_programs(0) - 1)
    def _():
        for dest, out in ((dest_own, own_out), (dest_halo, halo_out)):
            shape = (dest.shape[1], values.shape[0])
            at = lax.broadcasted_iota(jnp.int32, shape, 1)
            pick = (at == dest[...].reshape(dest.shape[1], 1)).astype(BF16)
            out[...] = dot(pick, values[...]).astype(out.dtype)


def finish(middle, one, two, dest_own, dest_halo, slots):
    rows, wide = middle.shape
    count = dest_own.shape[1]
    tile = pl.BlockSpec((SLOT, wide), lambda t: (t, 0))
    return pl.pallas_call(
        finish_kernel,
        grid=(slots,),
        in_specs=[tile, tile, tile, whole(dest_own.shape), whole(dest_halo.shape)],
        out_specs=[whole((count, wide)), whole((HALO, wide))],
        out_shape=[
            jax.ShapeDtypeStruct((count, wide), BF16),
            jax.ShapeDtypeStruct((HALO, wide), BF16),
        ],
        scratch_shapes=[pltpu.VMEM((rows, wide), BF16)],
        compiler_params=params(),
        cost_estimate=cost(5),
        name="finish",
    )(middle, one, two, dest_own, dest_halo)


def back_kernel(held_count, place, middle, one, two, cot, norms, qkv, prob, *refs):
    held = refs[:held_count]
    gp_out, dq_out, part_out, sums_out, weight, scored, sem = refs[held_count:]
    step = pl.program_id(0)
    third = weight.shape[2] // 4
    copies = weight_copies(place, held, weight, sem)

    @pl.when(step == 0)
    def _():
        load_weight(copies)
        sums_out[...] = jnp.zeros_like(sums_out)

    grad = one[...].astype(F32) + two[...].astype(F32)
    hat, inverse = stats(middle[...].astype(F32))
    sums_out[0:1] += jnp.sum(grad * hat, axis=0, keepdims=True)
    sums_out[1:2] += jnp.sum(grad, axis=0, keepdims=True)
    grad_middle = cot[...].astype(F32) + norm_back(grad, hat, inverse, norms[2:3])
    grad_proj = grad_middle.astype(BF16)
    gp_out[...] = grad_proj
    live = lax.broadcasted_iota(jnp.int32, (TAIL, 1), 0) < IMG - (CORE - TAIL)
    groups, heads = weight.shape[0], third // HEAD
    pairs = [(group, head) for group in range(groups) for head in range(heads)]

    def part_of(which, group, head):
        at = which * third + head * HEAD
        return qkv[group, :CORE, at : at + HEAD]

    grad_atts, grad_cores = [], []
    for group in range(groups):
        grad_att = dot(grad_proj, weight[group, :, 3 * third :]).astype(BF16)
        tail = grad_att[CORE - TAIL : CORE]
        tail = jnp.where(live, tail, jnp.zeros_like(tail))
        grad_atts.append(grad_att)
        grad_cores.append(jnp.concatenate([grad_att[: CORE - TAIL], tail]))
    grad_heads = [grad_cores[group][:, head * HEAD : (head + 1) * HEAD] for group, head in pairs]
    grad_probs = [dot(part_of(2, *pair), grad, NT) for pair, grad in zip(pairs, grad_heads)]
    grads_v = [dot(prob[(0, *pair)], grad) for pair, grad in zip(pairs, grad_heads)]
    for (group, head), grad_prob in zip(pairs, grad_probs):
        probs = prob[0, group, head].astype(F32)
        center = jnp.sum(probs * grad_prob, axis=0, keepdims=True)
        scored[group * heads + head] = (probs * (grad_prob - center)).astype(BF16)
    grads_q, grads_k = [], []
    for group, head in pairs:
        at = group * heads + head
        grads_q.append(dot(part_of(1, group, head) * 0.125, scored[at], TN))
        grads_k.append(dot(scored[at], part_of(0, group, head) * 0.125))
    total = None
    for group in range(groups):
        own = slice(group * heads, (group + 1) * heads)
        grad_q = jnp.concatenate(grads_q[own]).T.astype(BF16)
        grad_k = jnp.concatenate(grads_k[own], axis=1).astype(BF16)
        grad_v = jnp.concatenate(grads_v[own], axis=1).astype(BF16)
        tail = grad_atts[group][CORE - TAIL : CORE]
        dq_out[group, :CORE, : 3 * third] = jnp.concatenate([grad_q, grad_k, grad_v], axis=1)
        dq_out[group, CORE - TAIL : CORE, 2 * third :] = jnp.where(live, grad_v[CORE - TAIL :], tail)
        dq_out[group, CORE:, : 2 * third] = jnp.zeros((SLOT - CORE, 2 * third), BF16)
        dq_out[group, CORE:, 2 * third :] = grad_atts[group][CORE:]
        part = dot(dq_out[group], weight[group, :, : 3 * third], NT)
        total = part if total is None else total + part
    part_out[...] = total.astype(BF16)


def back(place, middle, one, two, cot, norms, held, qkv, prob, slots):
    rows, wide = middle.shape
    groups, third = qkv.shape[0], qkv.shape[2] // 3
    tile = pl.BlockSpec((SLOT, wide), lambda t: (t, 0))
    tile_q = pl.BlockSpec((groups, SLOT, 3 * third), lambda t: (0, t, 0))
    return pl.pallas_call(
        functools.partial(back_kernel, len(held)),
        grid=(slots,),
        in_specs=[
            SMEM,
            tile,
            tile,
            tile,
            tile,
            whole(norms.shape),
            tile_q,
            pl.BlockSpec((1,) + prob.shape[1:], lambda t: (t, 0, 0, 0, 0)),
        ]
        + [ANY] * len(held),
        out_specs=[tile, tile_q, tile, whole((8, wide))],
        out_shape=[
            jax.ShapeDtypeStruct((rows, wide), BF16),
            jax.ShapeDtypeStruct(qkv.shape, BF16),
            jax.ShapeDtypeStruct((rows, wide), BF16),
            jax.ShapeDtypeStruct((8, wide), F32),
        ],
        scratch_shapes=[
            pltpu.VMEM((groups, wide, 4 * third), BF16),
            pltpu.VMEM((groups * (third // HEAD), CORE, CORE), BF16),
            pltpu.SemaphoreType.DMA((piece_count(held),)),
        ],
        compiler_params=params(),
        cost_estimate=cost(19),
        name="back",
    )(place, middle, one, two, cot, norms, qkv, prob, *held)


def weight_kernel(held_count, place, normed, grad_proj, grad_qkv, att, *refs):
    held = refs[:held_count]
    result, sem = refs[held_count:]
    third = att.shape[2]
    cut = normed.shape[1]
    at = pl.ds(pl.multiple_of(pl.program_id(0) * cut, cut), cut)
    for group in range(2):
        result[group, at, : 3 * third] = dot(normed[...], grad_qkv[group], TN).astype(BF16)
        result[group, at, 3 * third :] = dot(grad_proj[...], att[group], TN).astype(BF16)

    @pl.when(pl.program_id(0) == pl.num_programs(0) - 1)
    def _():
        copies = [
            pltpu.make_async_copy(result.at[group, pl.ds(first, size)], ref, sem.at[i])
            for i, (ref, group, first, size) in enumerate(weight_pieces(place, held))
        ]
        for copy in copies:
            copy.start()
        for copy in copies:
            copy.wait()


def weight_grads(place, normed, grad_proj, grad_qkv, att, held):
    rows, wide = normed.shape
    groups, _, third = att.shape
    cut = 256
    tall = pl.BlockSpec((rows, cut), lambda d: (0, d))
    return pl.pallas_call(
        functools.partial(weight_kernel, len(held)),
        grid=(wide // cut,),
        in_specs=[SMEM, tall, tall, whole(grad_qkv.shape), whole(att.shape)],
        out_specs=[ANY] * len(held),
        out_shape=[jax.ShapeDtypeStruct(v.shape, BF16) for v in held],
        scratch_shapes=[
            pltpu.VMEM((groups, wide, 4 * third), BF16),
            pltpu.SemaphoreType.DMA((piece_count(held),)),
        ],
        compiler_params=params(),
        cost_estimate=cost(9),
        name="weight_grads",
    )(place, normed, grad_proj, grad_qkv, att)


def last_kernel(
    x_in, gm, one, two, norms, dest_own, dest_halo, own_out, halo_out, prompt_out, sums_out, values
):
    step = pl.program_id(0)

    @pl.when(step == 0)
    def _():
        sums_out[...] = jnp.zeros_like(sums_out)
        prompt_out[...] = jnp.zeros_like(prompt_out)

    grad = one[...].astype(F32) + two[...].astype(F32)
    hat, inverse = stats(x_in[...].astype(F32))
    sums_out[0:1] += jnp.sum(grad * hat, axis=0, keepdims=True)
    sums_out[1:2] += jnp.sum(grad, axis=0, keepdims=True)
    grad_in = gm[...].astype(F32) + norm_back(grad, hat, inverse, norms[0:1])
    prompt_out[...] += grad_in[: prompt_out.shape[0]]
    at = lax.broadcasted_iota(jnp.int32, (SLOT, 1), 0)
    value = jnp.where((at >= 1) & (at <= PROMPTS), 0.0, grad_in).astype(BF16)
    values[pl.ds(pl.multiple_of(step * SLOT, 16), SLOT)] = value
    spread_rows(values, dest_own, dest_halo, own_out, halo_out)


def last(x_in, gm, one, two, norms, dest_own, dest_halo, slots):
    rows, wide = x_in.shape
    count = dest_own.shape[1]
    tile = pl.BlockSpec((SLOT, wide), lambda t: (t, 0))
    return pl.pallas_call(
        last_kernel,
        grid=(slots,),
        in_specs=[tile] * 4 + [whole(norms.shape), whole(dest_own.shape), whole(dest_halo.shape)],
        out_specs=[whole((count, wide)), whole((HALO, wide)), whole((56, wide)), whole((8, wide))],
        out_shape=[
            jax.ShapeDtypeStruct((count, wide), F32),
            jax.ShapeDtypeStruct((HALO, wide), BF16),
            jax.ShapeDtypeStruct((56, wide), F32),
            jax.ShapeDtypeStruct((8, wide), F32),
        ],
        scratch_shapes=[pltpu.VMEM((rows, wide), BF16)],
        compiler_params=params(),
        cost_estimate=cost(7),
        name="last",
    )(x_in, gm, one, two, norms, dest_own, dest_halo)


class Grid:
    def __init__(self, rows, heads):
        self.deep = rows // 2
        self.size = rows * heads
        row = lax.axis_index("rows")
        col = lax.axis_index("heads")
        self.z = row // 2
        self.x = row % 2
        self.y = col // 2
        self.c = col % 2

    def send(self, value, move):
        pairs = []
        for i in range(self.size):
            z, x, y, c = move(i // 8, (i // 4) % 2, (i // 2) % 2, i % 2)
            pairs.append((i, ((z * 2 + x) * 2 + y) * 2 + c))
        return lax.ppermute(value, AXES, pairs)

    def by_x(self, value):
        return self.send(value, lambda z, x, y, c: (z, 1 - x, y, c))

    def by_y(self, value):
        return self.send(value, lambda z, x, y, c: (z, x, 1 - y, c))

    def by_core(self, value):
        return self.send(value, lambda z, x, y, c: (z, x, y, 1 - c))

    def by_z(self, value, bit):
        return self.send(value, lambda z, x, y, c: (z ^ bit, x, y, c))

    def gather_z(self, value, axis, *between):
        first = None
        bit = self.deep // 2
        while bit:
            got = self.by_z(value, bit)
            if first is None:
                got = first = after(got, *between)
            value = jnp.concatenate([value, got], axis=axis)
            bit //= 2
        return value, first

    def spread(self, first, second):
        a_next, b_next = tie(self.by_y(first), self.by_x(second))
        a_zero = jnp.stack([first, a_next])
        b_zero = jnp.stack([second, b_next])
        return a_zero, b_zero

    def spread_more(self, a_zero, b_zero):
        return self.by_x(a_zero), self.by_y(b_zero)

    def fold_z(self, keep, got):
        bit, first = 2, got
        while bit < self.deep:
            keep, send = sum_split([keep, got])
            got = self.by_z(send, bit)
            first = send if bit == 2 else first
            bit *= 2
        return keep, got, first

    def to_absolute(self, blocks, z_axis, x_axis):
        return self.turn(jnp.where(self.x == 0, blocks, jnp.flip(blocks, axis=x_axis)), z_axis, False)

    def to_relative(self, blocks, z_axis, x_axis):
        return self.turn(jnp.where(self.x == 0, blocks, jnp.flip(blocks, axis=x_axis)), z_axis, True)

    def turn(self, blocks, z_axis, back):
        shape = blocks.shape
        bits = self.deep.bit_length() - 1
        blocks = blocks.reshape(shape[:z_axis] + (2,) * bits + shape[z_axis + 1 :])
        order = list(range(blocks.ndim))
        order[z_axis : z_axis + bits] = order[z_axis : z_axis + bits][::-1]
        if back:
            blocks = blocks.transpose(order)
        for i in range(bits):
            flipped = jnp.flip(blocks, axis=z_axis + i)
            blocks = jnp.where((self.z >> i) & 1 == 0, blocks, flipped)
        if not back:
            blocks = blocks.transpose(order)
        return blocks.reshape(shape)


def exchange(value, send):
    low = value.astype(BF16)
    return low.astype(F32) + send(low).astype(F32)


def tie(*values):
    return lax.optimization_barrier(values)


def after(value, *earlier):
    return lax.optimization_barrier((value, *earlier))[0]


def local(
    rows,
    heads,
    tokens,
    segment,
    live_token,
    prompt_slot,
    prompts,
    attn_gain,
    attn_shift,
    qkv_weight,
    out_weight,
    mlp_gain,
    mlp_shift,
    up_weight,
    up_bias,
    down_weight,
    cotangent,
):
    grid = Grid(rows, heads)
    deep = grid.deep
    count, wide = tokens.shape
    slots = IMGS_ROW * 2 * count // ROW
    place = jnp.stack([grid.z, grid.x, grid.y, grid.c]).astype(jnp.int32)

    def row_of(vec):
        return vec.astype(F32).reshape(1, -1)

    norms = jnp.stack([attn_gain, attn_shift, mlp_gain, mlp_shift]).astype(F32)

    depth = qkv_weight.shape[0]
    third = qkv_weight.shape[2]
    shard = jnp.concatenate(
        [qkv_weight.reshape(depth, 3 * third), out_weight.swapaxes(0, 1)], axis=1
    ).reshape(2, 1, depth // 2, 4 * third)

    hidden = up_weight.shape[1]
    span = hidden // 2
    halves = jnp.stack(
        [up_weight.swapaxes(0, 1).reshape(2, span, wide), down_weight.reshape(2, span, wide)],
        axis=1,
    )
    bias, first = grid.gather_z(up_bias.reshape(1, hidden), 0)
    shard = after(shard, first)
    got, first = grid.gather_z(shard, 1, bias)
    bias = jnp.stack([bias, grid.by_x(bias)])
    bias = jnp.stack([bias, grid.by_y(bias)])

    code = ((segment % IMGS_ROW) * 2 + live_token).astype(BF16)
    marks = jnp.pad(code[None], ((0, 15), (0, wide - count)))
    own = after(jnp.concatenate([tokens, cotangent, marks]), shard)
    other = grid.by_core(own)
    mine = grid.c == 1 - grid.y
    first_row = jnp.where(grid.y == 0, count - HALO, 0)
    edge_parts = []
    for base in (0, count):
        edge_parts.append(
            jnp.where(
                mine,
                lax.dynamic_slice_in_dim(own, base + first_row, HALO),
                lax.dynamic_slice_in_dim(other, base + first_row, HALO),
            )
        )
    edge_code = jnp.where(mine, own[2 * count :], other[2 * count :])
    edge_code = jnp.where(grid.y == 0, edge_code[:, count - HALO : count], edge_code[:, :HALO])
    edge_parts.append(jnp.pad(edge_code, ((0, 0), (0, wide - HALO))))
    edge = jnp.concatenate(edge_parts)
    halo = grid.by_y(edge)

    got, bias, halo = tie(got, bias, halo)
    a_zero, b_zero = grid.spread(got[0], got[1])
    a_one, b_one = grid.spread_more(a_zero, b_zero)
    x_in, normed, cot, dest_own, dest_halo = prep(place, own, other, halo, prompts, norms, slots)

    held, _ = grid.gather_z(after(halves, first)[:, None], 1, normed)
    mlp_a, mlp_b = held[0], held[1]
    mlp_a0, mlp_b0 = grid.spread(mlp_a, mlp_b)
    mlp_a1, mlp_b1 = grid.spread_more(mlp_a0, mlp_b0)
    bias_a = jnp.stack([bias[:, 0, :, :span], bias[0, :, :, span:]])
    bias_b = jnp.stack([bias[:, 1, :, :span], bias[1, :, :, span:]])

    weights = [a_zero, a_one, b_zero, b_one]
    if (depth // 2) % 16:
        blocks = jnp.stack(
            [
                jnp.concatenate([(a_zero, a_one)[dx][dy], (b_zero, b_one)[dy][dx]], axis=1)
                for dy in range(2)
                for dx in range(2)
            ]
        ).reshape(2, 2, deep, depth, 4 * third)
        blocks = grid.to_absolute(blocks, 2, 1).swapaxes(1, 2)
        weights = [blocks.reshape(2, 2 * deep * depth, 4 * third)]
    qkv, prob, att, part = attend(place, normed, weights, slots)

    fine = span % 16 == 0

    def enter(value):
        value = value.reshape(-1, 2, span, wide)
        if fine:
            return value
        return value.swapaxes(0, 1).reshape(2, -1, 48, wide).swapaxes(0, 1)

    def leave(value):
        if fine:
            return value
        return value.swapaxes(0, 1).reshape(2, -1, span, wide).swapaxes(0, 1)

    start = (x_in, part, grid.by_core(part), norms)
    middle, normed_two, o_sum, g_sum, *grads, grad_bias_a = mlp(
        [enter(mlp_a0), enter(mlp_b0)], cot, row_of(bias_a), slots, start
    )
    grad_a0, grad_b0 = [leave(v).reshape(2, deep, 2, span, wide) for v in grads]
    o_part, g_part, *grads, grad_bias_b = mlp(
        [enter(mlp_a1), enter(mlp_b1)],
        cot,
        row_of(bias_b),
        slots,
        normed_two,
        (o_sum, g_sum),
    )
    grad_a1, grad_b1 = [leave(v).reshape(2, deep, 2, span, wide) for v in grads]
    a_got, b_got = grid.by_x(grad_a1), grid.by_y(grad_b1)
    g_other = grid.by_core(g_part)

    grad_proj, grad_qkv, g_one, sums_two = back(
        place, middle, g_part, g_other, cot, norms, weights, qkv, prob, slots
    )
    g_one_other = grid.by_core(g_one)
    o_other = grid.by_core(after(o_part, g_one))
    weight_blocks = weight_grads(place, normed, grad_proj, grad_qkv, att, weights)
    a_got, b_got, _ = tie(a_got, b_got, weight_blocks[0])
    a_send, b_send = add_second(grad_a0, a_got, grad_b0, b_got, 40)
    a_last, b_last = grid.by_y(a_send), grid.by_x(b_send)
    if len(weight_blocks) == 1:
        blocks = weight_blocks[0].reshape(2, deep, 2, depth, 4 * third).swapaxes(1, 2)
        blocks = grid.to_relative(blocks, 2, 1)
        blocks = blocks.reshape(2, 2, deep, 2, depth // 2, 4 * third)
        weight_blocks = [
            blocks[:, 0, :, 0],
            blocks[:, 1, :, 0],
            blocks[0, :, :, 1],
            blocks[1, :, :, 1],
        ]
    att_a0, att_a1, att_b0, att_b1 = weight_blocks
    att_a_got, att_b_got = grid.by_x(after(att_a1, a_send)), grid.by_y(after(att_b1, b_send))
    tok_own, tok_halo, prompt_sum, sums_one = last(
        x_in, grad_proj, g_one, after(g_one_other, a_send), norms, dest_own, dest_halo, slots
    )

    g_a = grad_bias_a.reshape(2, 2, deep, span)
    g_b = grad_bias_b.reshape(2, 2, deep, span)
    bias_blocks = jnp.stack(
        [jnp.stack([g_a[0], g_b[0]], axis=1), jnp.stack([g_a[1], g_b[1]], axis=0)], axis=3
    )
    bias_blocks = grid.to_absolute(bias_blocks, 2, 1)
    bias_blocks = jnp.where(grid.y == 0, bias_blocks, jnp.flip(bias_blocks, axis=0))
    small = jnp.concatenate(
        [prompt_sum, sums_one[:2], sums_two[:2], bias_blocks.reshape(-1, wide)]
    )
    out_own, out_halo = finish(
        middle, o_part, after(o_other, tok_halo), dest_own, dest_halo, slots
    )
    edges = grid.by_y(jnp.concatenate([out_halo, tok_halo]))
    small = exchange(small, lambda v: grid.by_z(v, 1))
    a_last, b_last, _ = tie(a_last, b_last, out_halo)
    grad_keep, grad_send = fold_first(grad_a0, a_got, a_last, grad_b0, b_got, b_last)
    grad_got = grid.by_z(grad_send, 1)
    att_a_got, att_b_got, small, _ = tie(att_a_got, att_b_got, small, grad_send)
    stride = 2
    while stride < deep:
        small = exchange(small, lambda v, stride=stride: grid.by_z(v, stride))
        stride *= 2
    a_send, b_send = add_second(att_a0, att_a_got, att_b0, att_b_got, 4)
    att_a_last, att_b_last = grid.by_y(a_send), grid.by_x(b_send)
    grad_got, _ = tie(grad_got, a_send)
    grad_keep, grad_got, grad_send = grid.fold_z(grad_keep, grad_got)
    att_a_last, att_b_last, _ = tie(att_a_last, att_b_last, grad_send)
    att_keep, att_send = fold_first(att_a0, att_a_got, att_a_last, att_b0, att_b_got, att_b_last)
    att_got = grid.by_z(att_send, 1)
    small, edges, _ = tie(small, edges, att_send)
    small = exchange(small, grid.by_x)
    att_got, small, grad_got = tie(att_got, small, grad_got)
    small = exchange(small, grid.by_y)
    att_keep, att_got, _ = grid.fold_z(att_keep, att_got)
    grad_shard = (grad_keep.astype(F32) + grad_got.astype(F32))[0]
    grad_up = grad_shard[:, 0].reshape(hidden, wide).swapaxes(0, 1)
    grad_down = grad_shard[:, 1].reshape(hidden, wide)
    att_shard = att_keep.astype(F32) + att_got.astype(F32)
    att_shard = att_shard.reshape(depth, 4 * third)
    grad_qkv_weight = att_shard[:, : 3 * third].reshape(depth, 3, third)
    grad_out_weight = att_shard[:, 3 * third :].swapaxes(0, 1)

    def merge(value, edge):
        edge = edge.astype(value.dtype)
        ends = jnp.where((grid.y == 0) & (grid.c == 1), edge, 0)
        begins = jnp.where((grid.y == 1) & (grid.c == 0), edge, 0)
        value = value.at[count - HALO :].add(ends)
        return value.at[:HALO].add(begins)

    bias_all = small[60:].reshape(2, 2, deep, hidden)
    grad_bias = lax.dynamic_slice(
        bias_all, (grid.y, grid.x, grid.z, jnp.int32(0)), (1, 1, 1, hidden)
    ).reshape(hidden)
    return (
        merge(out_own, edges[:HALO]),
        merge(tok_own, edges[HALO:]),
        small[1 : 1 + PROMPTS],
        small[56],
        small[57],
        grad_qkv_weight,
        grad_out_weight,
        small[58],
        small[59],
        grad_up,
        grad_bias,
        grad_down,
    )


def solution(mesh):
    both = P(AXES)
    lead = P(AXES, None)
    return jax.shard_map(
        functools.partial(local, mesh.shape["rows"], mesh.shape["heads"]),
        mesh=mesh,
        in_specs=(
            lead,
            both,
            both,
            both,
            P(),
            P(),
            P(),
            P("rows", None, "heads"),
            P("heads", "rows"),
            P(),
            P(),
            P(None, AXES),
            both,
            lead,
            lead,
        ),
        out_specs=(
            lead,
            lead,
            P(),
            P(),
            P(),
            P("rows", None, "heads"),
            P("heads", "rows"),
            P(),
            P(),
            P(None, AXES),
            both,
            lead,
        ),
        check_vma=False,
    )
```

```python
import functools

import jax
import jax.numpy as jnp
from jax import lax
from jax.experimental import pallas as pl
from jax.experimental.pallas import tpu as pltpu
from jax.sharding import PartitionSpec as P

HEAD = 64
ROW = 2048
IMG = 247
IMGS_ROW = 8
PROMPTS = 50
SLOT = 272
CORE = 256
TAIL = 16
HALO = 48
EPSILON = 1e-06
AXES = ("rows", "heads")
F32 = jnp.float32
BF16 = jnp.bfloat16
VMEM_LIMIT = 56 * 1024 * 1024

NN = (((1,), (0,)), ((), ()))
NT = (((1,), (1,)), ((), ()))
TN = (((0,), (0,)), ((), ()))


def dot(left, right, dims=NN):
    return lax.dot_general(left, right, dims, preferred_element_type=F32)


def whole(shape):
    return pl.BlockSpec(shape, lambda *_: (0,) * len(shape))


def params(limit=VMEM_LIMIT):
    return pltpu.CompilerParams(vmem_limit_bytes=limit)


SCALE = 0.15


def cost(time):
    return pl.CostEstimate(flops=int(time * SCALE * 1.15e9), bytes_accessed=1, transcendentals=0)


SMEM = pl.BlockSpec(memory_space=pltpu.SMEM)
ANY = pl.BlockSpec(memory_space=pl.ANY)


def stats(values):
    center = values - jnp.mean(values, axis=-1, keepdims=True)
    inverse = lax.rsqrt(jnp.mean(center * center, axis=-1, keepdims=True) + EPSILON)
    return center * inverse, inverse


def norm_back(grad, hat, inverse, gain):
    inner = grad * gain
    first = jnp.mean(inner, axis=-1, keepdims=True)
    second = jnp.mean(inner * hat, axis=-1, keepdims=True)
    return inverse * (inner - first - hat * second)


def pick_rows(step, sources, block):
    total = None
    for dest, ref in sources:
        size = dest.shape[1]
        at = step * SLOT + lax.broadcasted_iota(jnp.int32, (SLOT, size), 0)
        part = dot((at == dest[...]).astype(BF16), ref[block * size : (block + 1) * size])
        total = part if total is None else total + part
    return total


def prep_cot_kernel(own, other, halo, dest_own, dest_other, dest_halo, out):
    sources = ((dest_own, own), (dest_other, other), (dest_halo, halo))
    out[...] = pick_rows(pl.program_id(0), sources, 0).astype(BF16)


def prep_cot(own, other, halo, dest_own, dest_other, dest_halo, slots):
    count, wide = dest_own.shape[1], own.shape[1]
    rows = slots * SLOT
    second = [pl.BlockSpec((size, wide), lambda t: (1, 0)) for size in (count, count, HALO)]
    dests = (dest_own, dest_other, dest_halo)
    return pl.pallas_call(
        prep_cot_kernel,
        grid=(slots,),
        in_specs=second + [whole(v.shape) for v in dests],
        out_specs=pl.BlockSpec((SLOT, wide), lambda t: (t, 0)),
        out_shape=jax.ShapeDtypeStruct((rows, wide), BF16),
        compiler_params=params(24 * 1024 * 1024),
        cost_estimate=cost(5),
        name="prep_cot",
    )(own, other, halo, *dests)


def prep_kernel(
    place, own, other, halo, prom, norms, x_out, n_out, dest_own, dest_other, dest_halo
):
    step = pl.program_id(0)
    count = dest_own.shape[1]
    slots = pl.num_programs(0)
    y_at, c_at = place[2], place[3]

    @pl.when(step == 0)
    def _():
        big = 1 << 20
        spans = (
            (own[2 * count : 2 * count + 16, :count], 2 * count * y_at + count * c_at, True),
            (other[2 * count : 2 * count + 16, :count], 2 * count * y_at + count * (1 - c_at), True),
            (halo[2 * HALO : 2 * HALO + 16, :HALO], 2 * count - HALO * y_at, False),
        )
        parts = []
        for marks, base, home in spans:
            code = marks.astype(F32)[0:1].astype(jnp.int32)
            live = (code & 1) > 0
            slot = (code >> 1) - slots * y_at
            pos = base + lax.broadcasted_iota(jnp.int32, code.shape, 1)
            parts.append((live, slot, pos, home))
        starts = []
        for k in range(slots):
            low = None
            for live, slot, pos, home in parts:
                here = jnp.min(jnp.where(live & (slot == k), pos, big), axis=1, keepdims=True)
                low = here if low is None else jnp.minimum(low, here)
            starts.append(low)
        pads_own, pads_other = [
            jnp.sum(jnp.where(part[0], 0, 1), axis=1, keepdims=True) for part in parts[:2]
        ]
        befores = (c_at * pads_other, (1 - c_at) * pads_own, None)
        results = []
        for (live, slot, pos, home), before in zip(parts, befores):
            dest = jnp.full(pos.shape, -1, jnp.int32)
            for k in range(slots):
                dest = jnp.where(live & (slot == k), pos - starts[k] + k * SLOT, dest)
            if home:
                pads = jnp.where(live, 0.0, 1.0).astype(BF16)
                size = pads.shape[1]
                earlier = (
                    lax.broadcasted_iota(jnp.int32, (size, size), 0)
                    < lax.broadcasted_iota(jnp.int32, (size, size), 1)
                )
                wide = jnp.broadcast_to(pads, (16, size))
                rank = dot(wide, earlier.astype(BF16))[0:1].astype(jnp.int32) + before
                spare = (rank & (slots - 1)) * SLOT + IMG + (rank >> (slots.bit_length() - 1))
                dest = jnp.where(live, dest, spare)
            results.append(dest)
        dest_own[...] = results[0]
        dest_other[...] = results[1]
        dest_halo[...] = results[2]

    tokens = pick_rows(step, ((dest_own, own), (dest_other, other), (dest_halo, halo)), 0)
    at = lax.broadcasted_iota(jnp.int32, (SLOT, 1), 0)
    slot_row = lax.broadcasted_iota(jnp.int32, (SLOT, PROMPTS), 0)
    which = lax.broadcasted_iota(jnp.int32, (SLOT, PROMPTS), 1)
    prompted = dot((slot_row == which + 1).astype(BF16), prom[...])
    inputs = jnp.where((at >= 1) & (at <= PROMPTS), prompted, tokens)
    hat, _ = stats(inputs)
    x_out[...] = inputs.astype(BF16)
    n_out[...] = (hat * norms[0:1] + norms[1:2]).astype(BF16)


def prep(place, own, other, halo, prom, norms, slots):
    count = own.shape[0] // 2 - 8
    wide = own.shape[1]
    rows = slots * SLOT
    tile = pl.BlockSpec((SLOT, wide), lambda t: (t, 0))
    array = jax.ShapeDtypeStruct((rows, wide), BF16)
    return pl.pallas_call(
        prep_kernel,
        grid=(slots,),
        in_specs=[SMEM] + [whole(v.shape) for v in (own, other, halo, prom, norms)],
        out_specs=[tile, tile] + [whole((1, size)) for size in (count, count, HALO)],
        out_shape=[array, array]
        + [jax.ShapeDtypeStruct((1, size), jnp.int32) for size in (count, count, HALO)],
        compiler_params=params(24 * 1024 * 1024),
        cost_estimate=cost(8),
        name="prep",
    )(place, own, other, halo, prom, norms)


def reverse_bits(index, size):
    return sum(((index >> i) & 1) * (size >> (i + 1)) for i in range(size.bit_length() - 1))


def weight_pieces(place, refs):
    if len(refs) == 1:
        for group in range(2):
            yield refs[0].at[group], group, 0, refs[0].shape[1]
        return
    a_zero, a_one, b_zero, b_one = refs
    deep, half = a_zero.shape[1], a_zero.shape[2]
    for dx in range(2):
        col = place[1] if dx == 0 else 1 - place[1]
        for dy in range(2):
            for k in range(deep):
                row = place[0] ^ reverse_bits(k, deep)
                for part in range(2):
                    ref = ((a_zero, a_one)[dx].at[dy, k], (b_zero, b_one)[dy].at[dx, k])[part]
                    first = ((row * 2 + col) * 2 + part) * half
                    yield ref, dy, pl.multiple_of(first, 16), half


def piece_count(held):
    return 2 if len(held) == 1 else 8 * held[0].shape[1]


def weight_copies(place, held, weight, sem):
    return [
        pltpu.make_async_copy(ref, weight.at[group, pl.ds(first, size)], sem.at[i])
        for i, (ref, group, first, size) in enumerate(weight_pieces(place, held))
    ]


def load_weight(copies):
    for copy in copies:
        copy.start()
    for copy in copies:
        copy.wait()


def attend_kernel(held_count, place, normed, *refs):
    held = refs[:held_count]
    qkv_out, prob_out, att_out, part_out, weight, sem = refs[held_count:]
    copies = weight_copies(place, held, weight, sem)

    @pl.when(pl.program_id(0) == 0)
    def _():
        load_weight(copies)

    third = weight.shape[2] // 4
    live = lax.broadcasted_iota(jnp.int32, (TAIL, 1), 0) < IMG - (CORE - TAIL)
    groups, heads = weight.shape[0], third // HEAD
    pairs = [(group, head) for group in range(groups) for head in range(heads)]
    for group in range(groups):
        qkv_out[group] = dot(normed[...], weight[group, :, : 3 * third]).astype(BF16)

    def part_of(which, group, head):
        at = which * third + head * HEAD
        return qkv_out[group, :CORE, at : at + HEAD]

    scores = [dot(part_of(1, *pair), part_of(0, *pair) * 0.125, NT) for pair in pairs]
    for (group, head), score in zip(pairs, scores):
        score = jnp.concatenate(
            [score[: CORE - TAIL], jnp.where(live, score[CORE - TAIL :], -1e30)]
        )
        exp_scores = jnp.exp(score - jnp.max(score, axis=0, keepdims=True))
        shrink = 1.0 / jnp.sum(exp_scores, axis=0, keepdims=True)
        prob_out[0, group, head] = (exp_scores * shrink).astype(BF16)
    mixed = [dot(part_of(2, *pair), prob_out[(0, *pair)], TN) for pair in pairs]
    total = None
    for group in range(groups):
        mix = jnp.concatenate(mixed[group * heads : (group + 1) * heads]).T.astype(BF16)
        att_out[group, : CORE - TAIL] = mix[: CORE - TAIL]
        att_out[group, CORE - TAIL : CORE] = jnp.where(
            live, mix[CORE - TAIL :], qkv_out[group, CORE - TAIL : CORE, 2 * third :]
        )
        att_out[group, CORE:] = qkv_out[group, CORE:, 2 * third :]
        part = dot(att_out[group], weight[group, :, 3 * third :], NT)
        total = part if total is None else total + part
    part_out[...] = total.astype(BF16)


def attend(place, normed, held, slots):
    rows, deep = normed.shape
    groups, wide = 2, held[0].shape[-1]
    third = wide // 4
    heads = third // HEAD
    return pl.pallas_call(
        functools.partial(attend_kernel, len(held)),
        grid=(slots,),
        in_specs=[SMEM, pl.BlockSpec((SLOT, deep), lambda t: (t, 0))] + [ANY] * len(held),
        out_specs=[
            pl.BlockSpec((groups, SLOT, 3 * third), lambda t: (0, t, 0)),
            pl.BlockSpec((1, groups, heads, CORE, CORE), lambda t: (t, 0, 0, 0, 0)),
            pl.BlockSpec((groups, SLOT, third), lambda t: (0, t, 0)),
            pl.BlockSpec((SLOT, deep), lambda t: (t, 0)),
        ],
        out_shape=[
            jax.ShapeDtypeStruct((groups, rows, 3 * third), BF16),
            jax.ShapeDtypeStruct((slots, groups, heads, CORE, CORE), BF16),
            jax.ShapeDtypeStruct((groups, rows, third), BF16),
            jax.ShapeDtypeStruct((rows, deep), BF16),
        ],
        scratch_shapes=[
            pltpu.VMEM((groups, deep, wide), BF16),
            pltpu.SemaphoreType.DMA((piece_count(held),)),
        ],
        compiler_params=params(),
        cost_estimate=cost(13),
        name="attend",
    )(place, normed, *held)


def mlp_kernel(more, count, *refs):
    parts, refs = refs[:count], refs[count:]
    if more:
        (normed, cot, bias, o_acc, g_acc, *refs) = refs
    else:
        (x_in, one, two, norms, cot, bias, middle_out, normed, *refs) = refs
    (o_out, g_out), grads, refs = refs[:2], refs[2 : 2 + count], refs[2 + count :]
    (bias_out, weight, act, grad, result, in_sem, out_sem) = refs
    step = pl.program_id(0)
    _, pieces, span, wide = weight.shape
    hidden = pieces * span
    cut = 768
    spots = []
    for ref in parts:
        spots.append(sum(size for _, size in spots))
        spots[-1] = (spots[-1], ref.shape[0])
    loads = [
        pltpu.make_async_copy(
            parts[i].at[:, kind], weight.at[kind, pl.ds(first, size)], in_sem.at[2 * i + kind]
        )
        for i, (first, size) in enumerate(spots)
        for kind in range(2)
    ]
    stores = [
        pltpu.make_async_copy(
            result.at[kind, pl.ds(first, size)], grads[i].at[:, kind], out_sem.at[2 * i + kind]
        )
        for i, (first, size) in enumerate(spots)
        for kind in range(2)
    ]

    @pl.when(step == 0)
    def _():
        for copy in loads:
            copy.start()
        bias_out[...] = jnp.zeros_like(bias_out)
        for copy in loads:
            copy.wait()

    rows = pl.ds(pl.multiple_of(step * SLOT, 16), SLOT)
    if not more:
        middle = x_in[...].astype(F32) + (one[...].astype(F32) + two[...].astype(F32))
        middle_out[...] = middle.astype(BF16)
        hat, _ = stats(middle)
        normed[rows] = (hat * norms[2:3] + norms[3:4]).astype(BF16)
    tile_n = normed[rows]
    tile_c = cot[rows]
    for at in range(0, hidden, cut):
        up = weight[0, at // span : (at + cut) // span].reshape(cut, wide)
        down = weight[1, at // span : (at + cut) // span].reshape(cut, wide)
        pre = dot(tile_n, up, NT) + bias[:, at : at + cut]
        cdf = 0.5 * (1.0 + lax.erf(pre * 0.7071067811865476))
        pdf = jnp.exp(-0.5 * pre * pre) * 0.3989422804014327
        act[rows, at : at + cut] = (pre * cdf).astype(BF16)
        grad_low = (dot(tile_c, down, NT) * (cdf + pre * pdf)).astype(BF16)
        grad[rows, at : at + cut] = grad_low
        bias_out[:, at : at + cut] += jnp.sum(grad_low.astype(F32), axis=0, keepdims=True)
    o_sum = dot(act[rows], weight[1].reshape(hidden, wide))
    g_sum = dot(grad[rows], weight[0].reshape(hidden, wide))
    if more:
        o_sum = o_sum + o_acc[...].astype(F32)
        g_sum = g_sum + g_acc[...].astype(F32)
    o_out[...] = o_sum.astype(o_out.dtype)
    g_out[...] = g_sum.astype(g_out.dtype)

    @pl.when(step == pl.num_programs(0) - 1)
    def _():
        sent = 0
        for at in range(0, hidden, cut):
            own = pl.ds(at // span, cut // span)
            shape = (cut // span, span, wide)
            result[0, own] = dot(grad[:, at : at + cut], normed[...], TN).astype(BF16).reshape(shape)
            result[1, own] = dot(act[:, at : at + cut], cot[...], TN).astype(BF16).reshape(shape)
            done = sum((first + size) * span <= at + cut for first, size in spots)
            for copy in stores[2 * sent : 2 * done]:
                copy.start()
            sent = done
        for copy in stores:
            copy.wait()


def mlp(parts, cot, bias, slots, start=None, sums=None):
    rows, wide = cot.shape
    hidden = bias.shape[1]
    span = parts[0].shape[2]
    more = sums is not None
    tile = pl.BlockSpec((SLOT, wide), lambda t: (t, 0))
    wide_bf16 = jax.ShapeDtypeStruct((rows, wide), BF16)
    full = whole(cot.shape)
    count = len(parts)
    if more:
        operands = (*parts, start, cot, bias, *sums)
        specs = [ANY] * count + [full, full, whole(bias.shape), tile, tile]
    else:
        x_in, one, two, norms = start
        operands = (*parts, x_in, one, two, norms, cot, bias)
        specs = [ANY] * count + [tile, tile, tile, whole(norms.shape), full, whole(bias.shape)]
    return pl.pallas_call(
        functools.partial(mlp_kernel, more, count),
        grid=(slots,),
        in_specs=specs,
        out_specs=([] if more else [tile, full])
        + [tile, tile]
        + [ANY] * count
        + [whole(bias.shape)],
        out_shape=([] if more else [wide_bf16, wide_bf16])
        + [wide_bf16, wide_bf16]
        + [jax.ShapeDtypeStruct(v.shape, BF16) for v in parts]
        + [jax.ShapeDtypeStruct(bias.shape, F32)],
        scratch_shapes=[
            pltpu.VMEM((2, hidden // span, span, wide), BF16),
            pltpu.VMEM((rows, hidden), BF16),
            pltpu.VMEM((rows, hidden), BF16),
            pltpu.VMEM((2, hidden // span, span, wide), BF16),
            pltpu.SemaphoreType.DMA((2 * count,)),
            pltpu.SemaphoreType.DMA((2 * count,)),
        ],
        compiler_params=params(),
        cost_estimate=cost(17),
        name="mlp",
    )(*operands)


def add_kernel(a_zero, a_got, b_zero, b_got, a_out, b_out):
    for zero, got, out in ((a_zero, a_got, a_out), (b_zero, b_got, b_out)):
        out[...] = (zero[0].astype(F32) + got[0].astype(F32)).astype(BF16)


def add_second(a_zero, a_got, b_zero, b_got, time):
    shape = a_zero.shape[1:]
    size = shape[0] // 2
    block = pl.BlockSpec((1, size) + shape[1:], lambda k: (1, k) + (0,) * (len(shape) - 1))
    out = pl.BlockSpec((size,) + shape[1:], lambda k: (k,) + (0,) * (len(shape) - 1))
    return pl.pallas_call(
        add_kernel,
        grid=(2,),
        in_specs=[block] * 4,
        out_specs=[out] * 2,
        out_shape=[jax.ShapeDtypeStruct(shape, BF16)] * 2,
        compiler_params=params(24 * 1024 * 1024),
        cost_estimate=cost(time),
        name="add_second",
    )(a_zero, a_got, b_zero, b_got)


def split_kernel(count, *refs):
    total = refs[0][...].astype(F32)
    for ref in refs[1:count]:
        total = total + ref[...].astype(F32)
    low = total.astype(BF16)
    half = low.shape[0] // 2
    refs[count][...] = low[:half]
    refs[count + 1][...] = low[half:]


def sum_split(values):
    shape = values[0].shape
    half = (shape[0] // 2,) + shape[1:]
    return pl.pallas_call(
        functools.partial(split_kernel, len(values)),
        grid=(1,),
        in_specs=[whole(shape)] * len(values),
        out_specs=[whole(half)] * 2,
        out_shape=[jax.ShapeDtypeStruct(half, BF16)] * 2,
        compiler_params=params(24 * 1024 * 1024),
        cost_estimate=cost(2),
        name="sum_split",
    )(*values)


def fold_kernel(a_zero, a_got, a_last, b_zero, b_got, b_last, keep, send):
    half = keep.shape[0]
    for part, (zero, got, last_got) in enumerate(((a_zero, a_got, a_last), (b_zero, b_got, b_last))):
        total = zero[0].astype(F32) + got[0].astype(F32) + last_got[...].astype(F32)
        total = total.astype(BF16)
        keep[:, part] = total[:half]
        send[:, part] = total[half:]


def fold_first(a_zero, a_got, a_last, b_zero, b_got, b_last):
    shape = a_last.shape
    first = whole((1,) + shape)
    out = (shape[0] // 2, 2) + shape[1:]
    return pl.pallas_call(
        fold_kernel,
        grid=(1,),
        in_specs=[first, first, whole(shape)] * 2,
        out_specs=[whole(out)] * 2,
        out_shape=[jax.ShapeDtypeStruct(out, BF16)] * 2,
        compiler_params=params(24 * 1024 * 1024),
        cost_estimate=cost(3),
        name="fold_first",
    )(a_zero, a_got, a_last, b_zero, b_got, b_last)


def finish_kernel(middle, one, two, dest_own, dest_halo, own_out, halo_out, values):
    step = pl.program_id(0)
    value = middle[...].astype(F32) + (one[...].astype(F32) + two[...].astype(F32))
    values[pl.ds(pl.multiple_of(step * SLOT, 16), SLOT)] = value.astype(BF16)
    spread_rows(values, dest_own, dest_halo, own_out, halo_out)


def spread_rows(values, dest_own, dest_halo, own_out, halo_out):
    @pl.when(pl.program_id(0) == pl.num_programs(0) - 1)
    def _():
        for dest, out in ((dest_own, own_out), (dest_halo, halo_out)):
            shape = (dest.shape[1], values.shape[0])
            at = lax.broadcasted_iota(jnp.int32, shape, 1)
            pick = (at == dest[...].reshape(dest.shape[1], 1)).astype(BF16)
            out[...] = dot(pick, values[...]).astype(out.dtype)


def finish(middle, one, two, dest_own, dest_halo, slots):
    rows, wide = middle.shape
    count = dest_own.shape[1]
    tile = pl.BlockSpec((SLOT, wide), lambda t: (t, 0))
    return pl.pallas_call(
        finish_kernel,
        grid=(slots,),
        in_specs=[tile, tile, tile, whole(dest_own.shape), whole(dest_halo.shape)],
        out_specs=[whole((count, wide)), whole((HALO, wide))],
        out_shape=[
            jax.ShapeDtypeStruct((count, wide), BF16),
            jax.ShapeDtypeStruct((HALO, wide), BF16),
        ],
        scratch_shapes=[pltpu.VMEM((rows, wide), BF16)],
        compiler_params=params(24 * 1024 * 1024),
        cost_estimate=cost(5),
        name="finish",
    )(middle, one, two, dest_own, dest_halo)


def back_kernel(held_count, place, middle, one, two, cot, norms, qkv, prob, *refs):
    held = refs[:held_count]
    gp_out, dq_out, part_out, sums_out, weight, scored, sem = refs[held_count:]
    step = pl.program_id(0)
    third = weight.shape[2] // 4
    copies = weight_copies(place, held, weight, sem)

    @pl.when(step == 0)
    def _():
        load_weight(copies)
        sums_out[...] = jnp.zeros_like(sums_out)

    grad = one[...].astype(F32) + two[...].astype(F32)
    hat, inverse = stats(middle[...].astype(F32))
    sums_out[0:1] += jnp.sum(grad * hat, axis=0, keepdims=True)
    sums_out[1:2] += jnp.sum(grad, axis=0, keepdims=True)
    grad_middle = cot[...].astype(F32) + norm_back(grad, hat, inverse, norms[2:3])
    grad_proj = grad_middle.astype(BF16)
    gp_out[...] = grad_proj
    live = lax.broadcasted_iota(jnp.int32, (TAIL, 1), 0) < IMG - (CORE - TAIL)
    groups, heads = weight.shape[0], third // HEAD
    pairs = [(group, head) for group in range(groups) for head in range(heads)]

    def part_of(which, group, head):
        at = which * third + head * HEAD
        return qkv[group, :CORE, at : at + HEAD]

    grad_atts, grad_cores = [], []
    for group in range(groups):
        grad_att = dot(grad_proj, weight[group, :, 3 * third :]).astype(BF16)
        tail = grad_att[CORE - TAIL : CORE]
        tail = jnp.where(live, tail, jnp.zeros_like(tail))
        grad_atts.append(grad_att)
        grad_cores.append(jnp.concatenate([grad_att[: CORE - TAIL], tail]))
    grad_heads = [grad_cores[group][:, head * HEAD : (head + 1) * HEAD] for group, head in pairs]
    grad_probs = [dot(part_of(2, *pair), grad, NT) for pair, grad in zip(pairs, grad_heads)]
    grads_v = [dot(prob[(0, *pair)], grad) for pair, grad in zip(pairs, grad_heads)]
    for (group, head), grad_prob in zip(pairs, grad_probs):
        probs = prob[0, group, head].astype(F32)
        center = jnp.sum(probs * grad_prob, axis=0, keepdims=True)
        scored[group * heads + head] = (probs * (grad_prob - center)).astype(BF16)
    grads_q, grads_k = [], []
    for group, head in pairs:
        at = group * heads + head
        grads_q.append(dot(part_of(1, group, head) * 0.125, scored[at], TN))
        grads_k.append(dot(scored[at], part_of(0, group, head) * 0.125))
    total = None
    for group in range(groups):
        own = slice(group * heads, (group + 1) * heads)
        grad_q = jnp.concatenate(grads_q[own]).T.astype(BF16)
        grad_k = jnp.concatenate(grads_k[own], axis=1).astype(BF16)
        grad_v = jnp.concatenate(grads_v[own], axis=1).astype(BF16)
        tail = grad_atts[group][CORE - TAIL : CORE]
        dq_out[group, :CORE, : 3 * third] = jnp.concatenate([grad_q, grad_k, grad_v], axis=1)
        dq_out[group, CORE - TAIL : CORE, 2 * third :] = jnp.where(live, grad_v[CORE - TAIL :], tail)
        dq_out[group, CORE:, : 2 * third] = jnp.zeros((SLOT - CORE, 2 * third), BF16)
        dq_out[group, CORE:, 2 * third :] = grad_atts[group][CORE:]
        part = dot(dq_out[group], weight[group, :, : 3 * third], NT)
        total = part if total is None else total + part
    part_out[...] = total.astype(BF16)


def back(place, middle, one, two, cot, norms, held, qkv, prob, slots):
    rows, wide = middle.shape
    groups, third = qkv.shape[0], qkv.shape[2] // 3
    tile = pl.BlockSpec((SLOT, wide), lambda t: (t, 0))
    tile_q = pl.BlockSpec((groups, SLOT, 3 * third), lambda t: (0, t, 0))
    return pl.pallas_call(
        functools.partial(back_kernel, len(held)),
        grid=(slots,),
        in_specs=[
            SMEM,
            tile,
            tile,
            tile,
            tile,
            whole(norms.shape),
            tile_q,
            pl.BlockSpec((1,) + prob.shape[1:], lambda t: (t, 0, 0, 0, 0)),
        ]
        + [ANY] * len(held),
        out_specs=[tile, tile_q, tile, whole((8, wide))],
        out_shape=[
            jax.ShapeDtypeStruct((rows, wide), BF16),
            jax.ShapeDtypeStruct(qkv.shape, BF16),
            jax.ShapeDtypeStruct((rows, wide), BF16),
            jax.ShapeDtypeStruct((8, wide), F32),
        ],
        scratch_shapes=[
            pltpu.VMEM((groups, wide, 4 * third), BF16),
            pltpu.VMEM((groups * (third // HEAD), CORE, CORE), BF16),
            pltpu.SemaphoreType.DMA((piece_count(held),)),
        ],
        compiler_params=params(),
        cost_estimate=cost(19),
        name="back",
    )(place, middle, one, two, cot, norms, qkv, prob, *held)


def weight_kernel(held_count, place, normed, grad_proj, grad_qkv, att, *refs):
    held = refs[:held_count]
    result, sem = refs[held_count:]
    third = att.shape[2]
    cut = normed.shape[1]
    at = pl.ds(pl.multiple_of(pl.program_id(0) * cut, cut), cut)
    for group in range(2):
        result[group, at, : 3 * third] = dot(normed[...], grad_qkv[group], TN).astype(BF16)
        result[group, at, 3 * third :] = dot(grad_proj[...], att[group], TN).astype(BF16)

    @pl.when(pl.program_id(0) == pl.num_programs(0) - 1)
    def _():
        copies = [
            pltpu.make_async_copy(result.at[group, pl.ds(first, size)], ref, sem.at[i])
            for i, (ref, group, first, size) in enumerate(weight_pieces(place, held))
        ]
        for copy in copies:
            copy.start()
        for copy in copies:
            copy.wait()


def weight_grads(place, normed, grad_proj, grad_qkv, att, held):
    rows, wide = normed.shape
    groups, _, third = att.shape
    cut = 256
    tall = pl.BlockSpec((rows, cut), lambda d: (0, d))
    return pl.pallas_call(
        functools.partial(weight_kernel, len(held)),
        grid=(wide // cut,),
        in_specs=[SMEM, tall, tall, whole(grad_qkv.shape), whole(att.shape)],
        out_specs=[ANY] * len(held),
        out_shape=[jax.ShapeDtypeStruct(v.shape, BF16) for v in held],
        scratch_shapes=[
            pltpu.VMEM((groups, wide, 4 * third), BF16),
            pltpu.SemaphoreType.DMA((piece_count(held),)),
        ],
        compiler_params=params(),
        cost_estimate=cost(9),
        name="weight_grads",
    )(place, normed, grad_proj, grad_qkv, att)


def last_kernel(
    x_in, gm, one, two, norms, dest_own, dest_halo, own_out, halo_out, prompt_out, sums_out, values
):
    step = pl.program_id(0)

    @pl.when(step == 0)
    def _():
        sums_out[...] = jnp.zeros_like(sums_out)
        prompt_out[...] = jnp.zeros_like(prompt_out)

    grad = one[...].astype(F32) + two[...].astype(F32)
    hat, inverse = stats(x_in[...].astype(F32))
    sums_out[0:1] += jnp.sum(grad * hat, axis=0, keepdims=True)
    sums_out[1:2] += jnp.sum(grad, axis=0, keepdims=True)
    grad_in = gm[...].astype(F32) + norm_back(grad, hat, inverse, norms[0:1])
    prompt_out[...] += grad_in[: prompt_out.shape[0]]
    at = lax.broadcasted_iota(jnp.int32, (SLOT, 1), 0)
    value = jnp.where((at >= 1) & (at <= PROMPTS), 0.0, grad_in).astype(BF16)
    values[pl.ds(pl.multiple_of(step * SLOT, 16), SLOT)] = value
    spread_rows(values, dest_own, dest_halo, own_out, halo_out)


def last(x_in, gm, one, two, norms, dest_own, dest_halo, slots):
    rows, wide = x_in.shape
    count = dest_own.shape[1]
    tile = pl.BlockSpec((SLOT, wide), lambda t: (t, 0))
    return pl.pallas_call(
        last_kernel,
        grid=(slots,),
        in_specs=[tile] * 4 + [whole(norms.shape), whole(dest_own.shape), whole(dest_halo.shape)],
        out_specs=[whole((count, wide)), whole((HALO, wide)), whole((56, wide)), whole((8, wide))],
        out_shape=[
            jax.ShapeDtypeStruct((count, wide), F32),
            jax.ShapeDtypeStruct((HALO, wide), BF16),
            jax.ShapeDtypeStruct((56, wide), F32),
            jax.ShapeDtypeStruct((8, wide), F32),
        ],
        scratch_shapes=[pltpu.VMEM((rows, wide), BF16)],
        compiler_params=params(24 * 1024 * 1024),
        cost_estimate=cost(7),
        name="last",
    )(x_in, gm, one, two, norms, dest_own, dest_halo)


class Grid:
    def __init__(self, rows, heads):
        self.deep = rows // 2
        self.size = rows * heads
        row = lax.axis_index("rows")
        col = lax.axis_index("heads")
        self.z = row // 2
        self.x = row % 2
        self.y = col // 2
        self.c = col % 2

    def send(self, value, move):
        pairs = []
        for i in range(self.size):
            z, x, y, c = move(i // 8, (i // 4) % 2, (i // 2) % 2, i % 2)
            pairs.append((i, ((z * 2 + x) * 2 + y) * 2 + c))
        return lax.ppermute(value, AXES, pairs)

    def by_x(self, value):
        return self.send(value, lambda z, x, y, c: (z, 1 - x, y, c))

    def by_y(self, value):
        return self.send(value, lambda z, x, y, c: (z, x, 1 - y, c))

    def by_core(self, value):
        return self.send(value, lambda z, x, y, c: (z, x, y, 1 - c))

    def by_z(self, value, bit):
        return self.send(value, lambda z, x, y, c: (z ^ bit, x, y, c))

    def gather_z(self, value, axis, *between):
        first = None
        bit = self.deep // 2
        while bit:
            got = self.by_z(value, bit)
            if first is None:
                got = first = after(got, *between)
            value = jnp.concatenate([value, got], axis=axis)
            bit //= 2
        return value, first

    def spread(self, first, second):
        a_next, b_next = tie(self.by_y(first), self.by_x(second))
        a_zero = jnp.stack([first, a_next])
        b_zero = jnp.stack([second, b_next])
        return a_zero, b_zero

    def spread_more(self, a_zero, b_zero):
        return self.by_x(a_zero), self.by_y(b_zero)

    def fold_z(self, keep, got):
        bit, first = 2, got
        while bit < self.deep:
            keep, send = sum_split([keep, got])
            got = self.by_z(send, bit)
            first = send if bit == 2 else first
            bit *= 2
        return keep, got, first

    def to_absolute(self, blocks, z_axis, x_axis):
        return self.turn(jnp.where(self.x == 0, blocks, jnp.flip(blocks, axis=x_axis)), z_axis, False)

    def to_relative(self, blocks, z_axis, x_axis):
        return self.turn(jnp.where(self.x == 0, blocks, jnp.flip(blocks, axis=x_axis)), z_axis, True)

    def turn(self, blocks, z_axis, back):
        shape = blocks.shape
        bits = self.deep.bit_length() - 1
        blocks = blocks.reshape(shape[:z_axis] + (2,) * bits + shape[z_axis + 1 :])
        order = list(range(blocks.ndim))
        order[z_axis : z_axis + bits] = order[z_axis : z_axis + bits][::-1]
        if back:
            blocks = blocks.transpose(order)
        for i in range(bits):
            flipped = jnp.flip(blocks, axis=z_axis + i)
            blocks = jnp.where((self.z >> i) & 1 == 0, blocks, flipped)
        if not back:
            blocks = blocks.transpose(order)
        return blocks.reshape(shape)


def exchange(value, send):
    low = value.astype(BF16)
    return low.astype(F32) + send(low).astype(F32)


def tie(*values):
    return lax.optimization_barrier(values)


def after(value, *earlier):
    return lax.optimization_barrier((value, *earlier))[0]


def local(
    rows,
    heads,
    tokens,
    segment,
    live_token,
    prompt_slot,
    prompts,
    attn_gain,
    attn_shift,
    qkv_weight,
    out_weight,
    mlp_gain,
    mlp_shift,
    up_weight,
    up_bias,
    down_weight,
    cotangent,
):
    grid = Grid(rows, heads)
    deep = grid.deep
    count, wide = tokens.shape
    slots = IMGS_ROW * 2 * count // ROW
    place = jnp.stack([grid.z, grid.x, grid.y, grid.c]).astype(jnp.int32)

    def row_of(vec):
        return vec.astype(F32).reshape(1, -1)

    norms = jnp.stack([attn_gain, attn_shift, mlp_gain, mlp_shift]).astype(F32)

    depth = qkv_weight.shape[0]
    third = qkv_weight.shape[2]
    shard = jnp.concatenate(
        [qkv_weight.reshape(depth, 3 * third), out_weight.swapaxes(0, 1)], axis=1
    ).reshape(2, 1, depth // 2, 4 * third)

    hidden = up_weight.shape[1]
    span = hidden // 2
    halves = jnp.stack(
        [up_weight.swapaxes(0, 1).reshape(2, span, wide), down_weight.reshape(2, span, wide)],
        axis=1,
    )
    code = ((segment % IMGS_ROW) * 2 + live_token).astype(BF16)
    marks = jnp.pad(code[None], ((0, 15), (0, wide - count)))
    own = after(jnp.concatenate([tokens, cotangent, marks]), shard)
    other = grid.by_core(own)
    mine = grid.c == 1 - grid.y
    first_row = jnp.where(grid.y == 0, count - HALO, 0)
    edge_parts = []
    for base in (0, count):
        edge_parts.append(
            jnp.where(
                mine,
                lax.dynamic_slice_in_dim(own, base + first_row, HALO),
                lax.dynamic_slice_in_dim(other, base + first_row, HALO),
            )
        )
    edge_code = jnp.where(mine, own[2 * count :], other[2 * count :])
    edge_code = jnp.where(grid.y == 0, edge_code[:, count - HALO : count], edge_code[:, :HALO])
    edge_parts.append(jnp.pad(edge_code, ((0, 0), (0, wide - HALO))))
    edge = jnp.concatenate(edge_parts)
    halo = grid.by_y(edge)

    bias, first = grid.gather_z(up_bias.reshape(1, hidden), 0)
    got, first = grid.gather_z(after(shard, first), 1, bias, halo)
    bias = jnp.stack([bias, grid.by_x(bias)])
    bias = jnp.stack([bias, grid.by_y(bias)])
    x_in, normed, *dests = prep(place, own, other, halo, prompts, norms, slots)
    dest_own, _, dest_halo = dests
    got, bias, _ = tie(got, bias, normed)
    a_zero, b_zero = grid.spread(got[0], got[1])
    a_one, b_one = grid.spread_more(a_zero, b_zero)
    cot = prep_cot(own, other, after(halo, a_zero), *dests, slots)

    held, _ = grid.gather_z(after(halves, first)[:, None], 1)
    held, a_one, b_one = tie(held, a_one, b_one)
    mlp_a, mlp_b = held[0], held[1]
    mlp_a0, mlp_b0 = grid.spread(mlp_a, mlp_b)
    mlp_a1, mlp_b1 = grid.spread_more(mlp_a0, mlp_b0)
    bias_a = jnp.stack([bias[:, 0, :, :span], bias[0, :, :, span:]])
    bias_b = jnp.stack([bias[:, 1, :, :span], bias[1, :, :, span:]])

    weights = [a_zero, a_one, b_zero, b_one]
    if (depth // 2) % 16:
        blocks = jnp.stack(
            [
                jnp.concatenate([(a_zero, a_one)[dx][dy], (b_zero, b_one)[dy][dx]], axis=1)
                for dy in range(2)
                for dx in range(2)
            ]
        ).reshape(2, 2, deep, depth, 4 * third)
        blocks = grid.to_absolute(blocks, 2, 1).swapaxes(1, 2)
        weights = [blocks.reshape(2, 2 * deep * depth, 4 * third)]
    normed, cot = tie(normed, cot)
    qkv, prob, att, part = attend(place, normed, weights, slots)

    fine = span % 16 == 0

    def enter(value):
        value = value.reshape(-1, 2, span, wide)
        if fine:
            return value
        return value.swapaxes(0, 1).reshape(2, -1, 48, wide).swapaxes(0, 1)

    def leave(value):
        if fine:
            return value
        return value.swapaxes(0, 1).reshape(2, -1, span, wide).swapaxes(0, 1)

    start = (x_in, part, grid.by_core(part), norms)
    middle, normed_two, o_sum, g_sum, *grads, grad_bias_a = mlp(
        [enter(mlp_a0), enter(mlp_b0)], cot, row_of(bias_a), slots, start
    )
    grad_a0, grad_b0 = [leave(v).reshape(2, deep, 2, span, wide) for v in grads]
    o_part, g_part, *grads, grad_bias_b = mlp(
        [enter(mlp_a1), enter(mlp_b1)],
        cot,
        row_of(bias_b),
        slots,
        normed_two,
        (o_sum, g_sum),
    )
    grad_a1, grad_b1 = [leave(v).reshape(2, deep, 2, span, wide) for v in grads]
    a_got, b_got = grid.by_x(grad_a1), grid.by_y(grad_b1)
    g_other = grid.by_core(g_part)

    grad_proj, grad_qkv, g_one, sums_two = back(
        place, middle, g_part, g_other, cot, norms, weights, qkv, prob, slots
    )
    g_one_other = grid.by_core(g_one)
    o_other = grid.by_core(after(o_part, g_one))
    weight_blocks = weight_grads(place, normed, grad_proj, grad_qkv, att, weights)
    a_got, b_got, _ = tie(a_got, b_got, weight_blocks[0])
    a_send, b_send = add_second(grad_a0, a_got, grad_b0, b_got, 40)
    a_last, b_last = grid.by_y(a_send), grid.by_x(b_send)
    if len(weight_blocks) == 1:
        blocks = weight_blocks[0].reshape(2, deep, 2, depth, 4 * third).swapaxes(1, 2)
        blocks = grid.to_relative(blocks, 2, 1)
        blocks = blocks.reshape(2, 2, deep, 2, depth // 2, 4 * third)
        weight_blocks = [
            blocks[:, 0, :, 0],
            blocks[:, 1, :, 0],
            blocks[0, :, :, 1],
            blocks[1, :, :, 1],
        ]
    att_a0, att_a1, att_b0, att_b1 = weight_blocks
    att_a_got, att_b_got = grid.by_x(after(att_a1, a_send)), grid.by_y(after(att_b1, b_send))
    tok_own, tok_halo, prompt_sum, sums_one = last(
        x_in, grad_proj, g_one, after(g_one_other, a_send), norms, dest_own, dest_halo, slots
    )

    g_a = grad_bias_a.reshape(2, 2, deep, span)
    g_b = grad_bias_b.reshape(2, 2, deep, span)
    bias_blocks = jnp.stack(
        [jnp.stack([g_a[0], g_b[0]], axis=1), jnp.stack([g_a[1], g_b[1]], axis=0)], axis=3
    )
    bias_blocks = grid.to_absolute(bias_blocks, 2, 1)
    bias_blocks = jnp.where(grid.y == 0, bias_blocks, jnp.flip(bias_blocks, axis=0))
    small = jnp.concatenate(
        [prompt_sum, sums_one[:2], sums_two[:2], bias_blocks.reshape(-1, wide)]
    )
    out_own, out_halo = finish(
        middle, o_part, after(o_other, tok_halo), dest_own, dest_halo, slots
    )
    edges = grid.by_y(jnp.concatenate([out_halo, tok_halo]))
    small = exchange(small, lambda v: grid.by_z(v, 1))
    a_last, b_last, _ = tie(a_last, b_last, out_halo)
    grad_keep, grad_send = fold_first(grad_a0, a_got, a_last, grad_b0, b_got, b_last)
    grad_got = grid.by_z(grad_send, 1)
    att_a_got, att_b_got, small, _ = tie(att_a_got, att_b_got, small, grad_send)
    stride = 2
    while stride < deep:
        small = exchange(small, lambda v, stride=stride: grid.by_z(v, stride))
        stride *= 2
    a_send, b_send = add_second(att_a0, att_a_got, att_b0, att_b_got, 4)
    att_a_last, att_b_last = grid.by_y(a_send), grid.by_x(b_send)
    grad_got, _ = tie(grad_got, a_send)
    grad_keep, grad_got, grad_send = grid.fold_z(grad_keep, grad_got)
    att_a_last, att_b_last, _ = tie(att_a_last, att_b_last, grad_send)
    att_keep, att_send = fold_first(att_a0, att_a_got, att_a_last, att_b0, att_b_got, att_b_last)
    att_got = grid.by_z(att_send, 1)
    small, edges, _ = tie(small, edges, att_send)
    small = exchange(small, grid.by_x)
    att_got, small, grad_got = tie(att_got, small, grad_got)
    small = exchange(small, grid.by_y)
    att_keep, att_got, _ = grid.fold_z(att_keep, att_got)
    grad_shard = (grad_keep.astype(F32) + grad_got.astype(F32))[0]
    grad_up = grad_shard[:, 0].reshape(hidden, wide).swapaxes(0, 1)
    grad_down = grad_shard[:, 1].reshape(hidden, wide)
    att_shard = att_keep.astype(F32) + att_got.astype(F32)
    att_shard = att_shard.reshape(depth, 4 * third)
    grad_qkv_weight = att_shard[:, : 3 * third].reshape(depth, 3, third)
    grad_out_weight = att_shard[:, 3 * third :].swapaxes(0, 1)

    def merge(value, edge):
        edge = edge.astype(value.dtype)
        ends = jnp.where((grid.y == 0) & (grid.c == 1), edge, 0)
        begins = jnp.where((grid.y == 1) & (grid.c == 0), edge, 0)
        value = value.at[count - HALO :].add(ends)
        return value.at[:HALO].add(begins)

    bias_all = small[60:].reshape(2, 2, deep, hidden)
    grad_bias = lax.dynamic_slice(
        bias_all, (grid.y, grid.x, grid.z, jnp.int32(0)), (1, 1, 1, hidden)
    ).reshape(hidden)
    return (
        merge(out_own, edges[:HALO]),
        merge(tok_own, edges[HALO:]),
        small[1 : 1 + PROMPTS],
        small[56],
        small[57],
        grad_qkv_weight,
        grad_out_weight,
        small[58],
        small[59],
        grad_up,
        grad_bias,
        grad_down,
    )


def solution(mesh):
    both = P(AXES)
    lead = P(AXES, None)
    return jax.shard_map(
        functools.partial(local, mesh.shape["rows"], mesh.shape["heads"]),
        mesh=mesh,
        in_specs=(
            lead,
            both,
            both,
            both,
            P(),
            P(),
            P(),
            P("rows", None, "heads"),
            P("heads", "rows"),
            P(),
            P(),
            P(None, AXES),
            both,
            lead,
            lead,
        ),
        out_specs=(
            lead,
            lead,
            P(),
            P(),
            P(),
            P("rows", None, "heads"),
            P("heads", "rows"),
            P(),
            P(),
            P(None, AXES),
            both,
            lead,
        ),
        check_vma=False,
    )
```
